512 devices in a mesh: gx: 32 (over y, x), gy: 16 (over z, core).
Axes of the slice: x: 4, y: 8, z: 8, core: 2. Of those that a mesh axis runs over, the one named last changes fastest.
Arguments:
- diag_block: float32 [4, 4, 6, 64, 4096], P(None, None, None, 'gx', 'gy'), may hold values from -1.1 to 4.1
- block_inverse: float32 [4, 4, 6, 64, 4096], P(None, None, None, 'gx', 'gy'), may hold values from -0.4 to 1.4
- viscosity: float32 [6, 64, 4096], P(None, 'gx', 'gy'), may hold values from 0.4 to 1
- coupling: float32 [6, 4, 4], replicated, may hold values from -0.7 to 0.7
- active_layers: int32 [64, 4096], P('gx', 'gy'), may hold values from 3 to 6
- grounded: int32 [64, 4096], P('gx', 'gy'), may hold values 0 or 1
- weight_pattern: int32 [64, 4096], P('gx', 'gy'), may hold values from 0 to 3
- beta_step: float32 [64, 4096], P('gx', 'gy'), may hold values from -6 to 6
- base_vel: float32 [2, 64, 4096], P(None, 'gx', 'gy'), may hold values from -18 to 18
Outputs:
- hessian_vec: float32 [64, 4096], P('gx', 'gy')
- adjoint: float32 [4, 6, 64, 4096], P(None, None, 'gx', 'gy')
The draws below stay inside these ranges and needn't reach their ends.
All inputs are finite; a program needn't handle non-finite values. No bound on the sum of `grounded` on one device may be relied on, other than what follows from the above.
Results may differ from the reference program's by a relative error of at most 0.0001.
Values sent between devices are 32-bit elements; how exact they have to be, the bound alone decides.
No kernel may reach another device: no remote copies, remote signals or barrier semaphores. Data moves between devices by JAX's collectives and lax.ppermute only.
A program may use at most 192 MiB of HBM per device.

```python
import math
import jax
import jax.numpy as jnp
from jax import lax

L = 6
CX = 2
CY = 256
SWEEPS = 2
NX = 64
NY = 4096
N_GX = 32
N_GY = 16


def block_parts(key, lowest, highest, spread):
    first_key, second_key = jax.random.split(key)
    scales = jnp.exp(jax.random.uniform(first_key, (L, NX, NY), jnp.float32, math.log(lowest), math.log(highest)))
    offdiag = jax.random.uniform(second_key, (4, 4, L, NX, NY), jnp.float32, -spread, spread)
    identity = jnp.eye(4, dtype=jnp.float32)[:, :, None, None, None]
    return (scales, offdiag, identity)


def draw_diag_block(key, part):
    scales, offdiag, identity = block_parts(key, 1.2, 2.5, 0.3)
    return (scales[None, None] * (identity + offdiag)).astype(jnp.float32)


def draw_block_inverse(key, part):
    scales, offdiag, identity = block_parts(key, 1.2, 2.5, 0.3)
    return ((identity - offdiag) / scales[None, None]).astype(jnp.float32)


def place_ends(result, key, low, top_value):
    longest = result.shape.index(max(result.shape))
    spots = []
    for shift in (0, 1):
        where = [jax.random.randint(jax.random.fold_in(key, axis), (), 0, length) for axis, length in enumerate(result.shape)]
        where[longest] = (where[longest] + shift) % result.shape[longest]
        spots.append(tuple(where))
    return result.at[spots[0]].set(low).at[spots[1]].set(top_value)


def steps_of(stream_key, dims, shards, smallest, high):
    gain = 1.0
    for dim, shards_of in shards:
        heights = jax.random.uniform(jax.random.fold_in(jax.random.fold_in(stream_key, 6), dim), (shards_of,), jnp.float32, smallest / len(shards), high / len(shards))
        gain = gain * jnp.repeat(jnp.exp(heights), dims[dim] // shards_of).reshape((-1,) + (1,) * (len(dims) - 1 - dim))
    return gain


def noise(own_key, extent, width, reach, pieces=(), kind=jnp.bfloat16):
    values = jax.random.normal(own_key, extent, jnp.float32) * width
    if len(pieces) > 0:
        values = steps_of(own_key, extent, pieces, -0.22, 0.18) * values
    return jnp.clip(values, min=-reach, max=reach).astype(kind)


def setup_inputs(seed: int = 0) -> dict:
    splits = jax.random.split(jax.random.key(seed), 10)
    return {
        "diag_block": draw_diag_block(jax.random.fold_in(splits[9], 71), 0),
        "block_inverse": draw_block_inverse(jax.random.fold_in(splits[9], 71), 0),
        "viscosity": jnp.clip(jnp.exp(math.log(1.0) - 0.9162907 * jax.random.uniform(splits[2], (L, NX, NY), jnp.float32) ** steps_of(splits[2], (L, NX, NY), ((1, 32), (2, 16)), -0.2, 0.2)), 0.4, 1.0),
        "coupling": noise(splits[3], (6, 4, 4), 0.12, 0.7, (), jnp.float32),
        "active_layers": place_ends(jax.random.randint(splits[4], (NX, NY), L // 2, L + 1), jax.random.fold_in(splits[4], 1), L // 2, L).astype(jnp.int32),
        "grounded": place_ends((jax.random.randint(splits[5], (NX, NY), 0, 3) < 2).astype(jnp.int32), jax.random.fold_in(splits[5], 1), 0, 1),
        "weight_pattern": place_ends(jax.random.randint(splits[6], (NX, NY), 0, 4), jax.random.fold_in(splits[6], 1), 0, 3).astype(jnp.int32),
        "beta_step": noise(splits[7], (NX, NY), 1.0, 6.0, ((0, 32), (1, 16)), jnp.float32),
        "base_vel": noise(splits[8], (2, NX, NY), 3.0, 18.0, ((1, 32), (2, 16)), jnp.float32),
    }


DIRECTIONS = ((0, 1), (0, -1), (1, 1), (1, -1), (2, 1), (2, -1))
OPPOSITE = (1, 0, 3, 2, 5, 4)
PRIOR_WEIGHT = 0.05
EPSILON = 1e-6


def shifted(values, dim_at, offset):
    length = values.shape[dim_at]
    widths = [(0, 0)] * values.ndim
    if offset > 0:
        kept_part = lax.slice_in_dim(values, offset, length, axis=dim_at)
        widths[dim_at] = (0, offset)
    else:
        kept_part = lax.slice_in_dim(values, 0, length + offset, axis=dim_at)
        widths[dim_at] = (-offset, 0)
    return jnp.pad(kept_part, widths)


def block_apply(blocks, values):
    return jnp.sum(blocks * values[None], axis=1)


def small_apply(matrix, values):
    return jnp.sum(matrix.reshape(matrix.shape + (1,) * (values.ndim - 1)) * values[None], axis=1)


def operate(values, diagonal, viscous, active, couplings, axis_set):
    carried = viscous[None] * values
    summed = jnp.zeros_like(values)
    for direction in range(6):
        dim_at = axis_set[DIRECTIONS[direction][0]]
        summed = summed + small_apply(couplings[direction], shifted(carried, dim_at, DIRECTIONS[direction][1]))
    return active[None] * block_apply(diagonal, active[None] * values) + (1.0 - active[None]) * values - viscous[None] * summed


def precondition(values, inverse, active):
    return active[None] * block_apply(inverse, values) + (1.0 - active[None]) * values


def local_solve(residual, diagonal, inverse, viscous, active, couplings, axis_set):
    initial = precondition(residual, inverse, active)
    return initial + precondition(residual - operate(initial, diagonal, viscous, active, couplings, axis_set), inverse, active)


def extend(values):
    leading = values.shape[:-2]
    blocks = values.reshape(leading + (N_GX, CX, N_GY, CY))
    edge_zero = jnp.zeros_like(blocks[..., :1, :1, :, :])
    west_rim = jnp.concatenate([edge_zero, blocks[..., :-1, CX - 1:, :, :]], axis=-4)
    east_rim = jnp.concatenate([blocks[..., 1:, :1, :, :], edge_zero], axis=-4)
    middle = jnp.concatenate([west_rim, blocks, east_rim], axis=-3)
    side_zero = jnp.zeros_like(blocks[..., :1, :1])
    south_rim = jnp.concatenate([side_zero, blocks[..., :-1, CY - 1:]], axis=-2)
    north_rim = jnp.concatenate([blocks[..., 1:, :1], side_zero], axis=-2)
    spread = [(0, 0)] * (len(leading) + 4)
    spread[-3] = (1, 1)
    south_rim = jnp.pad(south_rim, spread)
    north_rim = jnp.pad(north_rim, spread)
    return jnp.concatenate([south_rim, middle, north_rim], axis=-1)


def blend_weights(weight_pattern):
    col_at = lax.broadcasted_iota(jnp.int32, (NX, NY), 0)
    row_at = lax.broadcasted_iota(jnp.int32, (NX, NY), 1)
    west_on = ((col_at % CX == 0) & (col_at >= CX)).astype(jnp.float32)
    east_on = ((col_at % CX == CX - 1) & (col_at < NX - CX)).astype(jnp.float32)
    south_on = ((row_at % CY == 0) & (row_at >= CY)).astype(jnp.float32)
    north_on = ((row_at % CY == CY - 1) & (row_at < NY - CY)).astype(jnp.float32)
    shared = west_on + east_on + south_on + north_on
    own_weight = jnp.where(shared > 0, (1.0 + weight_pattern.astype(jnp.float32)) / 5.0, 1.0)
    near_weight = (1.0 - own_weight) / jnp.maximum(shared, 1.0)
    layout = (N_GX, CX, N_GY, CY)
    return own_weight.reshape(layout), near_weight.reshape(layout)


def schwarz(residual, diag_ext, inverse_ext, viscous_ext, active_ext, couplings, own_weight, near_weight):
    residual_ext = extend(residual)
    solved = local_solve(residual_ext, diag_ext, inverse_ext, viscous_ext, active_ext, couplings, (1, 3, 5))
    own_part = solved[:, :, :, 1:-1, :, 1:-1]
    gap_x = jnp.zeros_like(solved[:, :, :1, 0, :, 1:-1])
    from_east = jnp.concatenate([solved[:, :, 1:, 0, :, 1:-1], gap_x], axis=2)
    from_west = jnp.concatenate([gap_x, solved[:, :, :-1, -1, :, 1:-1]], axis=2)
    gap_y = jnp.zeros_like(solved[:, :, :, 1:-1, :1, 0])
    from_north = jnp.concatenate([solved[:, :, :, 1:-1, 1:, 0], gap_y], axis=4)
    from_south = jnp.concatenate([gap_y, solved[:, :, :, 1:-1, :-1, -1]], axis=4)
    nearby = jnp.zeros_like(own_part)
    nearby = nearby.at[:, :, :, 0].add(from_west)
    nearby = nearby.at[:, :, :, -1].add(from_east)
    nearby = nearby.at[:, :, :, :, :, 0].add(from_south)
    nearby = nearby.at[:, :, :, :, :, -1].add(from_north)
    combined = own_weight * own_part + near_weight * nearby
    return combined.reshape(residual.shape)


def reference(diag_block, block_inverse, viscosity, coupling, active_layers, grounded, weight_pattern, beta_step, base_vel):
    layer_at = lax.broadcasted_iota(jnp.int32, (L, NX, NY), 0)
    active = (layer_at < active_layers[None]).astype(jnp.float32)
    viscous = viscosity * active
    own_weight, near_weight = blend_weights(weight_pattern)
    viscous_ext = extend(viscous)
    active_ext = extend(active)
    diag_ext = extend(diag_block)
    inverse_ext = extend(block_inverse)
    coupling_t = jnp.stack([coupling[OPPOSITE[direction]].T for direction in range(6)])

    def solve(rhs, diagonal, diagonal_ext, inverse_blocks, couplings):
        solution = jnp.zeros_like(rhs)
        residual = rhs
        for sweep_at in range(SWEEPS):
            update = schwarz(residual, diagonal_ext, inverse_blocks, viscous_ext, active_ext, couplings, own_weight, near_weight)
            image = operate(update, diagonal, viscous, active, couplings, (1, 2, 3))
            omega = jnp.sum(residual * image) / (jnp.sum(image * image) + EPSILON)
            solution = solution + omega * update
            residual = residual - omega * image
        return solution

    grounded_f = grounded.astype(jnp.float32)
    basal = -(grounded_f * beta_step)[None] * base_vel
    rhs_forward = jnp.zeros((4, L, NX, NY), jnp.float32).at[0:2, 0].set(basal)
    increment = solve(rhs_forward, diag_block, diag_ext, inverse_ext, coupling)
    counts = active_layers.astype(jnp.float32)
    average = jnp.sum(active[None] * increment[0:2], axis=1) / counts[None]
    rhs_adjoint = jnp.zeros((4, L, NX, NY), jnp.float32).at[0:2].set(-active[None] * (average / counts[None])[:, None])
    adjoint = solve(rhs_adjoint, jnp.swapaxes(diag_block, 0, 1), jnp.swapaxes(diag_ext, 0, 1), jnp.swapaxes(inverse_ext, 0, 1), coupling_t)
    padded = jnp.pad(beta_step, 1)
    prior = 4.0 * beta_step - (padded[2:, 1:-1] + padded[:-2, 1:-1] + padded[1:-1, 2:] + padded[1:-1, :-2])
    data_term = grounded_f * (base_vel[0] * adjoint[0, 0] + base_vel[1] * adjoint[1, 0])
    hessian_vec = data_term + PRIOR_WEIGHT * prior
    return hessian_vec, adjoint
```

```python
import functools

import jax
import jax.numpy as jnp
from jax import lax
from jax.experimental import pallas as pl
from jax.experimental.pallas import tpu as pltpu
from jax.sharding import PartitionSpec as P

PRIOR_WEIGHT = 0.05
EPSILON = 1e-06
OPPOSITE = (1, 0, 3, 2, 5, 4)
F32 = jnp.float32
LAYERS = 6
ROWS = 2
COLS = 256
WIDE = 384
HALO = 8
INV_AT, VIS_AT, SMALL_AT, DIAG1_AT, GROUPS = 16, 48, 50, 52, 68
SENT = 52
COUNT_ROW, PATTERN_ROW, RHS_ROW, BETA_ROW = 0, 1, 2, 4
HALO_TILES = 9


def iota(shape, dim):
    return lax.broadcasted_iota(jnp.int32, shape, dim)


def edge_lanes(shape):
    lane = iota(shape, 1)
    return (lane < HALO) | (lane >= 128 - HALO)


def prep_kernel(diag, inv, visc, count, grounded, pattern, beta, vel, own, to_west, to_east, north, south):
    layer = iota((LAYERS, COLS), 0)
    actives = [layer < count[r : r + 1, :] for r in range(ROWS)]
    lane = iota((8, 128), 1)
    north[...] = jnp.zeros(north.shape, F32)
    south[...] = jnp.zeros(south.shape, F32)

    def put(group, values, tile, slot, west=None, east=None):
        own[group, 0:LAYERS, :] = values
        own[group, LAYERS:8, :] = jnp.zeros((8 - LAYERS, COLS), F32)
        whole = own[group]
        if west is not None:
            to_west[west] = whole
        if east is not None:
            to_east[east] = whole
        shift = slot * 16 + HALO
        north[tile] += pltpu.roll(jnp.where(lane >= 128 - HALO, whole[:, 128:], 0.0), shift, 1)
        south[tile] += pltpu.roll(jnp.where(lane < HALO, whole[:, :128], 0.0), shift, 1)

    for half in range(2):

        def body(k, carry):
            cp = half * 8 + k
            eye = jnp.where(cp % 5 == 0, 1.0, 0.0).astype(F32)
            for r in range(ROWS):
                at = INV_AT + cp * 2 + r
                put(at, jnp.where(actives[r], inv[cp, :, r, :], eye), r * 2 + half, k, at, at - 16)
                values = jnp.where(actives[r], diag[cp, :, r, :], eye)
                if r == 0:
                    put(cp, values, 4 + half, k, cp, None)
                else:
                    put(DIAG1_AT + cp, values, 6 + half, k, None, DIAG1_AT - 16 + cp)
            return carry

        lax.fori_loop(0, 8, body, 0)
    for r in range(ROWS):
        at = VIS_AT + r
        put(at, jnp.where(actives[r], visc[:, r, :], 0.0), 8, r, at, at - 16)
        at = SMALL_AT + r
        row = slice(r, r + 1)
        force = -(grounded[row, :].astype(F32) * beta[row, :])
        own[at] = jnp.zeros((8, COLS), F32)
        own[at, COUNT_ROW : COUNT_ROW + 1, :] = count[row, :].astype(F32)
        own[at, PATTERN_ROW : PATTERN_ROW + 1, :] = pattern[row, :].astype(F32)
        own[at, RHS_ROW : RHS_ROW + 1, :] = force * vel[0, row, :]
        own[at, RHS_ROW + 1 : RHS_ROW + 2, :] = force * vel[1, row, :]
        own[at, BETA_ROW : BETA_ROW + 1, :] = beta[row, :]
        put(at, own[at, 0:LAYERS, :], 8, 2 + r, at, at - 16)


def unpack(tile, slot):
    rolled = pltpu.roll(tile, 128 - HALO - 16 * slot, 1)
    return jnp.where(edge_lanes((8, 128)), rolled, 0.0)


def block_times(table, base, values, transposed):
    out = []
    for c in range(4):
        total = None
        for k in range(4):
            entry = table[base + (k * 4 + c if transposed else c * 4 + k)] * values[k]
            total = entry if total is None else total + entry
        out.append(total)
    return out


def coupled(coupling, direction, values, transposed, sums):
    for c in range(4):
        for k in range(4):
            if transposed:
                factor = coupling[OPPOSITE[direction] * 16 + k * 4 + c]
            else:
                factor = coupling[direction * 16 + c * 4 + k]
            entry = factor * values[k]
            sums[c] = entry if sums[c] is None else sums[c] + entry
    return sums


def stencil(field, base, coupling, transposed, kappa):
    here = [field[base + c] for c in range(4)]
    sums = [None] * 4
    sums = coupled(coupling, 0, [pltpu.roll(h, 7, 0) for h in here], transposed, sums)
    sums = coupled(coupling, 1, [pltpu.roll(h, 1, 0) for h in here], transposed, sums)

    def weighted(direction, tiles):
        if kappa is None:
            return tiles
        weight = kappa(direction)
        return [weight * t for t in tiles]

    sums = coupled(coupling, 2, weighted(0, [field[base + 4 + c] for c in range(4)]), transposed, sums)
    sums = coupled(coupling, 3, weighted(1, [field[base - 4 + c] for c in range(4)]), transposed, sums)
    sums = coupled(
        coupling, 4, weighted(2, [pltpu.roll(h, WIDE - 1, 1) for h in here]), transposed, sums
    )
    sums = coupled(coupling, 5, weighted(3, [pltpu.roll(h, 1, 1) for h in here]), transposed, sums)
    return sums


def sweep(vectors, res, first, carried, update, image, inv, diag, vis, kappa, coupling, transposed):
    def initial(i, carry):
        row = i % 6
        values = [res[i * 4 + c] for c in range(4)]
        nu = vis[row]
        for c, y in enumerate(block_times(inv, row * 16, values, transposed)):
            first[i * 4 + c] = y
            carried[i * 4 + c] = nu * y
        return carry

    lax.fori_loop(0, vectors * 6, initial, 0)

    def correct(i, carry):
        v, row = i // 4, i % 4 + 1
        base = (v * 6 + row) * 4
        nu = vis[row]
        sums = stencil(
            carried, base, coupling, transposed, lambda d: kappa[(row - 1) * 4 + d]
        )
        y0 = [first[base + c] for c in range(4)]
        own = block_times(diag, (row - 1) * 16, y0, transposed)
        rest = [res[base + c] - own[c] + nu * sums[c] for c in range(4)]
        for c, y in enumerate(block_times(inv, row * 16, rest, transposed)):
            update[base + c] = y0[c] + y
        return carry

    lax.fori_loop(0, vectors * 4, correct, 0)

    def carry_on(i, carry):
        v, row = i // 4, i % 4 + 1
        base = (v * 6 + row) * 4
        nu = vis[row]
        for c in range(4):
            carried[base + c] = nu * update[base + c]
        return carry

    lax.fori_loop(0, vectors * 4, carry_on, 0)

    def apply(i, carry):
        v, row = i // 2, i % 2 + 2
        base = (v * 6 + row) * 4
        sums = stencil(carried, base, coupling, transposed, None)
        own = block_times(diag, (row - 1) * 16, [update[base + c] for c in range(4)], transposed)
        nu = vis[row]
        for c in range(4):
            image[i * 4 + c] = own[c] - nu * sums[c]
        return carry

    lax.fori_loop(0, vectors * 2, apply, 0)


def send_rows(message, vector, tiles):
    packed = jnp.zeros((8, 128), F32)
    keep = edge_lanes((8, 128))
    for t in range(8):
        tile = tiles[t]
        message[vector * 17 + 2 * t] = tile[:, 0:128]
        message[vector * 17 + 2 * t + 1] = tile[:, 128:256]
        packed += pltpu.roll(jnp.where(keep, tile[:, 256:], 0.0), 16 * t + HALO, 1)
    message[vector * 17 + 16] = packed


def receive_rows(res, vector, own, west, east):
    for source, row_at in ((west, 0), (east, 4)):
        packed = source[vector * 17 + 16]
        for t in range(8):
            at = (vector * 6 + row_at) * 4 + t
            res[at, :, 0:128] = source[vector * 17 + 2 * t]
            res[at, :, 128:256] = source[vector * 17 + 2 * t + 1]
            res[at, :, 256:] = unpack(packed, t)
    for t in range(8):
        res[(vector * 6 + 2) * 4 + t] = own[vector * 8 + t]


def layer_sums(update, vector, active_of, put):
    for c in range(2):
        for r in range(ROWS):
            tile = update[(vector * 6 + 2 + r) * 4 + c] * active_of(r)
            put(c * 2 + r, jnp.sum(tile, axis=0, keepdims=True))


def setup_kernel(
    coupling, own, west, east, halo_own, halo_west, halo_east,
    inv, diag, vis, kappa, spread, residual, image, sums, prior,
    small, res, first, carried, update,
):
    gx, gy = lax.axis_index("gx"), lax.axis_index("gy")
    nx, ny = lax.axis_size("gx"), lax.axis_size("gy")
    sources = ((west, halo_west, 0, 16), (own, halo_own, 2, 0), (east, halo_east, 4, 0))

    def place(target, at, source, group, halos, tile, slot):
        target[at, :, 0:COLS] = source[group]
        target[at, :, COLS:] = unpack(halos[tile], slot)

    for half in range(2):

        def body(k, carry):
            cp = half * 8 + k
            for source, halos, row, drop in sources:
                for r in range(ROWS):
                    group = INV_AT + cp * 2 + r - drop
                    place(inv, (row + r) * 16 + cp, source, group, halos, r * 2 + half, k)
            place(diag, cp, west, DIAG1_AT - 16 + cp, halo_west, 6 + half, k)
            place(diag, 16 + cp, own, cp, halo_own, 4 + half, k)
            place(diag, 32 + cp, own, DIAG1_AT + cp, halo_own, 6 + half, k)
            place(diag, 48 + cp, east, cp, halo_east, 4 + half, k)
            return carry

        lax.fori_loop(0, 8, body, 0)
    for source, halos, row, drop in sources:
        for r in range(ROWS):
            place(vis, row + r, source, VIS_AT + r - drop, halos, 8, r)
            place(small, row + r, source, SMALL_AT + r - drop, halos, 8, 2 + r)

    lane = iota((1, WIDE), 1)
    column = jnp.where(lane < COLS, lane, jnp.where(lane < COLS + 64, lane - COLS, lane - 128))
    block_y = gy + jnp.where(lane < COLS, 0, jnp.where(lane < COLS + 64, 1, -1))
    south_on = jnp.where((column == 0) & (block_y > 0), 1.0, 0.0)
    north_on = jnp.where((column == COLS - 1) & (block_y < ny - 1), 1.0, 0.0)
    south_in = jnp.where(column == 0, 0.0, 1.0)
    north_in = jnp.where(column == COLS - 1, 0.0, 1.0)
    layer = iota((8, WIDE), 0)
    for row in range(6):
        tile = small[row]
        counts = tile[COUNT_ROW : COUNT_ROW + 1]
        whole = jnp.maximum(counts, 1.0)
        active = jnp.where(layer.astype(F32) < counts, 1.0, 0.0)
        spread[row] = -active / (whole * whole)
        for c in range(2):
            rhs = tile[RHS_ROW + c : RHS_ROW + c + 1]
            res[row * 4 + c] = jnp.where(layer == 0, rhs, 0.0)
        for c in range(2, 4):
            res[row * 4 + c] = jnp.zeros((8, WIDE), F32)
        if row == 0 or row == 5:
            continue
        block_x = gx + (row // 2 - 1)
        level = (1.0 + tile[PATTERN_ROW : PATTERN_ROW + 1]) / 5.0
        first_row = row % 2 == 0
        side = jnp.where(block_x > 0, 1.0, 0.0) if first_row else jnp.where(block_x < nx - 1, 1.0, 0.0)
        shared = south_on + north_on + side
        own_weight = jnp.where(shared > 0, level, 1.0)
        near = (1.0 - own_weight) / jnp.maximum(shared, 1.0)
        rim = near * (south_on + north_on)
        away = own_weight
        toward = own_weight + near * side
        east_part = away + rim if first_row else toward
        west_part = toward if first_row else away + rim
        north_part = own_weight + near * (north_on + side * north_in)
        south_part = own_weight + near * (south_on + side * south_in)
        for d, part in enumerate((east_part, west_part, north_part, south_part)):
            kappa[(row - 1) * 4 + d] = jnp.broadcast_to(part, (8, WIDE))

    prior[...] = jnp.zeros(prior.shape, F32)
    for r in range(ROWS):
        betas = [small[2 + r + k] for k in (-1, 0, 1)]
        around = (
            betas[0] + betas[2] + pltpu.roll(betas[1], 1, 1) + pltpu.roll(betas[1], WIDE - 1, 1)
        )
        line = 4.0 * betas[1] - around
        prior[r : r + 1, :] = line[BETA_ROW : BETA_ROW + 1, :COLS]

    sweep(1, res, first, carried, update, image, inv, diag, vis, kappa, coupling, False)
    for t in range(8):
        residual[t] = res[8 + t] - image[t]
    sums[...] = jnp.zeros(sums.shape, F32)

    def put(at, line):
        sums[at : at + 1, :] = line

    def active_of(r):
        return jnp.where(spread[2 + r] < 0.0, 1.0, 0.0)

    layer_sums(update, 0, active_of, put)


def first_kernel(*refs):
    outs = refs[7:16]
    message = refs[16]
    setup_kernel(*refs[:7], *outs, *refs[17:])
    residual = outs[5]
    send_rows(message, 0, [residual[t] for t in range(8)])


def dots_of(residual, image, last, pairs, vectors, lane):
    total = jnp.zeros((8, 128), F32)
    at = 0

    def dot(x, i, y, j):
        part = jnp.zeros((8, 128), F32)
        for t in range(8):
            product = x[i * 8 + t, :, 0:COLS] * y[j * 8 + t, :, 0:COLS]
            part += product[:, 0:128] + product[:, 128:256]
        return part

    for x, y in ((image, image), (residual, image), (residual, last), (image, last), (last, last)):
        for i, j in pairs:
            part = dot(x, i, y, j)
            if i != j and x is not y:
                part += dot(x, j, y, i)
            elif i != j:
                part += part
            line = jnp.sum(part, axis=0, keepdims=True)
            total += jnp.where(lane == at, jnp.sum(line, axis=1, keepdims=True), 0.0)
            at += 1
    return total


def second_kernel(
    coupling, inv, diag, vis, kappa, spread, residual, image, sums, west, east,
    uv, dots,
    res, first, carried, update, last,
):
    receive_rows(res, 0, residual, west, east)
    sweep(1, res, first, carried, update, last, inv, diag, vis, kappa, coupling, False)
    uv[0:4, :] = sums[0:4, :]

    def put(at, line):
        uv[4 + at : 5 + at, :] = line

    def active_of(r):
        return jnp.where(spread[2 + r] < 0.0, 1.0, 0.0)

    layer_sums(update, 0, active_of, put)
    dots[...] = dots_of(residual, image, last, ((0, 0),), 1, iota((8, 128), 1))


def third_kernel(
    coupling, inv, diag, vis, kappa, spread, uv, west, east,
    residual, image, start, message,
    res, first, carried, update,
):
    for v in range(2):
        for row in range(6):
            source = (west, uv, east)[row // 2]
            for c in range(2):
                at = v * 4 + c * 2 + row % 2
                res[(v * 6 + row) * 4 + c] = spread[row] * source[at : at + 1, :]
            for c in range(2, 4):
                res[(v * 6 + row) * 4 + c] = jnp.zeros((8, WIDE), F32)
    sweep(2, res, first, carried, update, image, inv, diag, vis, kappa, coupling, True)
    for v in range(2):
        for t in range(8):
            at = (v * 6 + 2) * 4 + t
            residual[v * 8 + t] = res[at] - image[v * 8 + t]
            start[v * 8 + t] = update[at, :, 0:COLS]
        send_rows(message, v, [residual[v * 8 + t] for t in range(8)])


def fourth_kernel(
    coupling, inv, diag, vis, kappa, residual, image, west, east, dots,
    end, spread_dots,
    res, first, carried, update, last,
):
    for v in range(2):
        receive_rows(res, v, residual, west, east)
    sweep(2, res, first, carried, update, last, inv, diag, vis, kappa, coupling, True)
    for v in range(2):
        for t in range(8):
            end[v * 8 + t] = update[(v * 6 + 2) * 4 + t, :, 0:COLS]
    lane = iota((8, 128), 1)
    pairs = ((0, 0), (0, 1), (1, 1))
    adjoint_dots = dots_of(residual, image, last, pairs, 2, lane - 5)
    line = (dots[...] + adjoint_dots)[0:1]
    spread_dots[...] = jnp.broadcast_to(line, spread_dots.shape)


def steps(image2, residual_image, residual_last, image_last, last2):
    one = (residual_image + image2) / (image2 + EPSILON)
    off = 1.0 - one
    along = off * residual_image + one * residual_last + off * off * image2 + off * one * image_last
    squared = off * off * image2 + 2.0 * off * one * image_last + one * one * last2
    two = along / (squared + EPSILON)
    return one + two * off, one * two


def final_kernel(dots, start, end, prior, grounded, vel, hessian, adjoint):
    line = jnp.sum(dots[...], axis=0, keepdims=True)
    lane = iota((1, 128), 1)

    def get(k):
        return jnp.sum(jnp.where(lane == k, line, 0.0), axis=1, keepdims=True)

    a, b = steps(*[get(k) for k in range(5)])
    kinds = []
    for k in range(5):
        at = 5 + 3 * k
        kinds.append(a * a * get(at) + a * b * get(at + 1) + b * b * get(at + 2))
    p, q = steps(*kinds)
    weights = (p * a, p * b, q * a, q * b)
    lines = []
    for r in range(ROWS):
        for c in range(4):
            t = r * 4 + c
            total = (
                weights[0] * start[t]
                + weights[1] * start[8 + t]
                + weights[2] * end[t]
                + weights[3] * end[8 + t]
            )
            adjoint[c, :, r, :] = total[0:LAYERS]
            lines.append(total[0:1])
    for r in range(ROWS):
        row = slice(r, r + 1)
        data = grounded[row, :].astype(F32) * (
            vel[0, row, :] * lines[r * 4] + vel[1, row, :] * lines[r * 4 + 1]
        )
        hessian[row, :] = data + PRIOR_WEIGHT * prior[row, :]


VMEM = pl.BlockSpec(memory_space=pltpu.VMEM)
SMEM = pl.BlockSpec(memory_space=pltpu.SMEM)


def call(kernel, name, operands, outs, scratch=(), smem=True):
    return pl.pallas_call(
        kernel,
        out_shape=[jax.ShapeDtypeStruct(shape, F32) for shape in outs],
        in_specs=[SMEM if i == 0 and smem else VMEM for i in range(len(operands))],
        out_specs=[VMEM] * len(outs),
        scratch_shapes=[pltpu.VMEM(shape, F32) for shape in scratch],
        compiler_params=pltpu.CompilerParams(vmem_limit_bytes=40 * 1024 * 1024),
        name=name,
    )(*operands)


def shift_pairs(axis, step):
    count = lax.axis_size(axis)
    return [(i, i + step) for i in range(count) if 0 <= i + step < count]


def from_low(values, axis):
    return lax.ppermute(values, axis, shift_pairs(axis, 1))


def from_high(values, axis):
    return lax.ppermute(values, axis, shift_pairs(axis, -1))


def total_over(lines, axis, fan_out):
    swapped = lax.all_to_all(lines, axis, 0, 0, tiled=True)
    if fan_out is None:
        return swapped
    return jnp.broadcast_to(jnp.sum(swapped, axis=0, keepdims=True), (fan_out, 128))


def per_device(
    diag_block,
    block_inverse,
    viscosity,
    coupling,
    active_layers,
    grounded,
    weight_pattern,
    beta_step,
    base_vel,
):
    table = (16,) + viscosity.shape
    factors = coupling.reshape(96)
    own, to_west, to_east, to_north, to_south = call(
        prep_kernel,
        "prepare",
        [
            diag_block.reshape(table),
            block_inverse.reshape(table),
            viscosity,
            active_layers,
            grounded,
            weight_pattern,
            beta_step,
            base_vel,
        ],
        [
            (GROUPS, 8, COLS),
            (SENT, 8, COLS),
            (SENT, 8, COLS),
            (HALO_TILES, 8, 128),
            (HALO_TILES, 8, 128),
        ],
        smem=False,
    )
    halo_own = from_low(to_north, "gy") + from_high(to_south, "gy")
    west, east = from_low(to_east, "gx"), from_high(to_west, "gx")
    halo_west, halo_east = from_low(halo_own, "gx"), from_high(halo_own, "gx")

    def field(count):
        return (count, 8, WIDE)

    def work(vectors):
        return [field(24 * vectors)] * 4

    inv, diag, vis, kappa, spread, residual, image, sums, prior, message = call(
        first_kernel,
        "forward_first",
        [factors, own, west, east, halo_own, halo_west, halo_east],
        [
            field(96),
            field(64),
            field(6),
            field(16),
            field(6),
            field(8),
            field(8),
            (8, WIDE),
            (8, COLS),
            (17, 8, 128),
        ],
        [field(6)] + work(1),
    )
    west, east = from_low(message, "gx"), from_high(message, "gx")
    uv, dots = call(
        second_kernel,
        "forward_second",
        [factors, inv, diag, vis, kappa, spread, residual, image, sums, west, east],
        [(8, WIDE), (8, 128)],
        work(1) + [field(8)],
    )
    west, east = from_low(uv, "gx"), from_high(uv, "gx")
    residual, image, start, message = call(
        third_kernel,
        "adjoint_first",
        [factors, inv, diag, vis, kappa, spread, uv, west, east],
        [field(16), field(16), (16, 8, COLS), (34, 8, 128)],
        work(2),
    )
    west, east = from_low(message, "gx"), from_high(message, "gx")
    n_gx, n_gy = lax.axis_size("gx"), lax.axis_size("gy")
    end, lines = call(
        fourth_kernel,
        "adjoint_second",
        [factors, inv, diag, vis, kappa, residual, image, west, east, dots],
        [(16, 8, COLS), (n_gx, 128)],
        work(2) + [field(16)],
    )
    lines = total_over(lines, "gx", n_gy)
    lines = total_over(lines, "gy", None)
    hessian_vec, adjoint = call(
        final_kernel,
        "combine",
        [lines, start, end, prior, grounded, base_vel],
        [beta_step.shape, (4,) + viscosity.shape],
        smem=False,
    )
    return hessian_vec, adjoint


def solution(mesh):
    placed = (
        P(None, None, None, "gx", "gy"),
        P(None, None, None, "gx", "gy"),
        P(None, "gx", "gy"),
        P(),
        P("gx", "gy"),
        P("gx", "gy"),
        P("gx", "gy"),
        P("gx", "gy"),
        P(None, "gx", "gy"),
    )
    return jax.shard_map(
        per_device,
        mesh=mesh,
        in_specs=placed,
        out_specs=(P("gx", "gy"), P(None, None, "gx", "gy")),
        check_vma=False,
    )
```

```python
import jax
import jax.numpy as jnp
from jax import lax
from jax.experimental import pallas as pl
from jax.experimental.pallas import tpu as pltpu
from jax.sharding import PartitionSpec as P

PRIOR_WEIGHT = 0.05
EPSILON = 1e-06
OPPOSITE = (1, 0, 3, 2, 5, 4)
F32 = jnp.float32
LAYERS = 6
ROWS = 2
COLS = 256
CHUNK = 8
SLOTS = 16
OWN = 1
COUNT_ROW, PATTERN_ROW, RHS_ROW, BETA_ROW = 0, 1, 2, 4
SPARE = 6


def iota(shape, dim):
    return lax.broadcasted_iota(jnp.int32, shape, dim)


def swap_slots(tiles):
    slot = iota((8, 128), 1) // CHUNK
    tiles = list(tiles)
    for bit in (1, 2, 4, 8):
        odd = (slot & bit) != 0
        for i in range(SLOTS):
            if i & bit:
                continue
            low, high = tiles[i], tiles[i | bit]
            tiles[i] = jnp.where(odd, pltpu.roll(high, CHUNK * bit, 1), low)
            tiles[i | bit] = jnp.where(odd, high, pltpu.roll(low, 128 - CHUNK * bit, 1))
    return tiles


def pack_kernel(
    diag_in, inv_in, visc_in, count_in, grounded_in, pattern_in, beta_in, vel_in, message,
    diag, inv, visc, count, grounded, pattern, beta, vel, folded, arrived,
):
    pairs = (
        (count_in, count), (diag_in, diag), (inv_in, inv), (visc_in, visc), (grounded_in, grounded),
        (pattern_in, pattern), (beta_in, beta), (vel_in, vel),
    )
    copies = [
        pltpu.make_async_copy(source, target, arrived.at[i])
        for i, (source, target) in enumerate(pairs)
    ]
    for copy in copies:
        copy.start()
    folded[...] = jnp.zeros(folded.shape, F32)
    for copy in copies:
        copy.wait()
    layer = iota((LAYERS, COLS), 0)
    actives = [layer < count[r : r + 1, :] for r in range(ROWS)]

    def fold(cp, carry):
        eye = jnp.where(cp % 5 == 0, 1.0, 0.0).astype(F32)
        for t, table in enumerate((inv, diag)):
            for r in range(ROWS):
                values = jnp.where(actives[r], table[cp, :, r, :], eye)
                for part in range(2):
                    folded[(t * 2 + r) * 2 + part, cp, 0:LAYERS, :] = values[
                        :, part * 128 : part * 128 + 128
                    ]
        return carry

    lax.fori_loop(0, 16, fold, 0)
    for r in range(ROWS):
        row = slice(r, r + 1)
        viscous = jnp.where(actives[r], visc[:, r, :], 0.0)
        force = -(grounded[row, :].astype(F32) * beta[row, :])
        lines = [viscous[k : k + 1] for k in range(LAYERS)]
        lines += [count[row, :].astype(F32), pattern[row, :].astype(F32)]
        lines += [force * vel[0, row, :], force * vel[1, row, :], beta[row, :]]
        for slot, line in enumerate(lines):
            for part in range(2):
                folded[r * 2 + part, slot, SPARE : SPARE + 1, :] = line[
                    :, part * 128 : part * 128 + 128
                ]

    def send(i, carry):
        tiles = swap_slots([folded[i, cp] for cp in range(16)])
        for k in range(SLOTS):
            message[(i % 2) * SLOTS + k, i // 2] = tiles[k]
        return carry

    lax.fori_loop(0, 8, send, 0)


def block_times(table, base, values, transposed):
    out = []
    for c in range(4):
        total = None
        for k in range(4):
            entry = table[base + (k * 4 + c if transposed else c * 4 + k)] * values[k]
            total = entry if total is None else total + entry
        out.append(total)
    return out


def coupled(coupling, direction, values, transposed, sums):
    for c in range(4):
        for k in range(4):
            if transposed:
                factor = coupling[OPPOSITE[direction] * 16 + k * 4 + c]
            else:
                factor = coupling[direction * 16 + c * 4 + k]
            entry = factor * values[k]
            sums[c] = entry if sums[c] is None else sums[c] + entry
    return sums


def x_plus(v):
    first = iota((8, 128), 1) < CHUNK
    inner = pltpu.roll(jnp.where(first, v[2], v[0]), 128 - CHUNK, 1)
    outer = pltpu.roll(jnp.where(first, 0.0, v[2]), 128 - CHUNK, 1)
    return jnp.stack([v[1], inner, v[3], outer])


def x_minus(v):
    last = iota((8, 128), 1) >= 128 - CHUNK
    outer = pltpu.roll(jnp.where(last, 0.0, v[1]), CHUNK, 1)
    inner = pltpu.roll(jnp.where(last, v[1], v[3]), CHUNK, 1)
    return jnp.stack([outer, v[0], inner, v[2]])


def y_plus(v, after):
    column = iota((4, 8, 128), 2) % CHUNK
    return jnp.where(
        column < CHUNK - 1, pltpu.roll(v, 127, 2), pltpu.roll(after, CHUNK - 1, 2)
    )


def y_minus(v, before):
    column = iota((4, 8, 128), 2) % CHUNK
    return jnp.where(column > 0, pltpu.roll(v, 1, 2), pltpu.roll(before, 128 - CHUNK + 1, 2))


def stencil(field, base, coupling, transposed, kappa):
    here = [field[base + c] for c in range(4)]
    sums = [None] * 4
    sums = coupled(coupling, 0, [pltpu.roll(h, 7, 1) for h in here], transposed, sums)
    sums = coupled(coupling, 1, [pltpu.roll(h, 1, 1) for h in here], transposed, sums)

    def weighted(direction, tiles):
        if kappa is None:
            return tiles
        weight = kappa(direction)
        return [weight * t for t in tiles]

    moved = weighted(0, [x_plus(h) for h in here])
    sums = coupled(coupling, 2, moved, transposed, sums)
    moved = weighted(1, [x_minus(h) for h in here])
    sums = coupled(coupling, 3, moved, transposed, sums)
    moved = weighted(2, [y_plus(here[c], field[base + 4 + c]) for c in range(4)])
    sums = coupled(coupling, 4, moved, transposed, sums)
    moved = weighted(3, [y_minus(here[c], field[base - 4 + c]) for c in range(4)])
    return coupled(coupling, 5, moved, transposed, sums)


def sweep(vectors, res, first, carried, update, image, own_only, tables, transposed):
    inv, diag, vis, kappa, coupling = tables

    def initial(i, carry):
        v, j = i // 3, i % 3
        at = (v * 5 + j + 1) * 4
        nu = vis[j]
        values = [res[i * 4 + c] for c in range(4)]
        for c, y in enumerate(block_times(inv, j * 16, values, transposed)):
            first[i * 4 + c] = y
            carried[at + c] = nu * y
        return carry

    lax.fori_loop(0, vectors * 3, initial, 0)

    def correct(i, carry):
        v, j = i // 3, i % 3
        at = (v * 5 + j + 1) * 4
        nu = vis[j]
        sums = stencil(carried, at, coupling, transposed, lambda d: kappa[j * 4 + d])
        y0 = [first[i * 4 + c] for c in range(4)]
        own = block_times(diag, j * 16, y0, transposed)
        rest = [res[i * 4 + c] - own[c] + nu * sums[c] for c in range(4)]
        for c, y in enumerate(block_times(inv, j * 16, rest, transposed)):
            update[i * 4 + c] = y0[c] + y
        return carry

    lax.fori_loop(0, vectors * 3, correct, 0)

    def carry_on(i, carry):
        v, j = i // 3, i % 3
        nu = vis[j]
        for c in range(4):
            carried[(v * 5 + j + 1) * 4 + c] = nu * update[i * 4 + c]
        return carry

    lax.fori_loop(0, vectors * 3, carry_on, 0)

    def apply(i, carry):
        v, j = (i, OWN) if own_only else (i // 3, i % 3)
        sums = stencil(carried, (v * 5 + j + 1) * 4, coupling, transposed, None)
        values = [update[(v * 3 + j) * 4 + c] for c in range(4)]
        own = block_times(diag, j * 16, values, transposed)
        nu = vis[j]
        for c in range(4):
            image[i * 4 + c] = own[c] - nu * sums[c]
        return carry

    lax.fori_loop(0, vectors if own_only else vectors * 3, apply, 0)


def dots_of(residual, image, last, pairs, at):
    lane = iota((1, 128), 1)
    total = jnp.zeros((1, 128), F32)

    def own(ref, v):
        if ref is last:
            return [ref[v * 4 + c] for c in range(4)]
        return [ref[(v * 3 + OWN) * 4 + c] for c in range(4)]

    def dot(x, i, y, j):
        part = None
        for a, b in zip(own(x, i), own(y, j)):
            part = a * b if part is None else part + a * b
        return part

    for x, y in ((image, image), (residual, image), (residual, last), (image, last), (last, last)):
        for i, j in pairs:
            part = dot(x, i, y, j)
            if i != j:
                part += part if x is y else dot(x, j, y, i)
            tile = (part[0] + part[1]) + (part[2] + part[3])
            line = jnp.sum(tile, axis=0, keepdims=True)
            total += jnp.where(lane == at, jnp.sum(line, axis=1, keepdims=True), 0.0)
            at += 1
    return total


def layer_sums(update, spread, target, vector):
    for j in range(3):
        weight = spread[j]
        active = jnp.where(weight < 0.0, 1.0, 0.0)
        for c in range(2):
            total = jnp.sum(active * update[j * 4 + c], axis=1, keepdims=True)
            target[(vector * 3 + j) * 4 + c] = weight * total
        for c in range(2, 4):
            target[(vector * 3 + j) * 4 + c] = jnp.zeros((4, 8, 128), F32)


def unpack(block, j, inv, diag, vis, small):
    sub = iota((8, 128), 0)

    def place(i, carry):
        half, r = i // 2, i % 2
        tiles = swap_slots([block[half * SLOTS + s, r] for s in range(SLOTS)])
        for cp in range(16):
            inv[j * 16 + cp, i] = jnp.where(sub < LAYERS, tiles[cp], 0.0)
        for target, base, lines in ((vis, 0, LAYERS), (small, LAYERS, 5)):
            total = jnp.zeros((8, 128), F32)
            for k in range(lines):
                total = jnp.where(sub == k, pltpu.roll(tiles[base + k], (k - SPARE) % 8, 0), total)
            target[j, i] = total
        tiles = swap_slots([block[half * SLOTS + s, 2 + r] for s in range(SLOTS)])
        for cp in range(16):
            diag[j * 16 + cp, i] = tiles[cp]
        return carry

    lax.fori_loop(0, 4, place, 0)


def solve_kernel(
    coupling, low, mine, high, message,
    inv, diag, vis, small, kappa, spread, res, res_two, first, carried, update, image, last, start, lines,
):
    gx, gy = lax.axis_index("gx"), lax.axis_index("gy")
    nx, ny = lax.axis_size("gx"), lax.axis_size("gy")
    for j, block in enumerate((low, mine, high)):
        unpack(block, j, inv, diag, vis, small)
    for v in range(2):
        for c in range(4):
            carried[v * 20 + c] = jnp.zeros((4, 8, 128), F32)
            carried[v * 20 + 16 + c] = jnp.zeros((4, 8, 128), F32)

    shape = (4, 8, 128)
    layer = iota(shape, 1)
    lane = iota(shape, 2)
    source = (iota(shape, 0) // 2) * SLOTS + lane // CHUNK
    low_row = iota(shape, 0) % 2 == 0
    for j in range(3):
        tiles = small[j]
        counts = tiles[:, COUNT_ROW : COUNT_ROW + 1, :]
        whole = jnp.maximum(counts, 1.0)
        active = jnp.where(layer.astype(F32) < counts, 1.0, 0.0)
        spread[j] = -active / (whole * whole)
        for c in range(2):
            rhs = tiles[:, RHS_ROW + c : RHS_ROW + c + 1, :]
            res[j * 4 + c] = jnp.where(layer == 0, rhs, 0.0)
        for c in range(2, 4):
            res[j * 4 + c] = jnp.zeros(shape, F32)
        column = (gy * COLS + gx * CHUNK + (j - OWN) * CHUNK) + lane % CHUNK
        within = column & (COLS - 1)
        south_on = jnp.where((within == 0) & (column > 0), 1.0, 0.0)
        north_on = jnp.where((within == COLS - 1) & (column < ny * COLS - 1), 1.0, 0.0)
        south_in = jnp.where(within == 0, 0.0, 1.0)
        north_in = jnp.where(within == COLS - 1, 0.0, 1.0)
        side_exists = (low_row & (source > 0)) | (jnp.logical_not(low_row) & (source < nx - 1))
        side = jnp.where(side_exists, 1.0, 0.0)
        shared = south_on + north_on + side
        level = (1.0 + tiles[:, PATTERN_ROW : PATTERN_ROW + 1, :]) / 5.0
        own_weight = jnp.where(shared > 0.0, level, 1.0)
        near = (1.0 - own_weight) / jnp.maximum(shared, 1.0)
        inward = own_weight + near * (south_on + north_on)
        outward = own_weight + near * side
        kappa[j * 4] = jnp.where(low_row, inward, outward)
        kappa[j * 4 + 1] = jnp.where(low_row, outward, inward)
        kappa[j * 4 + 2] = own_weight + near * (north_on + side * north_in)
        kappa[j * 4 + 3] = own_weight + near * (south_on + side * south_in)

    tables = (inv, diag, vis, kappa, coupling)
    sweep(1, res, first, carried, update, image, False, tables, False)
    layer_sums(update, spread, res_two, 0)
    for t in range(12):
        res[t] = res[t] - image[t]
    sweep(1, res, first, carried, update, last, True, tables, False)
    layer_sums(update, spread, res_two, 1)
    lines[0:1, :] = dots_of(res, image, last, ((0, 0),), 0)

    sweep(2, res_two, first, carried, update, image, False, tables, True)
    for v in range(2):
        for c in range(4):
            start[v * 4 + c] = update[(v * 3 + OWN) * 4 + c]
    for t in range(24):
        res_two[t] = res_two[t] - image[t]
    sweep(2, res_two, first, carried, update, last, True, tables, True)
    dots = lines[0:1, :] + dots_of(res_two, image, last, ((0, 0), (0, 1), (1, 1)), 5)

    before, here, after = small[0], small[1], small[2]
    around = x_plus(here) + x_minus(here) + y_plus(here, after) + y_minus(here, before)
    first[0] = 4.0 * here - around
    sub = iota((8, 128), 0)

    def send(i, carry):
        half, r = i // 2, i % 2
        tiles = [start[k, i] for k in range(8)]
        tiles += [update[(v * 3 + OWN) * 4 + c, i] for v in range(2) for c in range(4)]
        prior = pltpu.roll(first[0, i], SPARE - BETA_ROW, 0)
        tiles[0] = jnp.where(sub == SPARE, prior, tiles[0])
        tiles = swap_slots(tiles)
        for s in range(SLOTS):
            message[half * SLOTS + s, r] = jnp.where(sub == 7, dots, tiles[s])
        return carry

    lax.fori_loop(0, 4, send, 0)


def steps(image2, residual_image, residual_last, image_last, last2):
    one = (residual_image + image2) / (image2 + EPSILON)
    off = 1.0 - one
    along = off * residual_image + one * residual_last + off * off * image2 + off * one * image_last
    squared = off * off * image2 + 2.0 * off * one * image_last + one * one * last2
    two = along / (squared + EPSILON)
    return one + two * off, one * two


def gather_kernel(block, lines):
    total = None
    for k in range(block.shape[0]):
        line = block[k, 0, 7:8, :]
        total = line if total is None else total + line
    lines[...] = jnp.broadcast_to(total, lines.shape)


def final_kernel(dots, block, grounded, vel, hessian, adjoint):
    line = jnp.sum(dots[...], axis=0, keepdims=True)
    lane = iota((1, 128), 1)

    def get(k):
        return jnp.sum(jnp.where(lane == k, line, 0.0), axis=1, keepdims=True)

    a, b = steps(*[get(k) for k in range(5)])
    kinds = []
    for k in range(5):
        at = 5 + 3 * k
        kinds.append(a * a * get(at) + a * b * get(at + 1) + b * b * get(at + 2))
    p, q = steps(*kinds)
    shape = (8, 128)
    vector = iota(shape, 1) // 32
    slot = iota(shape, 1) // CHUNK
    sub = iota(shape, 0)
    weights = jnp.where(
        vector == 0, p * a, jnp.where(vector == 1, p * b, jnp.where(vector == 2, q * a, q * b))
    )
    weights = jnp.where(sub < LAYERS, weights, jnp.where((sub == SPARE) & (slot == 0), 1.0, 0.0))
    for r in range(ROWS):
        heads = []
        for part in range(2):
            out = [None] * 4
            for k in range(SLOTS):
                tile = block[part * SLOTS + k, r] * weights
                tile = tile + pltpu.roll(tile, 64, 1)
                tile = tile + pltpu.roll(tile, 32, 1)
                for c in range(4):
                    turn = (CHUNK * (k - c)) % 32
                    moved = tile if turn == 0 else pltpu.roll(tile, turn, 1)
                    out[c] = moved if out[c] is None else jnp.where(slot == k, moved, out[c])
            at = slice(part * 128, part * 128 + 128)
            for c in range(4):
                adjoint[c, :, r, at] = out[c][0:LAYERS]
            row = slice(r, r + 1)
            data = grounded[row, at].astype(F32) * (
                vel[0, row, at] * out[0][0:1] + vel[1, row, at] * out[1][0:1]
            )
            hessian[row, at] = data + PRIOR_WEIGHT * out[0][SPARE : SPARE + 1]


VMEM = pl.BlockSpec(memory_space=pltpu.VMEM)
SMEM = pl.BlockSpec(memory_space=pltpu.SMEM)
HBM = pl.BlockSpec(memory_space=pltpu.HBM)


def call(kernel, name, operands, in_specs, outs, scratch=()):
    return pl.pallas_call(
        kernel,
        out_shape=[jax.ShapeDtypeStruct(shape, F32) for shape in outs],
        in_specs=in_specs,
        out_specs=[VMEM] * len(outs),
        scratch_shapes=scratch,
        compiler_params=pltpu.CompilerParams(vmem_limit_bytes=40 * 1024 * 1024),
        name=name,
    )(*operands)


def neighbour_pairs(step):
    n_gx, n_gy = lax.axis_size("gx"), lax.axis_size("gy")
    pairs = []
    for source in range(n_gx * n_gy):
        target = source + step
        if 0 <= target < n_gx * n_gy:
            pairs.append(
                tuple((i % n_gx) * n_gy + i // n_gx for i in (source, target))
            )
    return pairs


def per_device(
    diag_block,
    block_inverse,
    viscosity,
    coupling,
    active_layers,
    grounded,
    weight_pattern,
    beta_step,
    base_vel,
):
    n_gx, n_gy = lax.axis_size("gx"), lax.axis_size("gy")
    table = (16,) + viscosity.shape
    raw = [
        diag_block.reshape(table),
        block_inverse.reshape(table),
        viscosity,
        active_layers,
        grounded,
        weight_pattern,
        beta_step,
        base_vel,
    ]
    (sent,) = call(
        pack_kernel,
        "pack_tables",
        raw,
        [HBM] * 8,
        [(n_gx, 4, 8, 128)],
        [pltpu.VMEM(x.shape, x.dtype) for x in raw]
        + [pltpu.VMEM((8, 16, 8, 128), F32), pltpu.SemaphoreType.DMA((8,))],
    )
    mine = lax.all_to_all(sent, "gx", 0, 0, tiled=True)
    low = lax.ppermute(mine, ("gx", "gy"), neighbour_pairs(1))
    high = lax.ppermute(mine, ("gx", "gy"), neighbour_pairs(-1))

    def field(count):
        return pltpu.VMEM((count, 4, 8, 128), F32)

    (back,) = call(
        solve_kernel,
        "solve_both",
        [coupling.reshape(96), low, mine, high],
        [SMEM, VMEM, VMEM, VMEM],
        [(n_gx, 2, 8, 128)],
        [
            field(48),
            field(48),
            field(3),
            field(3),
            field(12),
            field(3),
            field(12),
            field(24),
            field(24),
            field(40),
            field(24),
            field(24),
            field(8),
            field(8),
            pltpu.VMEM((8, 128), F32),
        ],
    )
    block = lax.all_to_all(back, "gx", 0, 0, tiled=True)
    (lines,) = call(gather_kernel, "sum_gx", [block], [VMEM], [(n_gy, 128)])
    lines = lax.all_to_all(lines, "gy", 0, 0, tiled=True)
    hessian_vec, adjoint = call(
        final_kernel,
        "combine",
        [lines, block, grounded, base_vel],
        [VMEM] * 4,
        [beta_step.shape, (4,) + viscosity.shape],
    )
    return hessian_vec, adjoint


def solution(mesh):
    placed = (
        P(None, None, None, "gx", "gy"),
        P(None, None, None, "gx", "gy"),
        P(None, "gx", "gy"),
        P(),
        P("gx", "gy"),
        P("gx", "gy"),
        P("gx", "gy"),
        P("gx", "gy"),
        P(None, "gx", "gy"),
    )
    return jax.shard_map(
        per_device,
        mesh=mesh,
        in_specs=placed,
        out_specs=(P("gx", "gy"), P(None, None, "gx", "gy")),
        check_vma=False,
    )
```

```python
import jax
import jax.numpy as jnp
from jax import lax
from jax.experimental import pallas as pl
from jax.experimental.pallas import tpu as pltpu
from jax.sharding import PartitionSpec as P

PRIOR_WEIGHT = 0.05
EPSILON = 1e-06
OPPOSITE = (1, 0, 3, 2, 5, 4)
F32 = jnp.float32
LAYERS = 6
ROWS = 2
COLS = 256
CHUNK = 8
SLOTS = 16
OWN, NEAR = 1, 3
COUNT_ROW, PATTERN_ROW, RHS_ROW, BETA_ROW = 0, 1, 2, 4
SPARE = 6


def iota(shape, dim):
    return lax.broadcasted_iota(jnp.int32, shape, dim)


def turned(tiles):
    return tiles.reshape(128, 128).T.reshape(SLOTS, 8, 128)


def pack_kernel(
    diag_in, inv_in, visc_in, count_in, grounded_in, pattern_in, beta_in, vel_in, message,
    diag, inv, visc, count, grounded, pattern, beta, vel, folded, arrived,
):
    pairs = (
        (count_in, count), (diag_in, diag), (inv_in, inv), (visc_in, visc), (grounded_in, grounded),
        (pattern_in, pattern), (beta_in, beta), (vel_in, vel),
    )
    copies = [
        pltpu.make_async_copy(source, target, arrived.at[i])
        for i, (source, target) in enumerate(pairs)
    ]
    for copy in copies:
        copy.start()
    folded[...] = jnp.zeros(folded.shape, F32)
    for copy in copies:
        copy.wait()
    layer = iota((LAYERS, COLS), 0)
    actives = [layer < count[r : r + 1, :] for r in range(ROWS)]

    def fold(cp, carry):
        eye = jnp.where(cp % 5 == 0, 1.0, 0.0).astype(F32)
        for t, table in enumerate((inv, diag)):
            for r in range(ROWS):
                values = jnp.where(actives[r], table[cp, :, r, :], eye)
                for part in range(2):
                    folded[(t * 2 + r) * 2 + part, cp, 0:LAYERS, :] = values[
                        :, part * 128 : part * 128 + 128
                    ]
        return carry

    lax.fori_loop(0, 16, fold, 0)
    for r in range(ROWS):
        row = slice(r, r + 1)
        viscous = jnp.where(actives[r], visc[:, r, :], 0.0)
        force = -(grounded[row, :].astype(F32) * beta[row, :])
        lines = [viscous[k : k + 1] for k in range(LAYERS)]
        lines += [count[row, :].astype(F32), pattern[row, :].astype(F32)]
        lines += [force * vel[0, row, :], force * vel[1, row, :], beta[row, :]]
        for slot, line in enumerate(lines):
            for part in range(2):
                folded[r * 2 + part, slot, SPARE : SPARE + 1, :] = line[
                    :, part * 128 : part * 128 + 128
                ]

    for i in range(8):
        part = slice((i % 2) * SLOTS, (i % 2) * SLOTS + SLOTS)
        message[part, i // 2] = turned(folded[i])


def block_times(table, base, values, transposed):
    out = []
    for c in range(4):
        total = None
        for k in range(4):
            entry = table[base + (k * 4 + c if transposed else c * 4 + k)] * values[k]
            total = entry if total is None else total + entry
        out.append(total)
    return out


def coupled(coupling, direction, values, transposed, sums):
    for c in range(4):
        for k in range(4):
            if transposed:
                factor = coupling[OPPOSITE[direction] * 16 + k * 4 + c]
            else:
                factor = coupling[direction * 16 + c * 4 + k]
            entry = factor * values[k]
            sums[c] = entry if sums[c] is None else sums[c] + entry
    return sums


def x_plus(v):
    first = iota((8, 128), 1) < CHUNK
    inner = pltpu.roll(jnp.where(first, v[2], v[0]), 128 - CHUNK, 1)
    outer = pltpu.roll(jnp.where(first, 0.0, v[2]), 128 - CHUNK, 1)
    return jnp.stack([v[1], inner, v[3], outer])


def x_minus(v):
    last = iota((8, 128), 1) >= 128 - CHUNK
    outer = pltpu.roll(jnp.where(last, 0.0, v[1]), CHUNK, 1)
    inner = pltpu.roll(jnp.where(last, v[1], v[3]), CHUNK, 1)
    return jnp.stack([outer, v[0], inner, v[2]])


def y_plus(v, after):
    column = iota((4, 8, 128), 2) % CHUNK
    return jnp.where(
        column < CHUNK - 1, pltpu.roll(v, 127, 2), pltpu.roll(after, CHUNK - 1, 2)
    )


def y_minus(v, before):
    column = iota((4, 8, 128), 2) % CHUNK
    return jnp.where(column > 0, pltpu.roll(v, 1, 2), pltpu.roll(before, 128 - CHUNK + 1, 2))


def stencil(field, base, after, before, coupling, transposed, kappa):
    here = [field[base + c] for c in range(4)]
    sums = [None] * 4
    sums = coupled(coupling, 0, [pltpu.roll(h, 7, 1) for h in here], transposed, sums)
    sums = coupled(coupling, 1, [pltpu.roll(h, 1, 1) for h in here], transposed, sums)

    def weighted(direction, tiles):
        if kappa is None:
            return tiles
        weight = kappa(direction)
        return [weight * t for t in tiles]

    moved = weighted(0, [x_plus(h) for h in here])
    sums = coupled(coupling, 2, moved, transposed, sums)
    moved = weighted(1, [x_minus(h) for h in here])
    sums = coupled(coupling, 3, moved, transposed, sums)
    moved = weighted(2, [y_plus(here[c], field[after + c]) for c in range(4)])
    sums = coupled(coupling, 4, moved, transposed, sums)
    moved = weighted(3, [y_minus(here[c], field[before + c]) for c in range(4)])
    return coupled(coupling, 5, moved, transposed, sums)


class Forward:
    count, transposed, own = 3, False, 1

    def block(i):
        return i

    def place(i):
        return (i + 1) * 4, (i + 2) * 4, i * 4


class Adjoint:
    count, transposed, own = 4, True, 2

    def block(i):
        return (i % 2) * 2 + 1

    def place(i):
        other = (i + 1 - 2 * (i % 2)) * 4
        return i * 4, other, other


def sweep(kind, res, first, carried, update, image, own_only, tables):
    inv, diag, vis, kappa, coupling = tables
    transposed = kind.transposed

    def initial(i, carry):
        j = kind.block(i)
        at = kind.place(i)[0]
        nu = vis[j]
        values = [res[i * 4 + c] for c in range(4)]
        for c, y in enumerate(block_times(inv, j * 16, values, transposed)):
            first[i * 4 + c] = y
            carried[at + c] = nu * y
        return carry

    lax.fori_loop(0, kind.count, initial, 0)

    def correct(i, carry):
        j = kind.block(i)
        nu = vis[j]
        sums = stencil(
            carried, *kind.place(i), coupling, transposed, lambda d: kappa[j * 4 + d]
        )
        y0 = [first[i * 4 + c] for c in range(4)]
        own = block_times(diag, j * 16, y0, transposed)
        rest = [res[i * 4 + c] - own[c] + nu * sums[c] for c in range(4)]
        for c, y in enumerate(block_times(inv, j * 16, rest, transposed)):
            update[i * 4 + c] = y0[c] + y
        return carry

    lax.fori_loop(0, kind.count, correct, 0)

    def carry_on(i, carry):
        nu = vis[kind.block(i)]
        at = kind.place(i)[0]
        for c in range(4):
            carried[at + c] = nu * update[i * 4 + c]
        return carry

    lax.fori_loop(0, kind.count, carry_on, 0)

    def apply(i, carry):
        if own_only:
            i = i * 2 if kind is Adjoint else 1
        j = kind.block(i)
        sums = stencil(carried, *kind.place(i), coupling, transposed, None)
        values = [update[i * 4 + c] for c in range(4)]
        own = block_times(diag, j * 16, values, transposed)
        nu = vis[j]
        for c in range(4):
            image[i * 4 + c] = own[c] - nu * sums[c]
        return carry

    lax.fori_loop(0, kind.own if own_only else kind.count, apply, 0)


def dots_of(residual, image, last, at_of, pairs):
    def own(ref, v):
        return [ref[at_of(v) + c] for c in range(4)]

    def dot(x, i, y, j):
        part = None
        for a, b in zip(own(x, i), own(y, j)):
            part = a * b if part is None else part + a * b
        return part

    out = []
    for x, y in ((image, image), (residual, image), (residual, last), (image, last), (last, last)):
        for i, j in pairs:
            part = dot(x, i, y, j)
            if i != j:
                part += part if x is y else dot(x, j, y, i)
            tile = (part[0] + part[1]) + (part[2] + part[3])
            line = jnp.sum(tile, axis=0, keepdims=True)
            out.append(jnp.sum(line, axis=1, keepdims=True))
    return out


def merged(after, before):
    return jnp.where(iota((4, 8, 128), 2) % CHUNK < CHUNK // 2, after, before)


def layer_sums(update, spread, target, vector):
    for i, j in enumerate((OWN, NEAR)):
        weight = spread[j]
        active = jnp.where(weight < 0.0, 1.0, 0.0)
        at = (vector * 2 + i) * 4
        for c in range(2):
            tile = update[4 + c] if j == OWN else merged(update[8 + c], update[c])
            target[at + c] = weight * jnp.sum(active * tile, axis=1, keepdims=True)
        for c in range(2, 4):
            target[at + c] = jnp.zeros((4, 8, 128), F32)


def unpack(block, j, inv, diag, vis, small):
    sub = iota((8, 128), 0)

    def place(half, carry):
        part = pl.ds(half * SLOTS, SLOTS)
        for r in range(ROWS):
            i = half * 2 + r
            tiles = turned(block[part, r])
            inv[j * 16 : j * 16 + 16, i] = jnp.where(sub[None] < LAYERS, tiles, 0.0)
            for target, base, lines in ((vis, 0, LAYERS), (small, LAYERS, 5)):
                total = jnp.zeros((8, 128), F32)
                for k in range(lines):
                    moved = pltpu.roll(tiles[base + k], (k - SPARE) % 8, 0)
                    total = jnp.where(sub == k, moved, total)
                target[j, i] = total
            diag[j * 16 : j * 16 + 16, i] = turned(block[part, 2 + r])
        return carry

    lax.fori_loop(0, 2, place, 0)


def solve_kernel(
    coupling, low, mine, high, message,
    inv, diag, vis, small, kappa, spread, res, res_two, first, carried, update, image, last, start,
):
    gx, gy = lax.axis_index("gx"), lax.axis_index("gy")
    nx, ny = lax.axis_size("gx"), lax.axis_size("gy")
    for j, block in enumerate((low, mine, high)):
        unpack(block, j, inv, diag, vis, small)
    for c in range(4):
        carried[c] = jnp.zeros((4, 8, 128), F32)
        carried[16 + c] = jnp.zeros((4, 8, 128), F32)

    shape = (4, 8, 128)
    layer = iota(shape, 1)
    lane = iota(shape, 2)
    source = (iota(shape, 0) // 2) * SLOTS + lane // CHUNK
    low_row = iota(shape, 0) % 2 == 0
    for j in range(3):
        tiles = small[j]
        counts = tiles[:, COUNT_ROW : COUNT_ROW + 1, :]
        whole = jnp.maximum(counts, 1.0)
        active = jnp.where(layer.astype(F32) < counts, 1.0, 0.0)
        spread[j] = -active / (whole * whole)
        for c in range(2):
            rhs = tiles[:, RHS_ROW + c : RHS_ROW + c + 1, :]
            res[j * 4 + c] = jnp.where(layer == 0, rhs, 0.0)
        for c in range(2, 4):
            res[j * 4 + c] = jnp.zeros(shape, F32)
        column = (gy * COLS + gx * CHUNK + (j - OWN) * CHUNK) + lane % CHUNK
        within = column & (COLS - 1)
        south_on = jnp.where((within == 0) & (column > 0), 1.0, 0.0)
        north_on = jnp.where((within == COLS - 1) & (column < ny * COLS - 1), 1.0, 0.0)
        south_in = jnp.where(within == 0, 0.0, 1.0)
        north_in = jnp.where(within == COLS - 1, 0.0, 1.0)
        side_exists = (low_row & (source > 0)) | (jnp.logical_not(low_row) & (source < nx - 1))
        side = jnp.where(side_exists, 1.0, 0.0)
        shared = south_on + north_on + side
        level = (1.0 + tiles[:, PATTERN_ROW : PATTERN_ROW + 1, :]) / 5.0
        own_weight = jnp.where(shared > 0.0, level, 1.0)
        near = (1.0 - own_weight) / jnp.maximum(shared, 1.0)
        inward = own_weight + near * (south_on + north_on)
        outward = own_weight + near * side
        kappa[j * 4] = jnp.where(low_row, inward, outward)
        kappa[j * 4 + 1] = jnp.where(low_row, outward, inward)
        kappa[j * 4 + 2] = own_weight + near * (north_on + side * north_in)
        kappa[j * 4 + 3] = own_weight + near * (south_on + side * south_in)

    for table, size in ((inv, 16), (diag, 16), (kappa, 4), (vis, 1), (spread, 1)):
        for k in range(size):
            table[NEAR * size + k] = merged(table[2 * size + k], table[k])

    tables = (inv, diag, vis, kappa, coupling)
    sweep(Forward, res, first, carried, update, image, False, tables)
    layer_sums(update, spread, res_two, 0)
    for t in range(12):
        res[t] = res[t] - image[t]
    sweep(Forward, res, first, carried, update, last, True, tables)
    layer_sums(update, spread, res_two, 1)
    dots = dots_of(res, image, last, lambda v: 4, ((0, 0),))

    sweep(Adjoint, res_two, first, carried, update, image, False, tables)
    for v in range(2):
        for c in range(4):
            start[v * 4 + c] = update[v * 8 + c]
    for t in range(16):
        res_two[t] = res_two[t] - image[t]
    sweep(Adjoint, res_two, first, carried, update, last, True, tables)
    dots += dots_of(res_two, image, last, lambda v: v * 8, ((0, 0), (0, 1), (1, 1)))

    before, here, after = small[0], small[1], small[2]
    around = x_plus(here) + x_minus(here) + y_plus(here, after) + y_minus(here, before)
    first[0] = 4.0 * here - around
    sub = iota((8, 128), 0)
    column = iota((1, 128), 1) % CHUNK
    lines = []
    for k in range(0, len(dots), CHUNK):
        line = jnp.zeros((1, 128), F32)
        for m, dot in enumerate(dots[k : k + CHUNK]):
            line = jnp.where(column == m, dot, line)
        lines.append(line)

    def send(half, carry):
        for r in range(ROWS):
            i = half * 2 + r
            tiles = [start[k, i] for k in range(8)]
            tiles += [update[v * 8 + c, i] for v in range(2) for c in range(4)]
            prior = pltpu.roll(first[0, i], SPARE - BETA_ROW, 0)
            tiles[0] = jnp.where(sub == SPARE, prior, tiles[0])
            for k, line in enumerate(lines):
                tiles[k] = jnp.where(sub == 7, line, tiles[k])
            message[pl.ds(half * SLOTS, SLOTS), r] = turned(jnp.stack(tiles))
        return carry

    lax.fori_loop(0, 2, send, 0)


def steps(image2, residual_image, residual_last, image_last, last2):
    one = (residual_image + image2) / (image2 + EPSILON)
    off = 1.0 - one
    along = off * residual_image + one * residual_last + off * off * image2 + off * one * image_last
    squared = off * off * image2 + 2.0 * off * one * image_last + one * one * last2
    two = along / (squared + EPSILON)
    return one + two * off, one * two


def gather_kernel(block, lines):
    total = None
    for k in range(block.shape[0]):
        total = block[k, 0] if total is None else total + block[k, 0]
    lane, sub = iota((8, 128), 1), iota((8, 128), 0)
    out = jnp.zeros((8, 128), F32)
    for i in range(8):
        keep = (sub == i) & (lane % CHUNK == 7)
        out += pltpu.roll(jnp.where(keep, total, 0.0), (i - 7) % 128, 1)
    lines[...] = jnp.broadcast_to(jnp.sum(out, axis=0, keepdims=True), lines.shape)


def final_kernel(dots, block, grounded, vel, hessian, adjoint):
    line = jnp.sum(dots[...], axis=0, keepdims=True)
    lane = iota((1, 128), 1)

    def get(k):
        return jnp.sum(jnp.where(lane == k, line, 0.0), axis=1, keepdims=True)

    a, b = steps(*[get(k) for k in range(5)])
    kinds = []
    for k in range(5):
        at = 5 + 3 * k
        kinds.append(a * a * get(at) + a * b * get(at + 1) + b * b * get(at + 2))
    p, q = steps(*kinds)
    weights = (p * a, p * b, q * a, q * b)
    for r in range(ROWS):
        for part in range(2):
            tiles = turned(block[part * SLOTS : part * SLOTS + SLOTS, r])
            at = slice(part * 128, part * 128 + 128)
            heads = []
            for c in range(4):
                total = weights[0] * tiles[c]
                for v in range(1, 4):
                    total += weights[v] * tiles[v * 4 + c]
                adjoint[c, :, r, at] = total[0:LAYERS]
                heads.append(total[0:1])
            row = slice(r, r + 1)
            data = grounded[row, at].astype(F32) * (
                vel[0, row, at] * heads[0] + vel[1, row, at] * heads[1]
            )
            hessian[row, at] = data + PRIOR_WEIGHT * tiles[0, SPARE : SPARE + 1]


VMEM = pl.BlockSpec(memory_space=pltpu.VMEM)
SMEM = pl.BlockSpec(memory_space=pltpu.SMEM)
HBM = pl.BlockSpec(memory_space=pltpu.HBM)


def call(kernel, name, operands, in_specs, outs, scratch=()):
    return pl.pallas_call(
        kernel,
        out_shape=[jax.ShapeDtypeStruct(shape, F32) for shape in outs],
        in_specs=in_specs,
        out_specs=[VMEM] * len(outs),
        scratch_shapes=scratch,
        compiler_params=pltpu.CompilerParams(vmem_limit_bytes=(63 if name == "pack_tables" else 40) * 1024 * 1024),
        name=name,
    )(*operands)


def neighbour_pairs(step):
    n_gx, n_gy = lax.axis_size("gx"), lax.axis_size("gy")
    pairs = []
    for source in range(n_gx * n_gy):
        target = source + step
        if 0 <= target < n_gx * n_gy:
            pairs.append(
                tuple((i % n_gx) * n_gy + i // n_gx for i in (source, target))
            )
    return pairs


def per_device(
    diag_block,
    block_inverse,
    viscosity,
    coupling,
    active_layers,
    grounded,
    weight_pattern,
    beta_step,
    base_vel,
):
    n_gx, n_gy = lax.axis_size("gx"), lax.axis_size("gy")
    table = (16,) + viscosity.shape
    raw = [
        diag_block.reshape(table),
        block_inverse.reshape(table),
        viscosity,
        active_layers,
        grounded,
        weight_pattern,
        beta_step,
        base_vel,
    ]
    (sent,) = call(
        pack_kernel,
        "pack_tables",
        raw,
        [HBM] * 8,
        [(n_gx, 4, 8, 128)],
        [pltpu.VMEM(x.shape, x.dtype) for x in raw]
        + [pltpu.VMEM((8, 16, 8, 128), F32), pltpu.SemaphoreType.DMA((8,))],
    )
    mine = lax.all_to_all(sent, "gx", 0, 0, tiled=True)
    low = lax.ppermute(mine, ("gx", "gy"), neighbour_pairs(1))
    high = lax.ppermute(mine, ("gx", "gy"), neighbour_pairs(-1))

    def field(count):
        return pltpu.VMEM((count, 4, 8, 128), F32)

    (back,) = call(
        solve_kernel,
        "solve_both",
        [coupling.reshape(96), low, mine, high],
        [SMEM, VMEM, VMEM, VMEM],
        [(n_gx, 2, 8, 128)],
        [
            field(64),
            field(64),
            field(4),
            field(3),
            field(16),
            field(4),
            field(12),
            field(16),
            field(16),
            field(20),
            field(16),
            field(16),
            field(16),
            field(8),
        ],
    )
    block = lax.all_to_all(back, "gx", 0, 0, tiled=True)
    (lines,) = call(gather_kernel, "sum_gx", [block], [VMEM], [(n_gy, 128)])
    lines = lax.all_to_all(lines, "gy", 0, 0, tiled=True)
    hessian_vec, adjoint = call(
        final_kernel,
        "combine",
        [lines, block, grounded, base_vel],
        [VMEM] * 4,
        [beta_step.shape, (4,) + viscosity.shape],
    )
    return hessian_vec, adjoint


def solution(mesh):
    placed = (
        P(None, None, None, "gx", "gy"),
        P(None, None, None, "gx", "gy"),
        P(None, "gx", "gy"),
        P(),
        P("gx", "gy"),
        P("gx", "gy"),
        P("gx", "gy"),
        P("gx", "gy"),
        P(None, "gx", "gy"),
    )
    return jax.shard_map(
        per_device,
        mesh=mesh,
        in_specs=placed,
        out_specs=(P("gx", "gy"), P(None, None, "gx", "gy")),
        check_vma=False,
    )
```

```python
import jax
import jax.numpy as jnp
from jax import lax
from jax.experimental import pallas as pl
from jax.experimental.pallas import tpu as pltpu
from jax.sharding import PartitionSpec as P

PRIOR_WEIGHT = 0.05
EPSILON = 1e-06
OPPOSITE = (1, 0, 3, 2, 5, 4)
F32 = jnp.float32
LAYERS = 6
ROWS = 2
COLS = 256
CHUNK = 8
SLOTS = 16
OWN, NEAR = 1, 3
COUNT_ROW, PATTERN_ROW, RHS_ROW, BETA_ROW = 0, 1, 2, 4
SPARE = 6


def iota(shape, dim):
    return lax.broadcasted_iota(jnp.int32, shape, dim)


def chunk_order(turn, n_x, n_y):
    order = []
    if turn % 2 == 0:
        for i in range(n_y):
            for j in range(n_x):
                x, y = (j if i % 2 == 0 else n_x - 1 - j), i
                if turn == 2:
                    x, y = n_x - 1 - x, n_y - 1 - y
                order.append(y * n_x + x)
    else:
        for i in range(n_x):
            for j in range(n_y):
                x, y = i, (n_y - 1 - j if i % 2 == 0 else j)
                if turn == 3:
                    x, y = n_x - 1 - x, n_y - 1 - y
                order.append(y * n_x + x)
    return order


GRID_X, GRID_Y = 4, 8
ORDERS = [chunk_order(turn, GRID_X, GRID_Y) for turn in range(4)]


def pick(turn, choices):
    low = jnp.where(turn == 0, choices[0], choices[1])
    return jnp.where(turn < 2, low, jnp.where(turn == 2, choices[2], choices[3]))


def device_of(turn, chunk):
    return pick(turn, [order[chunk] for order in ORDERS])


def chunk_of(turn, gx):
    x, y = gx % GRID_X, gx // GRID_X
    back_x, back_y = GRID_X - 1 - x, GRID_Y - 1 - y
    along_x = jnp.where(turn == 0, y, back_y)
    step_x = jnp.where((along_x % 2 == 0) == (turn == 0), x, back_x)
    along_y = jnp.where(turn == 1, x, back_x)
    step_y = jnp.where((along_y % 2 == 0) == (turn == 1), back_y, y)
    return jnp.where(turn % 2 == 0, along_x * GRID_X + step_x, along_y * GRID_Y + step_y)


def turned(tiles):
    return tiles.reshape(128, 128).T.reshape(SLOTS, 8, 128)


def pack_kernel(
    diag_in, inv_in, visc_in, count_in, grounded_in, pattern_in, beta_in, vel_in, message,
    diag, inv, visc, count, grounded, pattern, beta, vel, folded, arrived,
):
    pairs = (
        (count_in, count), (diag_in, diag), (inv_in, inv), (visc_in, visc), (grounded_in, grounded),
        (pattern_in, pattern), (beta_in, beta), (vel_in, vel),
    )
    copies = [
        pltpu.make_async_copy(source, target, arrived.at[i])
        for i, (source, target) in enumerate(pairs)
    ]
    for copy in copies:
        copy.start()
    folded[...] = jnp.zeros(folded.shape, F32)
    for copy in copies:
        copy.wait()
    layer = iota((LAYERS, COLS), 0)
    actives = [layer < count[r : r + 1, :] for r in range(ROWS)]

    def fold(cp, carry):
        eye = jnp.where(cp % 5 == 0, 1.0, 0.0).astype(F32)
        for t, table in enumerate((inv, diag)):
            for r in range(ROWS):
                values = jnp.where(actives[r], table[cp, :, r, :], eye)
                for part in range(2):
                    folded[(t * 2 + r) * 2 + part, cp, 0:LAYERS, :] = values[
                        :, part * 128 : part * 128 + 128
                    ]
        return carry

    lax.fori_loop(0, 16, fold, 0)
    for r in range(ROWS):
        row = slice(r, r + 1)
        viscous = jnp.where(actives[r], visc[:, r, :], 0.0)
        force = -(grounded[row, :].astype(F32) * beta[row, :])
        lines = [viscous[k : k + 1] for k in range(LAYERS)]
        lines += [count[row, :].astype(F32), pattern[row, :].astype(F32)]
        lines += [force * vel[0, row, :], force * vel[1, row, :], beta[row, :]]
        for slot, line in enumerate(lines):
            for part in range(2):
                folded[r * 2 + part, slot, SPARE : SPARE + 1, :] = line[
                    :, part * 128 : part * 128 + 128
                ]

    turn = lax.axis_index("gy") % 4
    for part in range(2):
        targets = [device_of(turn, part * SLOTS + k) for k in range(SLOTS)]
        for i in range(4):
            tiles = turned(folded[i * 2 + part])
            for k in range(SLOTS):
                message[targets[k], i] = tiles[k]


def block_times(table, base, values, transposed):
    out = []
    for c in range(4):
        total = None
        for k in range(4):
            entry = table[base + (k * 4 + c if transposed else c * 4 + k)] * values[k]
            total = entry if total is None else total + entry
        out.append(total)
    return out


def coupled(coupling, direction, values, transposed, sums):
    for c in range(4):
        for k in range(4):
            if transposed:
                factor = coupling[OPPOSITE[direction] * 16 + k * 4 + c]
            else:
                factor = coupling[direction * 16 + c * 4 + k]
            entry = factor * values[k]
            sums[c] = entry if sums[c] is None else sums[c] + entry
    return sums


def x_plus(v):
    first = iota((8, 128), 1) < CHUNK
    inner = pltpu.roll(jnp.where(first, v[2], v[0]), 128 - CHUNK, 1)
    outer = pltpu.roll(jnp.where(first, 0.0, v[2]), 128 - CHUNK, 1)
    return jnp.stack([v[1], inner, v[3], outer])


def x_minus(v):
    last = iota((8, 128), 1) >= 128 - CHUNK
    outer = pltpu.roll(jnp.where(last, 0.0, v[1]), CHUNK, 1)
    inner = pltpu.roll(jnp.where(last, v[1], v[3]), CHUNK, 1)
    return jnp.stack([outer, v[0], inner, v[2]])


def y_plus(v, after):
    column = iota((4, 8, 128), 2) % CHUNK
    return jnp.where(
        column < CHUNK - 1, pltpu.roll(v, 127, 2), pltpu.roll(after, CHUNK - 1, 2)
    )


def y_minus(v, before):
    column = iota((4, 8, 128), 2) % CHUNK
    return jnp.where(column > 0, pltpu.roll(v, 1, 2), pltpu.roll(before, 128 - CHUNK + 1, 2))


def stencil(field, base, after, before, coupling, transposed, kappa):
    here = [field[base + c] for c in range(4)]
    sums = [None] * 4
    sums = coupled(coupling, 0, [pltpu.roll(h, 7, 1) for h in here], transposed, sums)
    sums = coupled(coupling, 1, [pltpu.roll(h, 1, 1) for h in here], transposed, sums)

    def weighted(direction, tiles):
        if kappa is None:
            return tiles
        weight = kappa(direction)
        return [weight * t for t in tiles]

    moved = weighted(0, [x_plus(h) for h in here])
    sums = coupled(coupling, 2, moved, transposed, sums)
    moved = weighted(1, [x_minus(h) for h in here])
    sums = coupled(coupling, 3, moved, transposed, sums)
    moved = weighted(2, [y_plus(here[c], field[after + c]) for c in range(4)])
    sums = coupled(coupling, 4, moved, transposed, sums)
    moved = weighted(3, [y_minus(here[c], field[before + c]) for c in range(4)])
    return coupled(coupling, 5, moved, transposed, sums)


class Forward:
    count, transposed, own = 3, False, 1

    def block(i):
        return i

    def place(i):
        return (i + 1) * 4, (i + 2) * 4, i * 4


class Adjoint:
    count, transposed, own = 4, True, 2

    def block(i):
        return (i % 2) * 2 + 1

    def place(i):
        other = (i + 1 - 2 * (i % 2)) * 4
        return i * 4, other, other


def sweep(kind, res, first, carried, update, image, own_only, tables):
    inv, diag, vis, kappa, coupling = tables
    transposed = kind.transposed

    def initial(i, carry):
        j = kind.block(i)
        at = kind.place(i)[0]
        nu = vis[j]
        values = [res[i * 4 + c] for c in range(4)]
        for c, y in enumerate(block_times(inv, j * 16, values, transposed)):
            first[i * 4 + c] = y
            carried[at + c] = nu * y
        return carry

    lax.fori_loop(0, kind.count, initial, 0)

    def correct(i, carry):
        j = kind.block(i)
        nu = vis[j]
        sums = stencil(
            carried, *kind.place(i), coupling, transposed, lambda d: kappa[j * 4 + d]
        )
        y0 = [first[i * 4 + c] for c in range(4)]
        own = block_times(diag, j * 16, y0, transposed)
        rest = [res[i * 4 + c] - own[c] + nu * sums[c] for c in range(4)]
        for c, y in enumerate(block_times(inv, j * 16, rest, transposed)):
            update[i * 4 + c] = y0[c] + y
        return carry

    lax.fori_loop(0, kind.count, correct, 0)

    def carry_on(i, carry):
        nu = vis[kind.block(i)]
        at = kind.place(i)[0]
        for c in range(4):
            carried[at + c] = nu * update[i * 4 + c]
        return carry

    lax.fori_loop(0, kind.count, carry_on, 0)

    def apply(i, carry):
        if own_only:
            i = i * 2 if kind is Adjoint else 1
        j = kind.block(i)
        sums = stencil(carried, *kind.place(i), coupling, transposed, None)
        values = [update[i * 4 + c] for c in range(4)]
        own = block_times(diag, j * 16, values, transposed)
        nu = vis[j]
        for c in range(4):
            image[i * 4 + c] = own[c] - nu * sums[c]
        return carry

    lax.fori_loop(0, kind.own if own_only else kind.count, apply, 0)


def dots_of(residual, image, last, at_of, pairs):
    def own(ref, v):
        return [ref[at_of(v) + c] for c in range(4)]

    def dot(x, i, y, j):
        part = None
        for a, b in zip(own(x, i), own(y, j)):
            part = a * b if part is None else part + a * b
        return part

    out = []
    for x, y in ((image, image), (residual, image), (residual, last), (image, last), (last, last)):
        for i, j in pairs:
            part = dot(x, i, y, j)
            if i != j:
                part += part if x is y else dot(x, j, y, i)
            tile = (part[0] + part[1]) + (part[2] + part[3])
            line = jnp.sum(tile, axis=0, keepdims=True)
            out.append(jnp.sum(line, axis=1, keepdims=True))
    return out


def merged(after, before):
    return jnp.where(iota((4, 8, 128), 2) % CHUNK < CHUNK // 2, after, before)


def layer_sums(update, spread, target, vector):
    for i, j in enumerate((OWN, NEAR)):
        weight = spread[j]
        active = jnp.where(weight < 0.0, 1.0, 0.0)
        at = (vector * 2 + i) * 4
        for c in range(2):
            tile = update[4 + c] if j == OWN else merged(update[8 + c], update[c])
            target[at + c] = weight * jnp.sum(active * tile, axis=1, keepdims=True)
        for c in range(2, 4):
            target[at + c] = jnp.zeros((4, 8, 128), F32)


def unpack(block, j, inv, diag, vis, small):
    sub = iota((8, 128), 0)

    def place(half, carry):
        part = pl.ds(half * SLOTS, SLOTS)
        for r in range(ROWS):
            i = half * 2 + r
            tiles = turned(block[part, r])
            inv[j * 16 : j * 16 + 16, i] = jnp.where(sub[None] < LAYERS, tiles, 0.0)
            for target, base, lines in ((vis, 0, LAYERS), (small, LAYERS, 5)):
                total = jnp.zeros((8, 128), F32)
                for k in range(lines):
                    moved = pltpu.roll(tiles[base + k], (k - SPARE) % 8, 0)
                    total = jnp.where(sub == k, moved, total)
                target[j, i] = total
            diag[j * 16 : j * 16 + 16, i] = turned(block[part, 2 + r])
        return carry

    lax.fori_loop(0, 2, place, 0)


def solve_kernel(
    coupling, low, mine, high, message,
    inv, diag, vis, small, kappa, spread, res, res_two, first, carried, update, image, last, start,
):
    gx, gy = lax.axis_index("gx"), lax.axis_index("gy")
    nx, ny = lax.axis_size("gx"), lax.axis_size("gy")
    chunk = chunk_of(gy % 4, gx)
    for j, block in enumerate((low, mine, high)):
        unpack(block, j, inv, diag, vis, small)
    for c in range(4):
        carried[c] = jnp.zeros((4, 8, 128), F32)
        carried[16 + c] = jnp.zeros((4, 8, 128), F32)

    shape = (4, 8, 128)
    layer = iota(shape, 1)
    lane = iota(shape, 2)
    source = (iota(shape, 0) // 2) * SLOTS + lane // CHUNK
    low_row = iota(shape, 0) % 2 == 0
    for j in range(3):
        tiles = small[j]
        counts = tiles[:, COUNT_ROW : COUNT_ROW + 1, :]
        whole = jnp.maximum(counts, 1.0)
        active = jnp.where(layer.astype(F32) < counts, 1.0, 0.0)
        spread[j] = -active / (whole * whole)
        for c in range(2):
            rhs = tiles[:, RHS_ROW + c : RHS_ROW + c + 1, :]
            res[j * 4 + c] = jnp.where(layer == 0, rhs, 0.0)
        for c in range(2, 4):
            res[j * 4 + c] = jnp.zeros(shape, F32)
        column = (gy * COLS + (chunk + j - OWN) * CHUNK) + lane % CHUNK
        within = column & (COLS - 1)
        south_on = jnp.where((within == 0) & (column > 0), 1.0, 0.0)
        north_on = jnp.where((within == COLS - 1) & (column < ny * COLS - 1), 1.0, 0.0)
        south_in = jnp.where(within == 0, 0.0, 1.0)
        north_in = jnp.where(within == COLS - 1, 0.0, 1.0)
        side_exists = (low_row & (source > 0)) | (jnp.logical_not(low_row) & (source < nx - 1))
        side = jnp.where(side_exists, 1.0, 0.0)
        shared = south_on + north_on + side
        level = (1.0 + tiles[:, PATTERN_ROW : PATTERN_ROW + 1, :]) / 5.0
        own_weight = jnp.where(shared > 0.0, level, 1.0)
        near = (1.0 - own_weight) / jnp.maximum(shared, 1.0)
        inward = own_weight + near * (south_on + north_on)
        outward = own_weight + near * side
        kappa[j * 4] = jnp.where(low_row, inward, outward)
        kappa[j * 4 + 1] = jnp.where(low_row, outward, inward)
        kappa[j * 4 + 2] = own_weight + near * (north_on + side * north_in)
        kappa[j * 4 + 3] = own_weight + near * (south_on + side * south_in)

    for table, size in ((inv, 16), (diag, 16), (kappa, 4), (vis, 1), (spread, 1)):
        for k in range(size):
            table[NEAR * size + k] = merged(table[2 * size + k], table[k])

    tables = (inv, diag, vis, kappa, coupling)
    sweep(Forward, res, first, carried, update, image, False, tables)
    layer_sums(update, spread, res_two, 0)
    for t in range(12):
        res[t] = res[t] - image[t]
    sweep(Forward, res, first, carried, update, last, True, tables)
    layer_sums(update, spread, res_two, 1)
    dots = dots_of(res, image, last, lambda v: 4, ((0, 0),))

    sweep(Adjoint, res_two, first, carried, update, image, False, tables)
    for v in range(2):
        for c in range(4):
            start[v * 4 + c] = update[v * 8 + c]
    for t in range(16):
        res_two[t] = res_two[t] - image[t]
    sweep(Adjoint, res_two, first, carried, update, last, True, tables)
    dots += dots_of(res_two, image, last, lambda v: v * 8, ((0, 0), (0, 1), (1, 1)))

    before, here, after = small[0], small[1], small[2]
    around = x_plus(here) + x_minus(here) + y_plus(here, after) + y_minus(here, before)
    first[0] = 4.0 * here - around
    sub = iota((8, 128), 0)
    column = iota((1, 128), 1) % CHUNK
    lines = []
    for k in range(0, len(dots), CHUNK):
        line = jnp.zeros((1, 128), F32)
        for m, dot in enumerate(dots[k : k + CHUNK]):
            line = jnp.where(column == m, dot, line)
        lines.append(line)

    def send(half, carry):
        for r in range(ROWS):
            i = half * 2 + r
            tiles = [start[k, i] for k in range(8)]
            tiles += [update[v * 8 + c, i] for v in range(2) for c in range(4)]
            prior = pltpu.roll(first[0, i], SPARE - BETA_ROW, 0)
            tiles[0] = jnp.where(sub == SPARE, prior, tiles[0])
            for k, line in enumerate(lines):
                tiles[k] = jnp.where(sub == 7, line, tiles[k])
            message[pl.ds(half * SLOTS, SLOTS), r] = turned(jnp.stack(tiles))
        return carry

    lax.fori_loop(0, 2, send, 0)


def steps(image2, residual_image, residual_last, image_last, last2):
    one = (residual_image + image2) / (image2 + EPSILON)
    off = 1.0 - one
    along = off * residual_image + one * residual_last + off * off * image2 + off * one * image_last
    squared = off * off * image2 + 2.0 * off * one * image_last + one * one * last2
    two = along / (squared + EPSILON)
    return one + two * off, one * two


def gather_kernel(block, lines):
    total = None
    for k in range(block.shape[0]):
        total = block[k, 0] if total is None else total + block[k, 0]
    lane, sub = iota((8, 128), 1), iota((8, 128), 0)
    out = jnp.zeros((8, 128), F32)
    for i in range(8):
        keep = (sub == i) & (lane % CHUNK == 7)
        out += pltpu.roll(jnp.where(keep, total, 0.0), (i - 7) % 128, 1)
    lines[...] = jnp.broadcast_to(jnp.sum(out, axis=0, keepdims=True), lines.shape)


def final_kernel(dots, block, grounded, vel, hessian, adjoint):
    line = jnp.sum(dots[...], axis=0, keepdims=True)
    lane = iota((1, 128), 1)

    def get(k):
        return jnp.sum(jnp.where(lane == k, line, 0.0), axis=1, keepdims=True)

    a, b = steps(*[get(k) for k in range(5)])
    kinds = []
    for k in range(5):
        at = 5 + 3 * k
        kinds.append(a * a * get(at) + a * b * get(at + 1) + b * b * get(at + 2))
    p, q = steps(*kinds)
    weights = (p * a, p * b, q * a, q * b)
    turn = lax.axis_index("gy") % 4
    for part in range(2):
        sources = [device_of(turn, part * SLOTS + k) for k in range(SLOTS)]
        for r in range(ROWS):
            tiles = turned(jnp.stack([block[source, r] for source in sources]))
            at = slice(part * 128, part * 128 + 128)
            heads = []
            for c in range(4):
                total = weights[0] * tiles[c]
                for v in range(1, 4):
                    total += weights[v] * tiles[v * 4 + c]
                adjoint[c, :, r, at] = total[0:LAYERS]
                heads.append(total[0:1])
            row = slice(r, r + 1)
            data = grounded[row, at].astype(F32) * (
                vel[0, row, at] * heads[0] + vel[1, row, at] * heads[1]
            )
            hessian[row, at] = data + PRIOR_WEIGHT * tiles[0, SPARE : SPARE + 1]


VMEM = pl.BlockSpec(memory_space=pltpu.VMEM)
SMEM = pl.BlockSpec(memory_space=pltpu.SMEM)
HBM = pl.BlockSpec(memory_space=pltpu.HBM)


def call(kernel, name, operands, in_specs, outs, scratch=()):
    return pl.pallas_call(
        kernel,
        out_shape=[jax.ShapeDtypeStruct(shape, F32) for shape in outs],
        in_specs=in_specs,
        out_specs=[VMEM] * len(outs),
        scratch_shapes=scratch,
        compiler_params=pltpu.CompilerParams(vmem_limit_bytes=(63 if name == "pack_tables" else 40) * 1024 * 1024),
        name=name,
    )(*operands)


def neighbour_pairs(step):
    n_gy = lax.axis_size("gy")
    places = [gx * n_gy + gy for gy in range(n_gy) for gx in ORDERS[gy % 4]]
    count = len(places)
    return [(places[i], places[i + step]) for i in range(count) if 0 <= i + step < count]


def per_device(
    diag_block,
    block_inverse,
    viscosity,
    coupling,
    active_layers,
    grounded,
    weight_pattern,
    beta_step,
    base_vel,
):
    n_gx, n_gy = lax.axis_size("gx"), lax.axis_size("gy")
    table = (16,) + viscosity.shape
    raw = [
        diag_block.reshape(table),
        block_inverse.reshape(table),
        viscosity,
        active_layers,
        grounded,
        weight_pattern,
        beta_step,
        base_vel,
    ]
    (sent,) = call(
        pack_kernel,
        "pack_tables",
        raw,
        [HBM] * 8,
        [(n_gx, 4, 8, 128)],
        [pltpu.VMEM(x.shape, x.dtype) for x in raw]
        + [pltpu.VMEM((8, 16, 8, 128), F32), pltpu.SemaphoreType.DMA((8,))],
    )
    mine = lax.all_to_all(sent, "gx", 0, 0, tiled=True)
    low = lax.ppermute(mine, ("gx", "gy"), neighbour_pairs(1))
    high = lax.ppermute(mine, ("gx", "gy"), neighbour_pairs(-1))

    def field(count):
        return pltpu.VMEM((count, 4, 8, 128), F32)

    (back,) = call(
        solve_kernel,
        "solve_both",
        [coupling.reshape(96), low, mine, high],
        [SMEM, VMEM, VMEM, VMEM],
        [(n_gx, 2, 8, 128)],
        [
            field(64),
            field(64),
            field(4),
            field(3),
            field(16),
            field(4),
            field(12),
            field(16),
            field(16),
            field(20),
            field(16),
            field(16),
            field(16),
            field(8),
        ],
    )
    block = lax.all_to_all(back, "gx", 0, 0, tiled=True)
    (lines,) = call(gather_kernel, "sum_gx", [block], [VMEM], [(n_gy, 128)])
    lines = lax.all_to_all(lines, "gy", 0, 0, tiled=True)
    hessian_vec, adjoint = call(
        final_kernel,
        "combine",
        [lines, block, grounded, base_vel],
        [VMEM] * 4,
        [beta_step.shape, (4,) + viscosity.shape],
    )
    return hessian_vec, adjoint


def solution(mesh):
    placed = (
        P(None, None, None, "gx", "gy"),
        P(None, None, None, "gx", "gy"),
        P(None, "gx", "gy"),
        P(),
        P("gx", "gy"),
        P("gx", "gy"),
        P("gx", "gy"),
        P("gx", "gy"),
        P(None, "gx", "gy"),
    )
    return jax.shard_map(
        per_device,
        mesh=mesh,
        in_specs=placed,
        out_specs=(P("gx", "gy"), P(None, None, "gx", "gy")),
        check_vma=False,
    )
```

```python
import jax
import jax.numpy as jnp
from jax import lax
from jax.experimental import pallas as pl
from jax.experimental.pallas import tpu as pltpu
from jax.sharding import PartitionSpec as P

PRIOR_WEIGHT = 0.05
EPSILON = 1e-06
OPPOSITE = (1, 0, 3, 2, 5, 4)
F32 = jnp.float32
LAYERS = 6
ROWS = 2
COLS = 256
CHUNK = 8
SLOTS = 16
OWN, NEAR = 1, 3
CHUNK_ROWS = 26
COUNT_ROW, PATTERN_ROW, RHS_ROW, BETA_ROW = 0, 1, 2, 4
SPARE = 6


def table_row(table, r, entry):
    return ((table * ROWS + r) * 16 + entry) * LAYERS


def iota(shape, dim):
    return lax.broadcasted_iota(jnp.int32, shape, dim)


ORDERS = (
    (1, 29, 25, 21, 20, 23, 22, 18, 17, 16, 19, 15, 14, 13, 12, 8)
    + (9, 10, 11, 7, 6, 5, 4, 0, 3, 31, 28, 24, 27, 26, 30, 2),
    (2, 3, 7, 4, 8, 11, 15, 12, 16, 20, 24, 25, 26, 22, 21, 17)
    + (13, 9, 5, 1, 0, 28, 29, 30, 31, 27, 23, 19, 18, 14, 10, 6),
    (6, 7, 11, 10, 9, 8, 12, 13, 14, 15, 19, 16, 17, 18, 22, 23)
    + (20, 21, 25, 29, 1, 2, 30, 26, 27, 24, 28, 31, 3, 0, 4, 5),
    (5, 9, 13, 17, 21, 22, 26, 25, 24, 20, 16, 12, 15, 11, 8, 4)
    + (7, 3, 2, 6, 10, 14, 18, 19, 23, 27, 31, 30, 29, 28, 0, 1),
)


def pick(turn, choices):
    low = jnp.where(turn == 0, choices[0], choices[1])
    return jnp.where(turn < 2, low, jnp.where(turn == 2, choices[2], choices[3]))


def device_of(turn, chunk):
    return pick(turn, [order[chunk] for order in ORDERS])


def chunk_of(turn, gx):
    chunk = 0
    for k in range(len(ORDERS[0])):
        chunk = jnp.where(device_of(turn, k) == gx, k, chunk)
    return chunk


def swap_slots(lines):
    slot = iota((8, 128), 1) // CHUNK
    sub = iota((8, 128), 0)
    tiles = []
    for part in range(2):
        total = jnp.zeros((8, 128), F32)
        for k in range(8):
            total = jnp.where(sub == k, lines[part * 8 + k], total)
        tiles.append(total)
    low, high = tiles
    odd = (slot & 8) != 0
    tiles = [
        jnp.where(odd, pltpu.roll(high, 64, 1), low),
        jnp.where(odd, high, pltpu.roll(low, 64, 1)),
    ]
    for bit in (1, 2, 4):
        up = ((sub & bit) == 0) & ((slot & bit) != 0)
        down = ((sub & bit) != 0) & ((slot & bit) == 0)
        for part in range(2):
            tile = tiles[part]
            raised = pltpu.roll(pltpu.roll(tile, 8 - bit, 0), CHUNK * bit, 1)
            lowered = pltpu.roll(pltpu.roll(tile, bit, 0), 128 - CHUNK * bit, 1)
            tiles[part] = jnp.where(up, raised, jnp.where(down, lowered, tile))
    return [tiles[t // 8][t % 8 : t % 8 + 1, :] for t in range(16)]


def turned(tiles):
    return tiles.reshape(128, 128).T.reshape(SLOTS, 8, 128)


def pack_kernel(
    diag_in, inv_in, visc_in, count_in, grounded_in, pattern_in, beta_in, vel_in, message,
    diag, inv, visc, count, grounded, pattern, beta, vel, folded, chunks, arrived,
):
    pairs = (
        (count_in, count), (diag_in, diag), (inv_in, inv), (visc_in, visc), (grounded_in, grounded),
        (pattern_in, pattern), (beta_in, beta), (vel_in, vel),
    )
    copies = [
        pltpu.make_async_copy(source, target, arrived.at[i])
        for i, (source, target) in enumerate(pairs)
    ]
    for copy in copies:
        copy.start()
    for copy in copies:
        copy.wait()
    layer = iota((LAYERS, COLS), 0)
    actives = [layer < count[r : r + 1, :] for r in range(ROWS)]
    for r in range(ROWS):
        for cp in range(16):
            eye = 1.0 if cp % 5 == 0 else 0.0
            for t, table in enumerate((inv, diag)):
                values = jnp.where(actives[r], table[cp, :, r, :], eye)
                at = table_row(t, r, cp)
                folded[at : at + LAYERS, :] = values
    for r in range(ROWS):
        row = slice(r, r + 1)
        viscous = jnp.where(actives[r], visc[:, r, :], 0.0)
        force = -(grounded[row, :].astype(F32) * beta[row, :])
        lines = [viscous[k : k + 1] for k in range(LAYERS)]
        lines += [count[row, :].astype(F32), pattern[row, :].astype(F32)]
        lines += [force * vel[0, row, :], force * vel[1, row, :], beta[row, :]]
        lines += [jnp.zeros((1, COLS), F32)] * (SLOTS - len(lines))
        for part in range(2):
            at = slice(part * 128, part * 128 + 128)
            for k, line in enumerate(swap_slots([line[:, at] for line in lines])):
                chunks[part * SLOTS + k, 24 + r : 25 + r, :] = line
    for part in range(2):
        for m in range(3):
            tiles = folded[m * 128 : m * 128 + 128, part * 128 : part * 128 + 128].T
            at = slice(part * SLOTS, part * SLOTS + SLOTS)
            chunks[at, m * 8 : m * 8 + 8, :] = tiles.reshape(SLOTS, 8, 128)
    turn = lax.axis_index("gy") % 4
    for device in range(2 * SLOTS):
        chunk = pick(turn, [order.index(device) for order in ORDERS])
        message[device * CHUNK_ROWS : (device + 1) * CHUNK_ROWS, :] = chunks[chunk, 0:CHUNK_ROWS, :]


def block_times(table, base, values, transposed):
    out = []
    for c in range(4):
        total = None
        for k in range(4):
            entry = table[base + (k * 4 + c if transposed else c * 4 + k)] * values[k]
            total = entry if total is None else total + entry
        out.append(total)
    return out


def coupled(coupling, direction, values, transposed, sums):
    for c in range(4):
        for k in range(4):
            if transposed:
                factor = coupling[OPPOSITE[direction] * 16 + k * 4 + c]
            else:
                factor = coupling[direction * 16 + c * 4 + k]
            entry = factor * values[k]
            sums[c] = entry if sums[c] is None else sums[c] + entry
    return sums


def x_plus(v):
    first = iota((8, 128), 1) < CHUNK
    inner = pltpu.roll(jnp.where(first, v[2], v[0]), 128 - CHUNK, 1)
    outer = pltpu.roll(jnp.where(first, 0.0, v[2]), 128 - CHUNK, 1)
    return jnp.stack([v[1], inner, v[3], outer])


def x_minus(v):
    last = iota((8, 128), 1) >= 128 - CHUNK
    outer = pltpu.roll(jnp.where(last, 0.0, v[1]), CHUNK, 1)
    inner = pltpu.roll(jnp.where(last, v[1], v[3]), CHUNK, 1)
    return jnp.stack([outer, v[0], inner, v[2]])


def y_plus(v, after):
    column = iota((4, 8, 128), 2) % CHUNK
    return jnp.where(
        column < CHUNK - 1, pltpu.roll(v, 127, 2), pltpu.roll(after, CHUNK - 1, 2)
    )


def y_minus(v, before):
    column = iota((4, 8, 128), 2) % CHUNK
    return jnp.where(column > 0, pltpu.roll(v, 1, 2), pltpu.roll(before, 128 - CHUNK + 1, 2))


def stencil(field, base, after, before, coupling, transposed, kappa):
    here = [field[base + c] for c in range(4)]
    sums = [None] * 4
    sums = coupled(coupling, 0, [pltpu.roll(h, 7, 1) for h in here], transposed, sums)
    sums = coupled(coupling, 1, [pltpu.roll(h, 1, 1) for h in here], transposed, sums)

    def weighted(direction, tiles):
        if kappa is None:
            return tiles
        weight = kappa(direction)
        return [weight * t for t in tiles]

    moved = weighted(0, [x_plus(h) for h in here])
    sums = coupled(coupling, 2, moved, transposed, sums)
    moved = weighted(1, [x_minus(h) for h in here])
    sums = coupled(coupling, 3, moved, transposed, sums)
    moved = weighted(2, [y_plus(here[c], field[after + c]) for c in range(4)])
    sums = coupled(coupling, 4, moved, transposed, sums)
    moved = weighted(3, [y_minus(here[c], field[before + c]) for c in range(4)])
    return coupled(coupling, 5, moved, transposed, sums)


class Forward:
    count, transposed, own = 3, False, 1

    def block(i):
        return i

    def place(i):
        return (i + 1) * 4, (i + 2) * 4, i * 4


class Adjoint:
    count, transposed, own = 4, True, 2

    def block(i):
        return (i % 2) * 2 + 1

    def place(i):
        other = (i + 1 - 2 * (i % 2)) * 4
        return i * 4, other, other


def sweep(kind, res, first, carried, update, image, own_only, tables):
    inv, diag, vis, kappa, coupling = tables
    transposed = kind.transposed

    def initial(i, carry):
        j = kind.block(i)
        at = kind.place(i)[0]
        nu = vis[j]
        values = [res[i * 4 + c] for c in range(4)]
        for c, y in enumerate(block_times(inv, j * 16, values, transposed)):
            first[i * 4 + c] = y
            carried[at + c] = nu * y
        return carry

    lax.fori_loop(0, kind.count, initial, 0)

    def correct(i, carry):
        j = kind.block(i)
        nu = vis[j]
        sums = stencil(
            carried, *kind.place(i), coupling, transposed, lambda d: kappa[j * 4 + d]
        )
        y0 = [first[i * 4 + c] for c in range(4)]
        own = block_times(diag, j * 16, y0, transposed)
        rest = [res[i * 4 + c] - own[c] + nu * sums[c] for c in range(4)]
        for c, y in enumerate(block_times(inv, j * 16, rest, transposed)):
            update[i * 4 + c] = y0[c] + y
        return carry

    lax.fori_loop(0, kind.count, correct, 0)

    def carry_on(i, carry):
        nu = vis[kind.block(i)]
        at = kind.place(i)[0]
        for c in range(4):
            carried[at + c] = nu * update[i * 4 + c]
        return carry

    lax.fori_loop(0, kind.count, carry_on, 0)

    def apply(i, carry):
        if own_only:
            i = i * 2 if kind is Adjoint else 1
        j = kind.block(i)
        sums = stencil(carried, *kind.place(i), coupling, transposed, None)
        values = [update[i * 4 + c] for c in range(4)]
        own = block_times(diag, j * 16, values, transposed)
        nu = vis[j]
        for c in range(4):
            image[i * 4 + c] = own[c] - nu * sums[c]
        return carry

    lax.fori_loop(0, kind.own if own_only else kind.count, apply, 0)


def dots_of(residual, image, last, at_of, pairs):
    def own(ref, v):
        return [ref[at_of(v) + c] for c in range(4)]

    def dot(x, i, y, j):
        part = None
        for a, b in zip(own(x, i), own(y, j)):
            part = a * b if part is None else part + a * b
        return part

    out = []
    for x, y in ((image, image), (residual, image), (residual, last), (image, last), (last, last)):
        for i, j in pairs:
            part = dot(x, i, y, j)
            if i != j:
                part += part if x is y else dot(x, j, y, i)
            tile = (part[0] + part[1]) + (part[2] + part[3])
            line = jnp.sum(tile, axis=0, keepdims=True)
            out.append(jnp.sum(line, axis=1, keepdims=True))
    return out


def merged(after, before):
    return jnp.where(iota((4, 8, 128), 2) % CHUNK < CHUNK // 2, after, before)


def layer_sums(update, spread, target, vector):
    for i, j in enumerate((OWN, NEAR)):
        weight = spread[j]
        active = jnp.where(weight < 0.0, 1.0, 0.0)
        at = (vector * 2 + i) * 4
        for c in range(2):
            tile = update[4 + c] if j == OWN else merged(update[8 + c], update[c])
            target[at + c] = weight * jnp.sum(active * tile, axis=1, keepdims=True)
        for c in range(2, 4):
            target[at + c] = jnp.zeros((4, 8, 128), F32)


def unpack(block, j, inv, diag, vis, small, turned_rows):
    sub = iota((8, 128), 0)
    for half in range(2):
        for m in range(3):
            rows = [
                block[pl.ds((half * SLOTS + s) * CHUNK_ROWS + m * 8, 8), :] for s in range(SLOTS)
            ]
            turned_rows[m * 128 : m * 128 + 128, :] = jnp.concatenate(rows, axis=0).T
        for r in range(ROWS):
            i = half * 2 + r
            for t, target in enumerate((inv, diag)):
                for cp in range(16):
                    at = table_row(t, r, cp)
                    tile = turned_rows[pl.ds(at, 8), :]
                    target[j * 16 + cp, i] = jnp.where(sub < LAYERS, tile, 0.0)
            lines = [
                block[pl.ds((half * SLOTS + s) * CHUNK_ROWS + 24 + r, 1), :] for s in range(SLOTS)
            ]
            tiles = swap_slots(lines)
            for target, base, count in ((vis, 0, LAYERS), (small, LAYERS, 5)):
                total = jnp.zeros((8, 128), F32)
                for k in range(count):
                    total = jnp.where(sub == k, tiles[base + k], total)
                target[j, i] = total


def solve_kernel(
    coupling, low, mine, high, message,
    inv, diag, vis, small, kappa, spread, res, res_two, first, carried, update, image, last, start, turned_rows,
):
    gx, gy = lax.axis_index("gx"), lax.axis_index("gy")
    nx, ny = lax.axis_size("gx"), lax.axis_size("gy")
    chunk = chunk_of(gy % 4, gx)
    for j, block in enumerate((low, mine, high)):
        unpack(block, j, inv, diag, vis, small, turned_rows)
    for c in range(4):
        carried[c] = jnp.zeros((4, 8, 128), F32)
        carried[16 + c] = jnp.zeros((4, 8, 128), F32)

    shape = (4, 8, 128)
    layer = iota(shape, 1)
    lane = iota(shape, 2)
    source = (iota(shape, 0) // 2) * SLOTS + lane // CHUNK
    low_row = iota(shape, 0) % 2 == 0
    for j in range(3):
        tiles = small[j]
        counts = tiles[:, COUNT_ROW : COUNT_ROW + 1, :]
        whole = jnp.maximum(counts, 1.0)
        active = jnp.where(layer.astype(F32) < counts, 1.0, 0.0)
        spread[j] = -active / (whole * whole)
        for c in range(2):
            rhs = tiles[:, RHS_ROW + c : RHS_ROW + c + 1, :]
            res[j * 4 + c] = jnp.where(layer == 0, rhs, 0.0)
        for c in range(2, 4):
            res[j * 4 + c] = jnp.zeros(shape, F32)
        column = (gy * COLS + (chunk + j - OWN) * CHUNK) + lane % CHUNK
        within = column & (COLS - 1)
        south_on = jnp.where((within == 0) & (column > 0), 1.0, 0.0)
        north_on = jnp.where((within == COLS - 1) & (column < ny * COLS - 1), 1.0, 0.0)
        south_in = jnp.where(within == 0, 0.0, 1.0)
        north_in = jnp.where(within == COLS - 1, 0.0, 1.0)
        side_exists = (low_row & (source > 0)) | (jnp.logical_not(low_row) & (source < nx - 1))
        side = jnp.where(side_exists, 1.0, 0.0)
        shared = south_on + north_on + side
        level = (1.0 + tiles[:, PATTERN_ROW : PATTERN_ROW + 1, :]) / 5.0
        own_weight = jnp.where(shared > 0.0, level, 1.0)
        near = (1.0 - own_weight) / jnp.maximum(shared, 1.0)
        inward = own_weight + near * (south_on + north_on)
        outward = own_weight + near * side
        kappa[j * 4] = jnp.where(low_row, inward, outward)
        kappa[j * 4 + 1] = jnp.where(low_row, outward, inward)
        kappa[j * 4 + 2] = own_weight + near * (north_on + side * north_in)
        kappa[j * 4 + 3] = own_weight + near * (south_on + side * south_in)

    for table, size in ((inv, 16), (diag, 16), (kappa, 4), (vis, 1), (spread, 1)):
        for k in range(size):
            table[NEAR * size + k] = merged(table[2 * size + k], table[k])

    tables = (inv, diag, vis, kappa, coupling)
    sweep(Forward, res, first, carried, update, image, False, tables)
    layer_sums(update, spread, res_two, 0)
    for t in range(12):
        res[t] = res[t] - image[t]
    sweep(Forward, res, first, carried, update, last, True, tables)
    layer_sums(update, spread, res_two, 1)
    dots = dots_of(res, image, last, lambda v: 4, ((0, 0),))

    sweep(Adjoint, res_two, first, carried, update, image, False, tables)
    for v in range(2):
        for c in range(4):
            start[v * 4 + c] = update[v * 8 + c]
    for t in range(16):
        res_two[t] = res_two[t] - image[t]
    sweep(Adjoint, res_two, first, carried, update, last, True, tables)
    dots += dots_of(res_two, image, last, lambda v: v * 8, ((0, 0), (0, 1), (1, 1)))

    before, here, after = small[0], small[1], small[2]
    around = x_plus(here) + x_minus(here) + y_plus(here, after) + y_minus(here, before)
    first[0] = 4.0 * here - around
    sub = iota((8, 128), 0)
    column = iota((1, 128), 1) % CHUNK
    lines = []
    for k in range(0, len(dots), CHUNK):
        line = jnp.zeros((1, 128), F32)
        for m, dot in enumerate(dots[k : k + CHUNK]):
            line = jnp.where(column == m, dot, line)
        lines.append(line)

    def send(half, carry):
        for r in range(ROWS):
            i = half * 2 + r
            tiles = [start[k, i] for k in range(8)]
            tiles += [update[v * 8 + c, i] for v in range(2) for c in range(4)]
            prior = pltpu.roll(first[0, i], SPARE - BETA_ROW, 0)
            tiles[0] = jnp.where(sub == SPARE, prior, tiles[0])
            for k, line in enumerate(lines):
                tiles[k] = jnp.where(sub == 7, line, tiles[k])
            message[pl.ds(half * SLOTS, SLOTS), r] = turned(jnp.stack(tiles))
        return carry

    lax.fori_loop(0, 2, send, 0)


def steps(image2, residual_image, residual_last, image_last, last2):
    one = (residual_image + image2) / (image2 + EPSILON)
    off = 1.0 - one
    along = off * residual_image + one * residual_last + off * off * image2 + off * one * image_last
    squared = off * off * image2 + 2.0 * off * one * image_last + one * one * last2
    two = along / (squared + EPSILON)
    return one + two * off, one * two


def gather_kernel(block, lines):
    total = None
    for k in range(block.shape[0]):
        total = block[k, 0] if total is None else total + block[k, 0]
    lane, sub = iota((8, 128), 1), iota((8, 128), 0)
    out = jnp.zeros((8, 128), F32)
    for i in range(8):
        keep = (sub == i) & (lane % CHUNK == 7)
        out += pltpu.roll(jnp.where(keep, total, 0.0), (i - 7) % 128, 1)
    lines[...] = jnp.broadcast_to(jnp.sum(out, axis=0, keepdims=True), lines.shape)


def final_kernel(dots, block, grounded, vel, hessian, adjoint):
    line = jnp.sum(dots[...], axis=0, keepdims=True)
    lane = iota((1, 128), 1)

    def get(k):
        return jnp.sum(jnp.where(lane == k, line, 0.0), axis=1, keepdims=True)

    a, b = steps(*[get(k) for k in range(5)])
    kinds = []
    for k in range(5):
        at = 5 + 3 * k
        kinds.append(a * a * get(at) + a * b * get(at + 1) + b * b * get(at + 2))
    p, q = steps(*kinds)
    weights = (p * a, p * b, q * a, q * b)
    turn = lax.axis_index("gy") % 4
    for part in range(2):
        sources = [device_of(turn, part * SLOTS + k) for k in range(SLOTS)]
        for r in range(ROWS):
            tiles = turned(jnp.stack([block[source, r] for source in sources]))
            at = slice(part * 128, part * 128 + 128)
            heads = []
            for c in range(4):
                total = weights[0] * tiles[c]
                for v in range(1, 4):
                    total += weights[v] * tiles[v * 4 + c]
                adjoint[c, :, r, at] = total[0:LAYERS]
                heads.append(total[0:1])
            row = slice(r, r + 1)
            data = grounded[row, at].astype(F32) * (
                vel[0, row, at] * heads[0] + vel[1, row, at] * heads[1]
            )
            hessian[row, at] = data + PRIOR_WEIGHT * tiles[0, SPARE : SPARE + 1]


VMEM = pl.BlockSpec(memory_space=pltpu.VMEM)
SMEM = pl.BlockSpec(memory_space=pltpu.SMEM)
HBM = pl.BlockSpec(memory_space=pltpu.HBM)


def call(kernel, name, operands, in_specs, outs, scratch=()):
    return pl.pallas_call(
        kernel,
        out_shape=[jax.ShapeDtypeStruct(shape, F32) for shape in outs],
        in_specs=in_specs,
        out_specs=[VMEM] * len(outs),
        scratch_shapes=scratch,
        compiler_params=pltpu.CompilerParams(vmem_limit_bytes=(63 if name == "pack_tables" else 40) * 1024 * 1024),
        name=name,
    )(*operands)


def neighbour_pairs(step):
    n_gy = lax.axis_size("gy")
    places = [gx * n_gy + gy for gy in range(n_gy) for gx in ORDERS[gy % 4]]
    count = len(places)
    return [(places[i], places[i + step]) for i in range(count) if 0 <= i + step < count]


def per_device(
    diag_block,
    block_inverse,
    viscosity,
    coupling,
    active_layers,
    grounded,
    weight_pattern,
    beta_step,
    base_vel,
):
    n_gx, n_gy = lax.axis_size("gx"), lax.axis_size("gy")
    table = (16,) + viscosity.shape
    raw = [
        diag_block.reshape(table),
        block_inverse.reshape(table),
        viscosity,
        active_layers,
        grounded,
        weight_pattern,
        beta_step,
        base_vel,
    ]
    (sent,) = call(
        pack_kernel,
        "pack_tables",
        raw,
        [HBM] * 8,
        [(n_gx * CHUNK_ROWS, 128)],
        [pltpu.VMEM(x.shape, x.dtype) for x in raw]
        + [
            pltpu.VMEM((384, COLS), F32),
            pltpu.VMEM((n_gx, 32, 128), F32),
            pltpu.SemaphoreType.DMA((8,)),
        ],
    )
    sent = sent.reshape(n_gx, CHUNK_ROWS // 2, 2, 128)
    mine = lax.all_to_all(sent, "gx", 0, 0, tiled=True)
    low = lax.ppermute(mine, ("gx", "gy"), neighbour_pairs(1))
    high = lax.ppermute(mine, ("gx", "gy"), neighbour_pairs(-1))
    blocks = [x.reshape(n_gx * CHUNK_ROWS, 128) for x in (low, mine, high)]

    def field(count):
        return pltpu.VMEM((count, 4, 8, 128), F32)

    (back,) = call(
        solve_kernel,
        "solve_both",
        [coupling.reshape(96)] + blocks,
        [SMEM] + [VMEM] * 3,
        [(n_gx, 2, 8, 128)],
        [
            field(64),
            field(64),
            field(4),
            field(3),
            field(16),
            field(4),
            field(12),
            field(16),
            field(16),
            field(20),
            field(16),
            field(16),
            field(16),
            field(8),
            pltpu.VMEM((392, 128), F32),
        ],
    )
    block = lax.all_to_all(back, "gx", 0, 0, tiled=True)
    (lines,) = call(gather_kernel, "sum_gx", [block], [VMEM], [(n_gy, 128)])
    lines = lax.all_to_all(lines, "gy", 0, 0, tiled=True)
    hessian_vec, adjoint = call(
        final_kernel,
        "combine",
        [lines, block, grounded, base_vel],
        [VMEM] * 4,
        [beta_step.shape, (4,) + viscosity.shape],
    )
    return hessian_vec, adjoint


def solution(mesh):
    placed = (
        P(None, None, None, "gx", "gy"),
        P(None, None, None, "gx", "gy"),
        P(None, "gx", "gy"),
        P(),
        P("gx", "gy"),
        P("gx", "gy"),
        P("gx", "gy"),
        P("gx", "gy"),
        P(None, "gx", "gy"),
    )
    return jax.shard_map(
        per_device,
        mesh=mesh,
        in_specs=placed,
        out_specs=(P("gx", "gy"), P(None, None, "gx", "gy")),
        check_vma=False,
    )
```

```python
import jax
import jax.numpy as jnp
from jax import lax
from jax.experimental import pallas as pl
from jax.experimental.pallas import tpu as pltpu
from jax.sharding import PartitionSpec as P

PRIOR_WEIGHT = 0.05
EPSILON = 1e-06
OPPOSITE = (1, 0, 3, 2, 5, 4)
F32 = jnp.float32
LAYERS = 6
ROWS = 2
COLS = 256
CHUNK = 8
SLOTS = 16
OWN, NEAR = 1, 3
CHUNK_ROWS = 26
LINES = 32
COUNT_ROW, PATTERN_ROW, RHS_ROW, BETA_ROW = 0, 1, 2, 4
SPARE = 6


def table_row(table, r, entry):
    return ((table * ROWS + r) * 16 + entry) * LAYERS


def iota(shape, dim):
    return lax.broadcasted_iota(jnp.int32, shape, dim)


ORDERS = (
    (1, 29, 25, 21, 20, 23, 22, 18, 17, 16, 19, 15, 14, 13, 12, 8)
    + (9, 10, 11, 7, 6, 5, 4, 0, 3, 31, 28, 24, 27, 26, 30, 2),
    (2, 3, 7, 4, 8, 11, 15, 12, 16, 20, 24, 25, 26, 22, 21, 17)
    + (13, 9, 5, 1, 0, 28, 29, 30, 31, 27, 23, 19, 18, 14, 10, 6),
    (6, 7, 11, 10, 9, 8, 12, 13, 14, 15, 19, 16, 17, 18, 22, 23)
    + (20, 21, 25, 29, 1, 2, 30, 26, 27, 24, 28, 31, 3, 0, 4, 5),
    (5, 9, 13, 17, 21, 22, 26, 25, 24, 20, 16, 12, 15, 11, 8, 4)
    + (7, 3, 2, 6, 10, 14, 18, 19, 23, 27, 31, 30, 29, 28, 0, 1),
)


def pick(turn, choices):
    low = jnp.where(turn == 0, choices[0], choices[1])
    return jnp.where(turn < 2, low, jnp.where(turn == 2, choices[2], choices[3]))


def device_of(turn, chunk):
    return pick(turn, [order[chunk] for order in ORDERS])


def chunk_of(turn, gx):
    chunk = 0
    for k in range(len(ORDERS[0])):
        chunk = jnp.where(device_of(turn, k) == gx, k, chunk)
    return chunk


def turned(tiles):
    return tiles.reshape(128, 128).T.reshape(SLOTS, 8, 128)


def pack_kernel(
    diag_in, inv_in, visc_in, count_in, grounded_in, pattern_in, beta_in, vel_in, message,
    diag, inv, visc, count, grounded, pattern, beta, vel, folded, others, chunks, arrived,
):
    pairs = (
        (count_in, count), (diag_in, diag), (inv_in, inv), (visc_in, visc), (grounded_in, grounded),
        (pattern_in, pattern), (beta_in, beta), (vel_in, vel),
    )
    copies = [
        pltpu.make_async_copy(source, target, arrived.at[i])
        for i, (source, target) in enumerate(pairs)
    ]
    for copy in copies:
        copy.start()
    for copy in copies:
        copy.wait()
    layer = iota((LAYERS, COLS), 0)
    actives = [layer < count[r : r + 1, :] for r in range(ROWS)]
    for r in range(ROWS):
        for cp in range(16):
            eye = 1.0 if cp % 5 == 0 else 0.0
            for t, table in enumerate((inv, diag)):
                values = jnp.where(actives[r], table[cp, :, r, :], eye)
                at = table_row(t, r, cp)
                folded[at : at + LAYERS, :] = values
    others[...] = jnp.zeros(others.shape, F32)
    for r in range(ROWS):
        row = slice(r, r + 1)
        force = -(grounded[row, :].astype(F32) * beta[row, :])
        others[r * 16 : r * 16 + LAYERS, :] = jnp.where(actives[r], visc[:, r, :], 0.0)
        lines = [count[row, :].astype(F32), pattern[row, :].astype(F32)]
        lines += [force * vel[0, row, :], force * vel[1, row, :], beta[row, :]]
        for k, line in enumerate(lines):
            others[r * 16 + 8 + k : r * 16 + 9 + k, :] = line
    for part in range(2):
        at = slice(part * 128, part * 128 + 128)
        moved = [pltpu.roll(others[:, at], 6 - 2 * m, 1) for m in range(3)] + [others[:, at]]
        tiles = jnp.concatenate(moved, axis=0).T
        chunks[part * SLOTS : part * SLOTS + SLOTS, 18:26, :] = tiles.reshape(SLOTS, 8, 128)
    for part in range(2):
        for m in range(3):
            tiles = folded[m * 128 : m * 128 + 128, part * 128 : part * 128 + 128].T
            at = slice(part * SLOTS, part * SLOTS + SLOTS)
            chunks[at, m * 8 : m * 8 + 8, :] = tiles.reshape(SLOTS, 8, 128)
    turn = lax.axis_index("gy") % 4
    for device in range(2 * SLOTS):
        chunk = pick(turn, [order.index(device) for order in ORDERS])
        message[device * CHUNK_ROWS : (device + 1) * CHUNK_ROWS, :] = chunks[chunk, 0:CHUNK_ROWS, :]


def block_times(table, base, values, transposed):
    out = []
    for c in range(4):
        total = None
        for k in range(4):
            entry = table[base + (k * 4 + c if transposed else c * 4 + k)] * values[k]
            total = entry if total is None else total + entry
        out.append(total)
    return out


def coupled(coupling, direction, values, transposed, sums):
    for c in range(4):
        for k in range(4):
            if transposed:
                factor = coupling[OPPOSITE[direction] * 16 + k * 4 + c]
            else:
                factor = coupling[direction * 16 + c * 4 + k]
            entry = factor * values[k]
            sums[c] = entry if sums[c] is None else sums[c] + entry
    return sums


def x_plus(v):
    first = iota((8, 128), 1) < CHUNK
    inner = pltpu.roll(jnp.where(first, v[2], v[0]), 128 - CHUNK, 1)
    outer = pltpu.roll(jnp.where(first, 0.0, v[2]), 128 - CHUNK, 1)
    return jnp.stack([v[1], inner, v[3], outer])


def x_minus(v):
    last = iota((8, 128), 1) >= 128 - CHUNK
    outer = pltpu.roll(jnp.where(last, 0.0, v[1]), CHUNK, 1)
    inner = pltpu.roll(jnp.where(last, v[1], v[3]), CHUNK, 1)
    return jnp.stack([outer, v[0], inner, v[2]])


def y_plus(v, after):
    column = iota((4, 8, 128), 2) % CHUNK
    return jnp.where(
        column < CHUNK - 1, pltpu.roll(v, 127, 2), pltpu.roll(after, CHUNK - 1, 2)
    )


def y_minus(v, before):
    column = iota((4, 8, 128), 2) % CHUNK
    return jnp.where(column > 0, pltpu.roll(v, 1, 2), pltpu.roll(before, 128 - CHUNK + 1, 2))


def stencil(field, base, after, before, coupling, transposed, kappa):
    here = [field[base + c] for c in range(4)]
    sums = [None] * 4
    sums = coupled(coupling, 0, [pltpu.roll(h, 7, 1) for h in here], transposed, sums)
    sums = coupled(coupling, 1, [pltpu.roll(h, 1, 1) for h in here], transposed, sums)

    def weighted(direction, tiles):
        if kappa is None:
            return tiles
        weight = kappa(direction)
        return [weight * t for t in tiles]

    moved = weighted(0, [x_plus(h) for h in here])
    sums = coupled(coupling, 2, moved, transposed, sums)
    moved = weighted(1, [x_minus(h) for h in here])
    sums = coupled(coupling, 3, moved, transposed, sums)
    moved = weighted(2, [y_plus(here[c], field[after + c]) for c in range(4)])
    sums = coupled(coupling, 4, moved, transposed, sums)
    moved = weighted(3, [y_minus(here[c], field[before + c]) for c in range(4)])
    return coupled(coupling, 5, moved, transposed, sums)


class Forward:
    count, transposed, own = 3, False, 1

    def block(i):
        return i

    def place(i):
        return (i + 1) * 4, (i + 2) * 4, i * 4


class Adjoint:
    count, transposed, own = 4, True, 2

    def block(i):
        return (i % 2) * 2 + 1

    def place(i):
        other = (i + 1 - 2 * (i % 2)) * 4
        return i * 4, other, other


def run_all(count, step):
    for i in range(count):
        step(i, 0)


def sweep(kind, res, first, carried, carried_on, update, image, own_only, tables):
    inv, diag, vis, kappa, coupling = tables
    transposed = kind.transposed

    def initial(i, carry):
        j = kind.block(i)
        at = kind.place(i)[0]
        nu = vis[j]
        values = [res[i * 4 + c] for c in range(4)]
        for c, y in enumerate(block_times(inv, j * 16, values, transposed)):
            first[i * 4 + c] = y
            carried[at + c] = nu * y
        return carry

    run_all(kind.count, initial)

    def correct(i, carry):
        j = kind.block(i)
        nu = vis[j]
        sums = stencil(
            carried, *kind.place(i), coupling, transposed, lambda d: kappa[j * 4 + d]
        )
        y0 = [first[i * 4 + c] for c in range(4)]
        own = block_times(diag, j * 16, y0, transposed)
        rest = [res[i * 4 + c] - own[c] + nu * sums[c] for c in range(4)]
        at = kind.place(i)[0]
        for c, y in enumerate(block_times(inv, j * 16, rest, transposed)):
            z = y0[c] + y
            update[i * 4 + c] = z
            carried_on[at + c] = nu * z
        return carry

    run_all(kind.count, correct)

    def apply(i, carry):
        if own_only:
            i = i * 2 if kind is Adjoint else 1
        j = kind.block(i)
        sums = stencil(carried_on, *kind.place(i), coupling, transposed, None)
        values = [update[i * 4 + c] for c in range(4)]
        own = block_times(diag, j * 16, values, transposed)
        nu = vis[j]
        for c in range(4):
            image[i * 4 + c] = own[c] - nu * sums[c]
        return carry

    run_all(kind.own if own_only else kind.count, apply)


def dots_of(residual, image, last, at_of, pairs):
    def own(ref, v):
        return [ref[at_of(v) + c] for c in range(4)]

    def dot(x, i, y, j):
        part = None
        for a, b in zip(own(x, i), own(y, j)):
            part = a * b if part is None else part + a * b
        return part

    out = []
    for x, y in ((image, image), (residual, image), (residual, last), (image, last), (last, last)):
        for i, j in pairs:
            part = dot(x, i, y, j)
            if i != j:
                part += part if x is y else dot(x, j, y, i)
            tile = (part[0] + part[1]) + (part[2] + part[3])
            line = jnp.sum(tile, axis=0, keepdims=True)
            out.append(jnp.sum(line, axis=1, keepdims=True))
    return out


def merged(after, before):
    return jnp.where(iota((4, 8, 128), 2) % CHUNK < CHUNK // 2, after, before)


def layer_sums(update, spread, target, vector):
    for i, j in enumerate((OWN, NEAR)):
        weight = spread[j]
        active = jnp.where(weight < 0.0, 1.0, 0.0)
        at = (vector * 2 + i) * 4
        for c in range(2):
            tile = update[4 + c] if j == OWN else merged(update[8 + c], update[c])
            target[at + c] = weight * jnp.sum(active * tile, axis=1, keepdims=True)
        for c in range(2, 4):
            target[at + c] = jnp.zeros((4, 8, 128), F32)


def unpack(block, j, inv, diag, vis, small, turned_rows):
    sub = iota((8, 128), 0)
    pair = iota((LINES, 128), 1) % CHUNK // 2
    for half in range(2):

        def rows_at(row):
            at = [(half * SLOTS + s) * CHUNK_ROWS + row for s in range(SLOTS)]
            return jnp.concatenate([block[pl.ds(k, 8), :] for k in at], axis=0).T

        for m in range(3):
            turned_rows[m * 128 : m * 128 + 128, :] = rows_at(m * 8)
        for r in range(ROWS):
            for t, target in enumerate((inv, diag)):
                for cp in range(16):
                    tile = turned_rows[pl.ds(table_row(t, r, cp), 8), :]
                    target[j * 16 + cp, half * 2 + r] = jnp.where(sub < LAYERS, tile, 0.0)
        others = rows_at(18)
        lines = others[3 * LINES :]
        for m in range(3):
            moved = pltpu.roll(others[m * LINES : (m + 1) * LINES], (2 * m - 6) % 128, 1)
            lines = jnp.where(pair == m, moved, lines)
        for r in range(ROWS):
            vis[j, half * 2 + r] = lines[r * 16 : r * 16 + 8]
            small[j, half * 2 + r] = lines[r * 16 + 8 : r * 16 + 16]


def solve_kernel(
    coupling, low, mine, high, message,
    inv, diag, vis, small, kappa, spread, res, res_two, first, carried, carried_on, update, image, last, start, turned_rows,
):
    gx, gy = lax.axis_index("gx"), lax.axis_index("gy")
    nx, ny = lax.axis_size("gx"), lax.axis_size("gy")
    chunk = chunk_of(gy % 4, gx)
    for j, block in enumerate((low, mine, high)):
        unpack(block, j, inv, diag, vis, small, turned_rows)
    for c in range(4):
        for field in (carried, carried_on):
            field[c] = jnp.zeros((4, 8, 128), F32)
            field[16 + c] = jnp.zeros((4, 8, 128), F32)

    shape = (4, 8, 128)
    layer = iota(shape, 1)
    lane = iota(shape, 2)
    source = (iota(shape, 0) // 2) * SLOTS + lane // CHUNK
    low_row = iota(shape, 0) % 2 == 0
    for j in range(3):
        tiles = small[j]
        counts = tiles[:, COUNT_ROW : COUNT_ROW + 1, :]
        whole = jnp.maximum(counts, 1.0)
        active = jnp.where(layer.astype(F32) < counts, 1.0, 0.0)
        spread[j] = -active / (whole * whole)
        for c in range(2):
            rhs = tiles[:, RHS_ROW + c : RHS_ROW + c + 1, :]
            res[j * 4 + c] = jnp.where(layer == 0, rhs, 0.0)
        for c in range(2, 4):
            res[j * 4 + c] = jnp.zeros(shape, F32)
        column = (gy * COLS + (chunk + j - OWN) * CHUNK) + lane % CHUNK
        within = column & (COLS - 1)
        south_on = jnp.where((within == 0) & (column > 0), 1.0, 0.0)
        north_on = jnp.where((within == COLS - 1) & (column < ny * COLS - 1), 1.0, 0.0)
        south_in = jnp.where(within == 0, 0.0, 1.0)
        north_in = jnp.where(within == COLS - 1, 0.0, 1.0)
        side_exists = (low_row & (source > 0)) | (jnp.logical_not(low_row) & (source < nx - 1))
        side = jnp.where(side_exists, 1.0, 0.0)
        shared = south_on + north_on + side
        level = (1.0 + tiles[:, PATTERN_ROW : PATTERN_ROW + 1, :]) / 5.0
        own_weight = jnp.where(shared > 0.0, level, 1.0)
        near = (1.0 - own_weight) / jnp.maximum(shared, 1.0)
        inward = own_weight + near * (south_on + north_on)
        outward = own_weight + near * side
        kappa[j * 4] = jnp.where(low_row, inward, outward)
        kappa[j * 4 + 1] = jnp.where(low_row, outward, inward)
        kappa[j * 4 + 2] = own_weight + near * (north_on + side * north_in)
        kappa[j * 4 + 3] = own_weight + near * (south_on + side * south_in)

    for table, size in ((inv, 16), (diag, 16), (kappa, 4), (vis, 1), (spread, 1)):
        for k in range(size):
            table[NEAR * size + k] = merged(table[2 * size + k], table[k])

    tables = (inv, diag, vis, kappa, coupling)
    sweep(Forward, res, first, carried, carried_on, update, image, False, tables)
    layer_sums(update, spread, res_two, 0)
    for t in range(12):
        res[t] = res[t] - image[t]
    sweep(Forward, res, first, carried, carried_on, update, last, True, tables)
    layer_sums(update, spread, res_two, 1)
    dots = dots_of(res, image, last, lambda v: 4, ((0, 0),))

    sweep(Adjoint, res_two, first, carried, carried_on, update, image, False, tables)
    for v in range(2):
        for c in range(4):
            start[v * 4 + c] = update[v * 8 + c]
    for t in range(16):
        res_two[t] = res_two[t] - image[t]
    sweep(Adjoint, res_two, first, carried, carried_on, update, last, True, tables)
    dots += dots_of(res_two, image, last, lambda v: v * 8, ((0, 0), (0, 1), (1, 1)))

    before, here, after = small[0], small[1], small[2]
    around = x_plus(here) + x_minus(here) + y_plus(here, after) + y_minus(here, before)
    first[0] = 4.0 * here - around
    sub = iota((8, 128), 0)
    column = iota((1, 128), 1) % CHUNK
    lines = []
    for k in range(0, len(dots), CHUNK):
        line = jnp.zeros((1, 128), F32)
        for m, dot in enumerate(dots[k : k + CHUNK]):
            line = jnp.where(column == m, dot, line)
        lines.append(line)

    def send(half, carry):
        for r in range(ROWS):
            i = half * 2 + r
            tiles = [start[k, i] for k in range(8)]
            tiles += [update[v * 8 + c, i] for v in range(2) for c in range(4)]
            prior = pltpu.roll(first[0, i], SPARE - BETA_ROW, 0)
            tiles[0] = jnp.where(sub == SPARE, prior, tiles[0])
            for k, line in enumerate(lines):
                tiles[k] = jnp.where(sub == 7, line, tiles[k])
            message[pl.ds(half * SLOTS, SLOTS), r] = turned(jnp.stack(tiles))
        return carry

    lax.fori_loop(0, 2, send, 0)


def steps(image2, residual_image, residual_last, image_last, last2):
    one = (residual_image + image2) / (image2 + EPSILON)
    off = 1.0 - one
    along = off * residual_image + one * residual_last + off * off * image2 + off * one * image_last
    squared = off * off * image2 + 2.0 * off * one * image_last + one * one * last2
    two = along / (squared + EPSILON)
    return one + two * off, one * two


def gather_kernel(block, lines):
    total = None
    for k in range(block.shape[0]):
        total = block[k, 0] if total is None else total + block[k, 0]
    lane, sub = iota((8, 128), 1), iota((8, 128), 0)
    out = jnp.zeros((8, 128), F32)
    for i in range(8):
        keep = (sub == i) & (lane % CHUNK == 7)
        out += pltpu.roll(jnp.where(keep, total, 0.0), (i - 7) % 128, 1)
    lines[...] = jnp.broadcast_to(jnp.sum(out, axis=0, keepdims=True), lines.shape)


def final_kernel(dots, block, grounded, vel, hessian, adjoint):
    line = jnp.sum(dots[...], axis=0, keepdims=True)
    lane = iota((1, 128), 1)

    def get(k):
        return jnp.sum(jnp.where(lane == k, line, 0.0), axis=1, keepdims=True)

    a, b = steps(*[get(k) for k in range(5)])
    kinds = []
    for k in range(5):
        at = 5 + 3 * k
        kinds.append(a * a * get(at) + a * b * get(at + 1) + b * b * get(at + 2))
    p, q = steps(*kinds)
    weights = (p * a, p * b, q * a, q * b)
    turn = lax.axis_index("gy") % 4
    for part in range(2):
        sources = [device_of(turn, part * SLOTS + k) for k in range(SLOTS)]
        for r in range(ROWS):
            tiles = turned(jnp.stack([block[source, r] for source in sources]))
            at = slice(part * 128, part * 128 + 128)
            heads = []
            for c in range(4):
                total = weights[0] * tiles[c]
                for v in range(1, 4):
                    total += weights[v] * tiles[v * 4 + c]
                adjoint[c, :, r, at] = total[0:LAYERS]
                heads.append(total[0:1])
            row = slice(r, r + 1)
            data = grounded[row, at].astype(F32) * (
                vel[0, row, at] * heads[0] + vel[1, row, at] * heads[1]
            )
            hessian[row, at] = data + PRIOR_WEIGHT * tiles[0, SPARE : SPARE + 1]


VMEM = pl.BlockSpec(memory_space=pltpu.VMEM)
SMEM = pl.BlockSpec(memory_space=pltpu.SMEM)
HBM = pl.BlockSpec(memory_space=pltpu.HBM)


def call(kernel, name, operands, in_specs, outs, scratch=()):
    return pl.pallas_call(
        kernel,
        out_shape=[jax.ShapeDtypeStruct(shape, F32) for shape in outs],
        in_specs=in_specs,
        out_specs=[VMEM] * len(outs),
        scratch_shapes=scratch,
        compiler_params=pltpu.CompilerParams(vmem_limit_bytes=(63 if name == "pack_tables" else 40) * 1024 * 1024),
        name=name,
    )(*operands)


def neighbour_pairs(step):
    n_gy = lax.axis_size("gy")
    places = [gx * n_gy + gy for gy in range(n_gy) for gx in ORDERS[gy % 4]]
    count = len(places)
    return [(places[i], places[i + step]) for i in range(count) if 0 <= i + step < count]


def per_device(
    diag_block,
    block_inverse,
    viscosity,
    coupling,
    active_layers,
    grounded,
    weight_pattern,
    beta_step,
    base_vel,
):
    n_gx, n_gy = lax.axis_size("gx"), lax.axis_size("gy")
    table = (16,) + viscosity.shape
    raw = [
        diag_block.reshape(table),
        block_inverse.reshape(table),
        viscosity,
        active_layers,
        grounded,
        weight_pattern,
        beta_step,
        base_vel,
    ]
    (sent,) = call(
        pack_kernel,
        "pack_tables",
        raw,
        [HBM] * 8,
        [(n_gx * CHUNK_ROWS, 128)],
        [pltpu.VMEM(x.shape, x.dtype) for x in raw]
        + [
            pltpu.VMEM((384, COLS), F32),
            pltpu.VMEM((LINES, COLS), F32),
            pltpu.VMEM((n_gx, 32, 128), F32),
            pltpu.SemaphoreType.DMA((8,)),
        ],
    )
    sent = sent.reshape(n_gx, CHUNK_ROWS // 2, 2, 128)
    mine = lax.all_to_all(sent, "gx", 0, 0, tiled=True)
    low = lax.ppermute(mine, ("gx", "gy"), neighbour_pairs(1))
    high = lax.ppermute(mine, ("gx", "gy"), neighbour_pairs(-1))
    blocks = [x.reshape(n_gx * CHUNK_ROWS, 128) for x in (low, mine, high)]

    def field(count):
        return pltpu.VMEM((count, 4, 8, 128), F32)

    (back,) = call(
        solve_kernel,
        "solve_both",
        [coupling.reshape(96)] + blocks,
        [SMEM] + [VMEM] * 3,
        [(n_gx, 2, 8, 128)],
        [
            field(64),
            field(64),
            field(4),
            field(3),
            field(16),
            field(4),
            field(12),
            field(16),
            field(16),
            field(20),
            field(20),
            field(16),
            field(16),
            field(16),
            field(8),
            pltpu.VMEM((392, 128), F32),
        ],
    )
    block = lax.all_to_all(back, "gx", 0, 0, tiled=True)
    (lines,) = call(gather_kernel, "sum_gx", [block], [VMEM], [(n_gy, 128)])
    lines = lax.all_to_all(lines, "gy", 0, 0, tiled=True)
    hessian_vec, adjoint = call(
        final_kernel,
        "combine",
        [lines, block, grounded, base_vel],
        [VMEM] * 4,
        [beta_step.shape, (4,) + viscosity.shape],
    )
    return hessian_vec, adjoint


def solution(mesh):
    placed = (
        P(None, None, None, "gx", "gy"),
        P(None, None, None, "gx", "gy"),
        P(None, "gx", "gy"),
        P(),
        P("gx", "gy"),
        P("gx", "gy"),
        P("gx", "gy"),
        P("gx", "gy"),
        P(None, "gx", "gy"),
    )
    return jax.shard_map(
        per_device,
        mesh=mesh,
        in_specs=placed,
        out_specs=(P("gx", "gy"), P(None, None, "gx", "gy")),
        check_vma=False,
    )
```

```python
import jax
import jax.numpy as jnp
from jax import lax
from jax.experimental import pallas as pl
from jax.experimental.pallas import tpu as pltpu
from jax.sharding import PartitionSpec as P

PRIOR_WEIGHT = 0.05
EPSILON = 1e-06
OPPOSITE = (1, 0, 3, 2, 5, 4)
F32 = jnp.float32
LAYERS = 6
ROWS = 2
COLS = 256
CHUNK = 8
SLOTS = 16
OWN, NEAR = 1, 3
CHUNK_ROWS = 26
RUNS = (((0, 6, 7), (7, 7, 25)), ((0, 2, 4), (3, 7, 16)), ((0, 3, 0), (4, 7, 21)))
OTHER_ROWS = 14
TO_BEFORE, TO_AFTER = (0, 18), (8, 26)
LINES = 32
COUNT_ROW, PATTERN_ROW, RHS_ROW, BETA_ROW = 0, 1, 2, 4
SPARE = 6


def table_line(table, r, entry):
    return ((table * ROWS + r) * 16 + entry) * 2


def iota(shape, dim):
    return lax.broadcasted_iota(jnp.int32, shape, dim)


ORDERS = (
    (1, 29, 25, 21, 20, 23, 22, 18, 17, 16, 19, 15, 14, 13, 12, 8)
    + (9, 10, 11, 7, 6, 5, 4, 0, 3, 31, 28, 24, 27, 26, 30, 2),
    (2, 3, 7, 4, 8, 11, 15, 12, 16, 20, 24, 25, 26, 22, 21, 17)
    + (13, 9, 5, 1, 0, 28, 29, 30, 31, 27, 23, 19, 18, 14, 10, 6),
    (6, 7, 11, 10, 9, 8, 12, 13, 14, 15, 19, 16, 17, 18, 22, 23)
    + (20, 21, 25, 29, 1, 2, 30, 26, 27, 24, 28, 31, 3, 0, 4, 5),
    (5, 9, 13, 17, 21, 22, 26, 25, 24, 20, 16, 12, 15, 11, 8, 4)
    + (7, 3, 2, 6, 10, 14, 18, 19, 23, 27, 31, 30, 29, 28, 0, 1),
)


def pick(turn, choices):
    low = jnp.where(turn == 0, choices[0], choices[1])
    return jnp.where(turn < 2, low, jnp.where(turn == 2, choices[2], choices[3]))


def device_of(turn, chunk):
    return pick(turn, [order[chunk] for order in ORDERS])


def chunk_of(turn, gx):
    chunk = 0
    for k in range(len(ORDERS[0])):
        chunk = jnp.where(device_of(turn, k) == gx, k, chunk)
    return chunk


def turned(tiles):
    return tiles.reshape(128, 128).T.reshape(SLOTS, 8, 128)


def pack_kernel(
    diag_in, inv_in, visc_in, count_in, grounded_in, pattern_in, beta_in, vel_in, message,
    diag, inv, visc, count, grounded, pattern, beta, vel, folded, others, chunks, arrived,
):
    pairs = (
        (count_in, count), (diag_in, diag), (inv_in, inv), (visc_in, visc), (grounded_in, grounded),
        (pattern_in, pattern), (beta_in, beta), (vel_in, vel),
    )
    copies = [
        pltpu.make_async_copy(source, target, arrived.at[i])
        for i, (source, target) in enumerate(pairs)
    ]
    for copy in copies:
        copy.start()
    for copy in copies:
        copy.wait()
    layer = iota((LAYERS, COLS), 0)
    actives = [layer < count[r : r + 1, :] for r in range(ROWS)]
    for r in range(ROWS):
        for cp in range(16):
            eye = 1.0 if cp % 5 == 0 else 0.0
            for t, table in enumerate((inv, diag)):
                values = jnp.where(actives[r], table[cp, :, r, :], eye)
                for m in range(3):
                    at = m * 128 + table_line(t, r, cp)
                    folded[at : at + 2, :] = values[2 * m : 2 * m + 2]
    others[...] = jnp.zeros(others.shape, F32)
    for r in range(ROWS):
        row = slice(r, r + 1)
        force = -(grounded[row, :].astype(F32) * beta[row, :])
        others[r * 16 : r * 16 + LAYERS, :] = jnp.where(actives[r], visc[:, r, :], 0.0)
        lines = [count[row, :].astype(F32), pattern[row, :].astype(F32)]
        lines += [force * vel[0, row, :], force * vel[1, row, :], beta[row, :]]
        for k, line in enumerate(lines):
            others[r * 16 + 8 + k : r * 16 + 9 + k, :] = line
    for part in range(2):
        at = slice(part * 128, part * 128 + 128)
        moved = [pltpu.roll(others[:, at], 6 - 2 * m, 1) for m in range(3)] + [others[:, at]]
        tiles = jnp.concatenate(moved, axis=0).T
        targets = slice(part * SLOTS, part * SLOTS + SLOTS)
        rows = slice(OTHER_ROWS, OTHER_ROWS + 2)
        chunks[targets, rows, :] = tiles.reshape(SLOTS, 8, 128)[:, 6:8]
    for part in range(2):
        for m in range(3):
            tiles = folded[m * 128 : m * 128 + 128, part * 128 : part * 128 + 128].T
            tiles = tiles.reshape(SLOTS, 8, 128)
            targets = slice(part * SLOTS, part * SLOTS + SLOTS)
            for first, last, row in RUNS[m]:
                rows = slice(row, row + last - first + 1)
                chunks[targets, rows, :] = tiles[:, first : last + 1]
    turn = lax.axis_index("gy") % 4
    for device in range(2 * SLOTS):
        chunk = pick(turn, [order.index(device) for order in ORDERS])
        message[device * CHUNK_ROWS : (device + 1) * CHUNK_ROWS, :] = chunks[chunk, 0:CHUNK_ROWS, :]


def block_times(table, base, values, transposed):
    out = []
    for c in range(4):
        total = None
        for k in range(4):
            entry = table[base + (k * 4 + c if transposed else c * 4 + k)] * values[k]
            total = entry if total is None else total + entry
        out.append(total)
    return out


def coupled(coupling, direction, values, transposed, sums):
    for c in range(4):
        for k in range(4):
            if transposed:
                factor = coupling[OPPOSITE[direction] * 16 + k * 4 + c]
            else:
                factor = coupling[direction * 16 + c * 4 + k]
            entry = factor * values[k]
            sums[c] = entry if sums[c] is None else sums[c] + entry
    return sums


def x_plus(v):
    first = iota((8, 128), 1) < CHUNK
    inner = pltpu.roll(jnp.where(first, v[2], v[0]), 128 - CHUNK, 1)
    outer = pltpu.roll(jnp.where(first, 0.0, v[2]), 128 - CHUNK, 1)
    return jnp.stack([v[1], inner, v[3], outer])


def x_minus(v):
    last = iota((8, 128), 1) >= 128 - CHUNK
    outer = pltpu.roll(jnp.where(last, 0.0, v[1]), CHUNK, 1)
    inner = pltpu.roll(jnp.where(last, v[1], v[3]), CHUNK, 1)
    return jnp.stack([outer, v[0], inner, v[2]])


def y_plus(v, after):
    column = iota((4, 8, 128), 2) % CHUNK
    return jnp.where(
        column < CHUNK - 1, pltpu.roll(v, 127, 2), pltpu.roll(after, CHUNK - 1, 2)
    )


def y_minus(v, before):
    column = iota((4, 8, 128), 2) % CHUNK
    return jnp.where(column > 0, pltpu.roll(v, 1, 2), pltpu.roll(before, 128 - CHUNK + 1, 2))


def stencil(field, base, after, before, coupling, transposed, kappa):
    here = [field[base + c] for c in range(4)]
    sums = [None] * 4
    sums = coupled(coupling, 0, [pltpu.roll(h, 7, 1) for h in here], transposed, sums)
    sums = coupled(coupling, 1, [pltpu.roll(h, 1, 1) for h in here], transposed, sums)

    def weighted(direction, tiles):
        if kappa is None:
            return tiles
        weight = kappa(direction)
        return [weight * t for t in tiles]

    moved = weighted(0, [x_plus(h) for h in here])
    sums = coupled(coupling, 2, moved, transposed, sums)
    moved = weighted(1, [x_minus(h) for h in here])
    sums = coupled(coupling, 3, moved, transposed, sums)
    moved = weighted(2, [y_plus(here[c], field[after + c]) for c in range(4)])
    sums = coupled(coupling, 4, moved, transposed, sums)
    moved = weighted(3, [y_minus(here[c], field[before + c]) for c in range(4)])
    return coupled(coupling, 5, moved, transposed, sums)


class Forward:
    count, transposed, own = 3, False, 1

    def block(i):
        return i

    def place(i):
        return (i + 1) * 4, (i + 2) * 4, i * 4


class Adjoint:
    count, transposed, own = 4, True, 2

    def block(i):
        return (i % 2) * 2 + 1

    def place(i):
        other = (i + 1 - 2 * (i % 2)) * 4
        return i * 4, other, other


def run_all(count, step):
    for i in range(count):
        step(i, 0)


def sweep(kind, res, first, carried, carried_on, update, image, own_only, tables):
    inv, diag, vis, kappa, coupling = tables
    transposed = kind.transposed

    def initial(i, carry):
        j = kind.block(i)
        at = kind.place(i)[0]
        nu = vis[j]
        values = [res[i * 4 + c] for c in range(4)]
        for c, y in enumerate(block_times(inv, j * 16, values, transposed)):
            first[i * 4 + c] = y
            carried[at + c] = nu * y
        return carry

    run_all(kind.count, initial)

    def correct(i, carry):
        j = kind.block(i)
        nu = vis[j]
        sums = stencil(
            carried, *kind.place(i), coupling, transposed, lambda d: kappa[j * 4 + d]
        )
        y0 = [first[i * 4 + c] for c in range(4)]
        own = block_times(diag, j * 16, y0, transposed)
        rest = [res[i * 4 + c] - own[c] + nu * sums[c] for c in range(4)]
        at = kind.place(i)[0]
        for c, y in enumerate(block_times(inv, j * 16, rest, transposed)):
            z = y0[c] + y
            update[i * 4 + c] = z
            carried_on[at + c] = nu * z
        return carry

    run_all(kind.count, correct)

    def apply(i, carry):
        if own_only:
            i = i * 2 if kind is Adjoint else 1
        j = kind.block(i)
        sums = stencil(carried_on, *kind.place(i), coupling, transposed, None)
        values = [update[i * 4 + c] for c in range(4)]
        own = block_times(diag, j * 16, values, transposed)
        nu = vis[j]
        for c in range(4):
            image[i * 4 + c] = own[c] - nu * sums[c]
        return carry

    run_all(kind.own if own_only else kind.count, apply)


def dots_of(residual, image, last, at_of, pairs):
    def own(ref, v):
        return [ref[at_of(v) + c] for c in range(4)]

    def dot(x, i, y, j):
        part = None
        for a, b in zip(own(x, i), own(y, j)):
            part = a * b if part is None else part + a * b
        return part

    out = []
    for x, y in ((image, image), (residual, image), (residual, last), (image, last), (last, last)):
        for i, j in pairs:
            part = dot(x, i, y, j)
            if i != j:
                part += part if x is y else dot(x, j, y, i)
            tile = (part[0] + part[1]) + (part[2] + part[3])
            line = jnp.sum(tile, axis=0, keepdims=True)
            out.append(jnp.sum(line, axis=1, keepdims=True))
    return out


def merged(after, before):
    return jnp.where(iota((4, 8, 128), 2) % CHUNK < CHUNK // 2, after, before)


def layer_sums(update, spread, target, vector):
    for i, j in enumerate((OWN, NEAR)):
        weight = spread[j]
        active = jnp.where(weight < 0.0, 1.0, 0.0)
        at = (vector * 2 + i) * 4
        for c in range(2):
            tile = update[4 + c] if j == OWN else merged(update[8 + c], update[c])
            target[at + c] = weight * jnp.sum(active * tile, axis=1, keepdims=True)
        for c in range(2, 4):
            target[at + c] = jnp.zeros((4, 8, 128), F32)


def unpack(block, part, j, inv, diag, vis, small, turned_rows):
    sub = iota((8, 128), 0)
    pair = iota((LINES, 128), 1) % CHUNK // 2
    size = part[1] - part[0]
    last_start = 2 * SLOTS * size - 8

    def eight(start):
        if start < 0:
            return pltpu.roll(block[pl.ds(0, 8), :], -start, 0)
        if start > last_start:
            return pltpu.roll(block[pl.ds(last_start, 8), :], 8 + last_start - start, 0)
        return block[pl.ds(start, 8), :]

    for half in range(2):
        bases = [(half * SLOTS + s) * size - part[0] for s in range(SLOTS)]
        for m in range(3):
            tiles = [jnp.zeros((8, 128), F32)] * SLOTS
            for first, last, row in RUNS[m]:
                from_row, to_row = max(row, part[0]), min(row + last - first, part[1] - 1)
                if from_row > to_row:
                    continue
                keep = (sub >= from_row - row + first) & (sub <= to_row - row + first)
                tiles = [
                    jnp.where(keep, eight(base + row - first), tile)
                    for base, tile in zip(bases, tiles)
                ]
            turned_rows[m * 128 : m * 128 + 128, :] = jnp.concatenate(tiles, axis=0).T
        for r in range(ROWS):
            for t, target in enumerate((inv, diag)):
                for cp in range(16):
                    line = table_line(t, r, cp)
                    tile = jnp.zeros((8, 128), F32)
                    for m in range(3):
                        layers = turned_rows[pl.ds(m * 128 + line - 2 * m, 8), :]
                        tile = jnp.where(sub // 2 == m, layers, tile)
                    target[j * 16 + cp, half * 2 + r] = tile
        tiles = [eight(base + OTHER_ROWS - 6) for base in bases]
        others = jnp.concatenate(tiles, axis=0).T
        lines = others[3 * LINES :]
        for m in range(3):
            moved = pltpu.roll(others[m * LINES : (m + 1) * LINES], (2 * m - 6) % 128, 1)
            lines = jnp.where(pair == m, moved, lines)
        for r in range(ROWS):
            vis[j, half * 2 + r] = lines[r * 16 : r * 16 + 8]
            small[j, half * 2 + r] = lines[r * 16 + 8 : r * 16 + 16]


def solve_kernel(
    coupling, low, mine, high, message,
    inv, diag, vis, small, kappa, spread, res, res_two, first, carried, carried_on, update, image, last, start, turned_rows,
):
    gx, gy = lax.axis_index("gx"), lax.axis_index("gy")
    nx, ny = lax.axis_size("gx"), lax.axis_size("gy")
    chunk = chunk_of(gy % 4, gx)
    parts = ((low, TO_AFTER), (mine, (0, CHUNK_ROWS)), (high, TO_BEFORE))
    for j, (block, part) in enumerate(parts):
        unpack(block, part, j, inv, diag, vis, small, turned_rows)
    for c in range(4):
        for field in (carried, carried_on):
            field[c] = jnp.zeros((4, 8, 128), F32)
            field[16 + c] = jnp.zeros((4, 8, 128), F32)

    shape = (4, 8, 128)
    layer = iota(shape, 1)
    lane = iota(shape, 2)
    source = (iota(shape, 0) // 2) * SLOTS + lane // CHUNK
    low_row = iota(shape, 0) % 2 == 0
    for j in range(3):
        tiles = small[j]
        counts = tiles[:, COUNT_ROW : COUNT_ROW + 1, :]
        whole = jnp.maximum(counts, 1.0)
        active = jnp.where(layer.astype(F32) < counts, 1.0, 0.0)
        spread[j] = -active / (whole * whole)
        for c in range(2):
            rhs = tiles[:, RHS_ROW + c : RHS_ROW + c + 1, :]
            res[j * 4 + c] = jnp.where(layer == 0, rhs, 0.0)
        for c in range(2, 4):
            res[j * 4 + c] = jnp.zeros(shape, F32)
        column = (gy * COLS + (chunk + j - OWN) * CHUNK) + lane % CHUNK
        within = column & (COLS - 1)
        south_on = jnp.where((within == 0) & (column > 0), 1.0, 0.0)
        north_on = jnp.where((within == COLS - 1) & (column < ny * COLS - 1), 1.0, 0.0)
        south_in = jnp.where(within == 0, 0.0, 1.0)
        north_in = jnp.where(within == COLS - 1, 0.0, 1.0)
        side_exists = (low_row & (source > 0)) | (jnp.logical_not(low_row) & (source < nx - 1))
        side = jnp.where(side_exists, 1.0, 0.0)
        shared = south_on + north_on + side
        level = (1.0 + tiles[:, PATTERN_ROW : PATTERN_ROW + 1, :]) / 5.0
        own_weight = jnp.where(shared > 0.0, level, 1.0)
        near = (1.0 - own_weight) / jnp.maximum(shared, 1.0)
        inward = own_weight + near * (south_on + north_on)
        outward = own_weight + near * side
        kappa[j * 4] = jnp.where(low_row, inward, outward)
        kappa[j * 4 + 1] = jnp.where(low_row, outward, inward)
        kappa[j * 4 + 2] = own_weight + near * (north_on + side * north_in)
        kappa[j * 4 + 3] = own_weight + near * (south_on + side * south_in)

    for table, size in ((inv, 16), (diag, 16), (kappa, 4), (vis, 1), (spread, 1)):
        for k in range(size):
            table[NEAR * size + k] = merged(table[2 * size + k], table[k])

    tables = (inv, diag, vis, kappa, coupling)
    sweep(Forward, res, first, carried, carried_on, update, image, False, tables)
    layer_sums(update, spread, res_two, 0)
    for t in range(12):
        res[t] = res[t] - image[t]
    sweep(Forward, res, first, carried, carried_on, update, last, True, tables)
    layer_sums(update, spread, res_two, 1)
    dots = dots_of(res, image, last, lambda v: 4, ((0, 0),))

    sweep(Adjoint, res_two, first, carried, carried_on, update, image, False, tables)
    for v in range(2):
        for c in range(4):
            start[v * 4 + c] = update[v * 8 + c]
    for t in range(16):
        res_two[t] = res_two[t] - image[t]
    sweep(Adjoint, res_two, first, carried, carried_on, update, last, True, tables)
    dots += dots_of(res_two, image, last, lambda v: v * 8, ((0, 0), (0, 1), (1, 1)))

    before, here, after = small[0], small[1], small[2]
    around = x_plus(here) + x_minus(here) + y_plus(here, after) + y_minus(here, before)
    first[0] = 4.0 * here - around
    sub = iota((8, 128), 0)
    column = iota((1, 128), 1) % CHUNK
    lines = []
    for k in range(0, len(dots), CHUNK):
        line = jnp.zeros((1, 128), F32)
        for m, dot in enumerate(dots[k : k + CHUNK]):
            line = jnp.where(column == m, dot, line)
        lines.append(line)

    def send(half, carry):
        for r in range(ROWS):
            i = half * 2 + r
            tiles = [start[k, i] for k in range(8)]
            tiles += [update[v * 8 + c, i] for v in range(2) for c in range(4)]
            prior = pltpu.roll(first[0, i], SPARE - BETA_ROW, 0)
            tiles[0] = jnp.where(sub == SPARE, prior, tiles[0])
            for k, line in enumerate(lines):
                tiles[k] = jnp.where(sub == 7, line, tiles[k])
            message[pl.ds(half * SLOTS, SLOTS), r] = turned(jnp.stack(tiles))
        return carry

    lax.fori_loop(0, 2, send, 0)


def steps(image2, residual_image, residual_last, image_last, last2):
    one = (residual_image + image2) / (image2 + EPSILON)
    off = 1.0 - one
    along = off * residual_image + one * residual_last + off * off * image2 + off * one * image_last
    squared = off * off * image2 + 2.0 * off * one * image_last + one * one * last2
    two = along / (squared + EPSILON)
    return one + two * off, one * two


def gather_kernel(block, lines):
    total = None
    for k in range(block.shape[0]):
        total = block[k, 0] if total is None else total + block[k, 0]
    lane, sub = iota((8, 128), 1), iota((8, 128), 0)
    out = jnp.zeros((8, 128), F32)
    for i in range(8):
        keep = (sub == i) & (lane % CHUNK == 7)
        out += pltpu.roll(jnp.where(keep, total, 0.0), (i - 7) % 128, 1)
    lines[...] = jnp.broadcast_to(jnp.sum(out, axis=0, keepdims=True), lines.shape)


def final_kernel(dots, block, grounded, vel, hessian, adjoint):
    line = jnp.sum(dots[...], axis=0, keepdims=True)
    lane = iota((1, 128), 1)

    def get(k):
        return jnp.sum(jnp.where(lane == k, line, 0.0), axis=1, keepdims=True)

    a, b = steps(*[get(k) for k in range(5)])
    kinds = []
    for k in range(5):
        at = 5 + 3 * k
        kinds.append(a * a * get(at) + a * b * get(at + 1) + b * b * get(at + 2))
    p, q = steps(*kinds)
    weights = (p * a, p * b, q * a, q * b)
    turn = lax.axis_index("gy") % 4
    for part in range(2):
        sources = [device_of(turn, part * SLOTS + k) for k in range(SLOTS)]
        for r in range(ROWS):
            tiles = turned(jnp.stack([block[source, r] for source in sources]))
            at = slice(part * 128, part * 128 + 128)
            heads = []
            for c in range(4):
                total = weights[0] * tiles[c]
                for v in range(1, 4):
                    total += weights[v] * tiles[v * 4 + c]
                adjoint[c, :, r, at] = total[0:LAYERS]
                heads.append(total[0:1])
            row = slice(r, r + 1)
            data = grounded[row, at].astype(F32) * (
                vel[0, row, at] * heads[0] + vel[1, row, at] * heads[1]
            )
            hessian[row, at] = data + PRIOR_WEIGHT * tiles[0, SPARE : SPARE + 1]


VMEM = pl.BlockSpec(memory_space=pltpu.VMEM)
SMEM = pl.BlockSpec(memory_space=pltpu.SMEM)
HBM = pl.BlockSpec(memory_space=pltpu.HBM)


def call(kernel, name, operands, in_specs, outs, scratch=()):
    return pl.pallas_call(
        kernel,
        out_shape=[jax.ShapeDtypeStruct(shape, F32) for shape in outs],
        in_specs=in_specs,
        out_specs=[VMEM] * len(outs),
        scratch_shapes=scratch,
        compiler_params=pltpu.CompilerParams(vmem_limit_bytes=(63 if name == "pack_tables" else 40) * 1024 * 1024),
        name=name,
    )(*operands)


def neighbour_pairs(step):
    n_gy = lax.axis_size("gy")
    places = [gx * n_gy + gy for gy in range(n_gy) for gx in ORDERS[gy % 4]]
    count = len(places)
    return [(places[i], places[i + step]) for i in range(count) if 0 <= i + step < count]


def per_device(
    diag_block,
    block_inverse,
    viscosity,
    coupling,
    active_layers,
    grounded,
    weight_pattern,
    beta_step,
    base_vel,
):
    n_gx, n_gy = lax.axis_size("gx"), lax.axis_size("gy")
    table = (16,) + viscosity.shape
    raw = [
        diag_block.reshape(table),
        block_inverse.reshape(table),
        viscosity,
        active_layers,
        grounded,
        weight_pattern,
        beta_step,
        base_vel,
    ]
    (sent,) = call(
        pack_kernel,
        "pack_tables",
        raw,
        [HBM] * 8,
        [(n_gx * CHUNK_ROWS, 128)],
        [pltpu.VMEM(x.shape, x.dtype) for x in raw]
        + [
            pltpu.VMEM((384, COLS), F32),
            pltpu.VMEM((LINES, COLS), F32),
            pltpu.VMEM((n_gx, 32, 128), F32),
            pltpu.SemaphoreType.DMA((8,)),
        ],
    )
    sent = sent.reshape(n_gx, CHUNK_ROWS // 2, 2, 128)
    mine = lax.all_to_all(sent, "gx", 0, 0, tiled=True)
    to_after = mine[:, TO_AFTER[0] // 2 : TO_AFTER[1] // 2]
    to_before = mine[:, TO_BEFORE[0] // 2 : TO_BEFORE[1] // 2]
    low = lax.ppermute(to_after, ("gx", "gy"), neighbour_pairs(1))
    high = lax.ppermute(to_before, ("gx", "gy"), neighbour_pairs(-1))
    blocks = [x.reshape(-1, 128) for x in (low, mine, high)]

    def field(count):
        return pltpu.VMEM((count, 4, 8, 128), F32)

    (back,) = call(
        solve_kernel,
        "solve_both",
        [coupling.reshape(96)] + blocks,
        [SMEM] + [VMEM] * 3,
        [(n_gx, 2, 8, 128)],
        [
            field(64),
            field(64),
            field(4),
            field(3),
            field(16),
            field(4),
            field(12),
            field(16),
            field(16),
            field(20),
            field(20),
            field(16),
            field(16),
            field(16),
            field(8),
            pltpu.VMEM((392, 128), F32),
        ],
    )
    block = lax.all_to_all(back, "gx", 0, 0, tiled=True)
    (lines,) = call(gather_kernel, "sum_gx", [block], [VMEM], [(n_gy, 128)])
    lines = lax.all_to_all(lines, "gy", 0, 0, tiled=True)
    hessian_vec, adjoint = call(
        final_kernel,
        "combine",
        [lines, block, grounded, base_vel],
        [VMEM] * 4,
        [beta_step.shape, (4,) + viscosity.shape],
    )
    return hessian_vec, adjoint


def solution(mesh):
    placed = (
        P(None, None, None, "gx", "gy"),
        P(None, None, None, "gx", "gy"),
        P(None, "gx", "gy"),
        P(),
        P("gx", "gy"),
        P("gx", "gy"),
        P("gx", "gy"),
        P("gx", "gy"),
        P(None, "gx", "gy"),
    )
    return jax.shard_map(
        per_device,
        mesh=mesh,
        in_specs=placed,
        out_specs=(P("gx", "gy"), P(None, None, "gx", "gy")),
        check_vma=False,
    )
```

```python
import jax
import jax.numpy as jnp
from jax import lax
from jax.experimental import pallas as pl
from jax.experimental.pallas import tpu as pltpu
from jax.sharding import PartitionSpec as P

PRIOR_WEIGHT = 0.05
EPSILON = 1e-06
OPPOSITE = (1, 0, 3, 2, 5, 4)
F32 = jnp.float32
LAYERS = 6
ROWS = 2
COLS = 256
CHUNK = 8
SLOTS = 16
OWN, NEAR = 1, 3
CHUNK_ROWS = 26
RUNS = (((0, 6, 7), (7, 7, 25)), ((0, 2, 4), (3, 7, 16)), ((0, 3, 0), (4, 7, 21)))
OTHER_ROWS = 14
TO_BEFORE, TO_AFTER = (0, 18), (8, 26)
LINES = 32
COUNT_ROW, PATTERN_ROW, RHS_ROW, BETA_ROW = 0, 1, 2, 4
SPARE = 6


def table_line(table, r, entry):
    return ((table * ROWS + r) * 16 + entry) * 2


def iota(shape, dim):
    return lax.broadcasted_iota(jnp.int32, shape, dim)


ORDERS = (
    (1, 29, 25, 21, 20, 23, 22, 18, 17, 16, 19, 15, 14, 13, 12, 8)
    + (9, 10, 11, 7, 6, 5, 4, 0, 3, 31, 28, 24, 27, 26, 30, 2),
    (2, 3, 7, 4, 8, 11, 15, 12, 16, 20, 24, 25, 26, 22, 21, 17)
    + (13, 9, 5, 1, 0, 28, 29, 30, 31, 27, 23, 19, 18, 14, 10, 6),
    (6, 7, 11, 10, 9, 8, 12, 13, 14, 15, 19, 16, 17, 18, 22, 23)
    + (20, 21, 25, 29, 1, 2, 30, 26, 27, 24, 28, 31, 3, 0, 4, 5),
    (5, 9, 13, 17, 21, 22, 26, 25, 24, 20, 16, 12, 15, 11, 8, 4)
    + (7, 3, 2, 6, 10, 14, 18, 19, 23, 27, 31, 30, 29, 28, 0, 1),
)


def pick(turn, choices):
    low = jnp.where(turn == 0, choices[0], choices[1])
    return jnp.where(turn < 2, low, jnp.where(turn == 2, choices[2], choices[3]))


def device_of(turn, chunk):
    return pick(turn, [order[chunk] for order in ORDERS])


def chunk_of(turn, gx):
    chunk = 0
    for k in range(len(ORDERS[0])):
        chunk = jnp.where(device_of(turn, k) == gx, k, chunk)
    return chunk


def turned(tiles):
    return tiles.reshape(128, 128).T.reshape(SLOTS, 8, 128)


def pack_kernel(
    diag_in, inv_in, visc_in, count_in, grounded_in, pattern_in, beta_in, vel_in, message,
    diag, inv, visc, count, grounded, pattern, beta, vel, folded, others, chunks, arrived,
):
    pairs = (
        (count_in, count), (diag_in, diag), (inv_in, inv), (visc_in, visc), (grounded_in, grounded),
        (pattern_in, pattern), (beta_in, beta), (vel_in, vel),
    )
    copies = [
        pltpu.make_async_copy(source, target, arrived.at[i])
        for i, (source, target) in enumerate(pairs)
    ]
    for copy in copies:
        copy.start()
    for copy in copies:
        copy.wait()
    layer = iota((LAYERS, COLS), 0)
    actives = [layer < count[r : r + 1, :] for r in range(ROWS)]
    for r in range(ROWS):
        for cp in range(16):
            eye = 1.0 if cp % 5 == 0 else 0.0
            for t, table in enumerate((inv, diag)):
                values = jnp.where(actives[r], table[cp, :, r, :], eye)
                for m in range(3):
                    at = m * 128 + table_line(t, r, cp)
                    folded[at : at + 2, :] = values[2 * m : 2 * m + 2]
    others[...] = jnp.zeros(others.shape, F32)
    for r in range(ROWS):
        row = slice(r, r + 1)
        force = -(grounded[row, :].astype(F32) * beta[row, :])
        others[r * 16 : r * 16 + LAYERS, :] = jnp.where(actives[r], visc[:, r, :], 0.0)
        lines = [count[row, :].astype(F32), pattern[row, :].astype(F32)]
        lines += [force * vel[0, row, :], force * vel[1, row, :], beta[row, :]]
        for k, line in enumerate(lines):
            others[r * 16 + 8 + k : r * 16 + 9 + k, :] = line
    for part in range(2):
        at = slice(part * 128, part * 128 + 128)
        moved = [pltpu.roll(others[:, at], 6 - 2 * m, 1) for m in range(3)] + [others[:, at]]
        tiles = jnp.concatenate(moved, axis=0).T
        targets = slice(part * SLOTS, part * SLOTS + SLOTS)
        rows = slice(OTHER_ROWS, OTHER_ROWS + 2)
        chunks[targets, rows, :] = tiles.reshape(SLOTS, 8, 128)[:, 6:8]
    for part in range(2):
        for m in range(3):
            tiles = folded[m * 128 : m * 128 + 128, part * 128 : part * 128 + 128].T
            tiles = tiles.reshape(SLOTS, 8, 128)
            targets = slice(part * SLOTS, part * SLOTS + SLOTS)
            for first, last, row in RUNS[m]:
                rows = slice(row, row + last - first + 1)
                chunks[targets, rows, :] = tiles[:, first : last + 1]
    turn = lax.axis_index("gy") % 4
    for device in range(2 * SLOTS):
        chunk = pick(turn, [order.index(device) for order in ORDERS])
        message[device * CHUNK_ROWS : (device + 1) * CHUNK_ROWS, :] = chunks[chunk, 0:CHUNK_ROWS, :]


def block_times(table, base, values, transposed):
    out = []
    for c in range(4):
        total = None
        for k in range(4):
            entry = table[base + (k * 4 + c if transposed else c * 4 + k)] * values[k]
            total = entry if total is None else total + entry
        out.append(total)
    return out


def split(values):
    parts = []
    for _ in range(3):
        parts.append(values.astype(jnp.bfloat16))
        values = values - parts[-1].astype(F32)
    return parts


PASSES = ((0, 0), (0, 1), (1, 0), (0, 2), (1, 1), (2, 0))
GROUPS = 5


def coupling_matrix(coupling, transposed):
    shape = (8, 32)
    source, layer = iota(shape, 1) // 8, iota(shape, 1) % 8 - iota(shape, 0)

    def line(direction, c):
        if transposed:
            entries = [coupling[OPPOSITE[direction] * 16 + k * 4 + c] for k in range(4)]
        else:
            entries = [coupling[direction * 16 + c * 4 + k] for k in range(4)]
        low = jnp.where(source == 0, entries[0], entries[1])
        high = jnp.where(source == 2, entries[2], entries[3])
        return jnp.where(source < 2, low, high)

    lines = []
    for c in range(4):
        below = jnp.where(layer == -1, line(1, c), 0.0)
        lines.append(jnp.where(layer == 1, line(0, c), below))
    for direction in range(2, 6):
        lines += [jnp.where(layer == 0, line(direction, c), 0.0) for c in range(4)]
    parts = split(jnp.concatenate(lines, axis=0))
    return jnp.concatenate([parts[a] for a, _ in PASSES], axis=1)


def products(matrix, tiles, start=0):
    field = jnp.concatenate(
        [jnp.concatenate([tiles[c][i] for c in range(4)], axis=0) for i in range(4)], axis=1
    )
    parts = split(field)
    rows = jnp.concatenate([parts[b] for _, b in PASSES], axis=0)
    return jnp.dot(matrix[start:], rows, preferred_element_type=F32)


def x_plus(v):
    first = iota((8, 128), 1) < CHUNK
    inner = pltpu.roll(jnp.where(first, v[2], v[0]), 128 - CHUNK, 1)
    outer = pltpu.roll(jnp.where(first, 0.0, v[2]), 128 - CHUNK, 1)
    return jnp.stack([v[1], inner, v[3], outer])


def x_minus(v):
    last = iota((8, 128), 1) >= 128 - CHUNK
    outer = pltpu.roll(jnp.where(last, 0.0, v[1]), CHUNK, 1)
    inner = pltpu.roll(jnp.where(last, v[1], v[3]), CHUNK, 1)
    return jnp.stack([outer, v[0], inner, v[2]])


def y_plus(v, after):
    column = iota((4, 8, 128), 2) % CHUNK
    return jnp.where(
        column < CHUNK - 1, pltpu.roll(v, 127, 2), pltpu.roll(after, CHUNK - 1, 2)
    )


def y_minus(v, before):
    column = iota((4, 8, 128), 2) % CHUNK
    return jnp.where(column > 0, pltpu.roll(v, 1, 2), pltpu.roll(before, 128 - CHUNK + 1, 2))


def stencil(field, place, kappa):
    at, after, before = place

    def group(block, g):
        return [
            jnp.stack(
                [field[block, (g * 4 + c) * 8 : (g * 4 + c) * 8 + 8, pl.ds(i * 128, 128)] for i in range(4)]
            )
            for c in range(4)
        ]

    moved = [
        [x_plus(t) for t in group(at, 1)],
        [x_minus(t) for t in group(at, 2)],
        [y_plus(t, n) for t, n in zip(group(at, 3), group(after, 3))],
        [y_minus(t, n) for t, n in zip(group(at, 4), group(before, 4))],
    ]
    sums = group(at, 0)
    for direction, tiles in enumerate(moved):
        if kappa is not None:
            weight = kappa(direction)
            tiles = [weight * t for t in tiles]
        sums = [a + b for a, b in zip(sums, tiles)]
    return sums


class Forward:
    count, transposed, own = 3, False, 1

    def block(i):
        return i

    def place(i):
        return i + 1, i + 2, i


class Adjoint:
    count, transposed, own = 4, True, 2

    def block(i):
        return (i % 2) * 2 + 1

    def place(i):
        other = i + 1 - 2 * (i % 2)
        return i, other, other


def run_all(count, step):
    for i in range(count):
        step(i, 0)


def sweep(kind, res, first, carried, carried_on, update, image, own_only, tables):
    inv, diag, vis, kappa, matrices = tables
    transposed = kind.transposed
    matrix = matrices[int(transposed)]

    def initial(i, carry):
        j = kind.block(i)
        at = kind.place(i)[0]
        nu = vis[j]
        values = [res[i * 4 + c] for c in range(4)]
        y0 = block_times(inv, j * 16, values, transposed)
        for c in range(4):
            first[i * 4 + c] = y0[c]
        carried[at] = products(matrix, [nu * y for y in y0])
        return carry

    run_all(kind.count, initial)

    def correct(i, carry):
        j = kind.block(i)
        nu = vis[j]
        sums = stencil(carried, kind.place(i), lambda d: kappa[j * 4 + d])
        y0 = [first[i * 4 + c] for c in range(4)]
        own = block_times(diag, j * 16, y0, transposed)
        rest = [res[i * 4 + c] - own[c] + nu * sums[c] for c in range(4)]
        at = kind.place(i)[0]
        y = block_times(inv, j * 16, rest, transposed)
        z = [a + b for a, b in zip(y0, y)]
        for c in range(4):
            update[i * 4 + c] = z[c]
        start = 3 * 32 if own_only and j != OWN else 0
        carried_on[at, start:] = products(matrix, [nu * t for t in z], start)
        return carry

    run_all(kind.count, correct)

    def apply(i, carry):
        if own_only:
            i = i * 2 if kind is Adjoint else 1
        j = kind.block(i)
        sums = stencil(carried_on, kind.place(i), None)
        values = [update[i * 4 + c] for c in range(4)]
        own = block_times(diag, j * 16, values, transposed)
        nu = vis[j]
        for c in range(4):
            image[i * 4 + c] = own[c] - nu * sums[c]
        return carry

    run_all(kind.own if own_only else kind.count, apply)


def dots_of(residual, image, last, at_of, pairs):
    def own(ref, v):
        return [ref[at_of(v) + c] for c in range(4)]

    def dot(x, i, y, j):
        part = None
        for a, b in zip(own(x, i), own(y, j)):
            part = a * b if part is None else part + a * b
        return part

    out = []
    for x, y in ((image, image), (residual, image), (residual, last), (image, last), (last, last)):
        for i, j in pairs:
            part = dot(x, i, y, j)
            if i != j:
                part += part if x is y else dot(x, j, y, i)
            tile = (part[0] + part[1]) + (part[2] + part[3])
            line = jnp.sum(tile, axis=0, keepdims=True)
            out.append(jnp.sum(line, axis=1, keepdims=True))
    return out


def merged(after, before):
    return jnp.where(iota((4, 8, 128), 2) % CHUNK < CHUNK // 2, after, before)


def layer_sums(update, spread, target, vector):
    for i, j in enumerate((OWN, NEAR)):
        weight = spread[j]
        active = jnp.where(weight < 0.0, 1.0, 0.0)
        at = (vector * 2 + i) * 4
        for c in range(2):
            tile = update[4 + c] if j == OWN else merged(update[8 + c], update[c])
            target[at + c] = weight * jnp.sum(active * tile, axis=1, keepdims=True)
        for c in range(2, 4):
            target[at + c] = jnp.zeros((4, 8, 128), F32)


def unpack(block, part, j, inv, diag, vis, small, turned_rows):
    sub = iota((8, 128), 0)
    pair = iota((LINES, 128), 1) % CHUNK // 2
    size = part[1] - part[0]
    last_start = 2 * SLOTS * size - 8

    def eight(start):
        if start < 0:
            return pltpu.roll(block[pl.ds(0, 8), :], -start, 0)
        if start > last_start:
            return pltpu.roll(block[pl.ds(last_start, 8), :], 8 + last_start - start, 0)
        return block[pl.ds(start, 8), :]

    for half in range(2):
        bases = [(half * SLOTS + s) * size - part[0] for s in range(SLOTS)]
        for m in range(3):
            tiles = [jnp.zeros((8, 128), F32)] * SLOTS
            for first, last, row in RUNS[m]:
                from_row, to_row = max(row, part[0]), min(row + last - first, part[1] - 1)
                if from_row > to_row:
                    continue
                keep = (sub >= from_row - row + first) & (sub <= to_row - row + first)
                tiles = [
                    jnp.where(keep, eight(base + row - first), tile)
                    for base, tile in zip(bases, tiles)
                ]
            turned_rows[m * 128 : m * 128 + 128, :] = jnp.concatenate(tiles, axis=0).T
        for r in range(ROWS):
            for t, target in enumerate((inv, diag)):
                for cp in range(16):
                    line = table_line(t, r, cp)
                    tile = jnp.zeros((8, 128), F32)
                    for m in range(3):
                        layers = turned_rows[pl.ds(m * 128 + line - 2 * m, 8), :]
                        tile = jnp.where(sub // 2 == m, layers, tile)
                    target[j * 16 + cp, half * 2 + r] = tile
        tiles = [eight(base + OTHER_ROWS - 6) for base in bases]
        others = jnp.concatenate(tiles, axis=0).T
        lines = others[3 * LINES :]
        for m in range(3):
            moved = pltpu.roll(others[m * LINES : (m + 1) * LINES], (2 * m - 6) % 128, 1)
            lines = jnp.where(pair == m, moved, lines)
        for r in range(ROWS):
            vis[j, half * 2 + r] = lines[r * 16 : r * 16 + 8]
            small[j, half * 2 + r] = lines[r * 16 + 8 : r * 16 + 16]


def solve_kernel(
    coupling, low, mine, high, message,
    inv, diag, vis, small, kappa, spread, res, res_two, first, carried, carried_on, update, image, last, start, turned_rows,
    matrix_forward, matrix_adjoint,
):
    gx, gy = lax.axis_index("gx"), lax.axis_index("gy")
    nx, ny = lax.axis_size("gx"), lax.axis_size("gy")
    chunk = chunk_of(gy % 4, gx)
    parts = ((low, TO_AFTER), (mine, (0, CHUNK_ROWS)), (high, TO_BEFORE))
    for j, (block, part) in enumerate(parts):
        unpack(block, part, j, inv, diag, vis, small, turned_rows)
    for field in (carried, carried_on):
        for empty in (0, 4):
            field[empty] = jnp.zeros(field.shape[1:], F32)
    for transposed, matrix in enumerate((matrix_forward, matrix_adjoint)):
        matrix[...] = coupling_matrix(coupling, transposed)

    shape = (4, 8, 128)
    layer = iota(shape, 1)
    lane = iota(shape, 2)
    source = (iota(shape, 0) // 2) * SLOTS + lane // CHUNK
    low_row = iota(shape, 0) % 2 == 0
    for j in range(3):
        tiles = small[j]
        counts = tiles[:, COUNT_ROW : COUNT_ROW + 1, :]
        whole = jnp.maximum(counts, 1.0)
        active = jnp.where(layer.astype(F32) < counts, 1.0, 0.0)
        spread[j] = -active / (whole * whole)
        for c in range(2):
            rhs = tiles[:, RHS_ROW + c : RHS_ROW + c + 1, :]
            res[j * 4 + c] = jnp.where(layer == 0, rhs, 0.0)
        for c in range(2, 4):
            res[j * 4 + c] = jnp.zeros(shape, F32)
        column = (gy * COLS + (chunk + j - OWN) * CHUNK) + lane % CHUNK
        within = column & (COLS - 1)
        south_on = jnp.where((within == 0) & (column > 0), 1.0, 0.0)
        north_on = jnp.where((within == COLS - 1) & (column < ny * COLS - 1), 1.0, 0.0)
        south_in = jnp.where(within == 0, 0.0, 1.0)
        north_in = jnp.where(within == COLS - 1, 0.0, 1.0)
        side_exists = (low_row & (source > 0)) | (jnp.logical_not(low_row) & (source < nx - 1))
        side = jnp.where(side_exists, 1.0, 0.0)
        shared = south_on + north_on + side
        level = (1.0 + tiles[:, PATTERN_ROW : PATTERN_ROW + 1, :]) / 5.0
        own_weight = jnp.where(shared > 0.0, level, 1.0)
        near = (1.0 - own_weight) / jnp.maximum(shared, 1.0)
        inward = own_weight + near * (south_on + north_on)
        outward = own_weight + near * side
        kappa[j * 4] = jnp.where(low_row, inward, outward)
        kappa[j * 4 + 1] = jnp.where(low_row, outward, inward)
        kappa[j * 4 + 2] = own_weight + near * (north_on + side * north_in)
        kappa[j * 4 + 3] = own_weight + near * (south_on + side * south_in)

    for table, size in ((inv, 16), (diag, 16), (kappa, 4), (vis, 1), (spread, 1)):
        for k in range(size):
            table[NEAR * size + k] = merged(table[2 * size + k], table[k])

    tables = (inv, diag, vis, kappa, (matrix_forward, matrix_adjoint))
    sweep(Forward, res, first, carried, carried_on, update, image, False, tables)
    layer_sums(update, spread, res_two, 0)
    for t in range(12):
        res[t] = res[t] - image[t]
    sweep(Forward, res, first, carried, carried_on, update, last, True, tables)
    layer_sums(update, spread, res_two, 1)
    dots = dots_of(res, image, last, lambda v: 4, ((0, 0),))

    sweep(Adjoint, res_two, first, carried, carried_on, update, image, False, tables)
    for v in range(2):
        for c in range(4):
            start[v * 4 + c] = update[v * 8 + c]
    for t in range(16):
        res_two[t] = res_two[t] - image[t]
    sweep(Adjoint, res_two, first, carried, carried_on, update, last, True, tables)
    dots += dots_of(res_two, image, last, lambda v: v * 8, ((0, 0), (0, 1), (1, 1)))

    before, here, after = small[0], small[1], small[2]
    around = x_plus(here) + x_minus(here) + y_plus(here, after) + y_minus(here, before)
    first[0] = 4.0 * here - around
    sub = iota((8, 128), 0)
    column = iota((1, 128), 1) % CHUNK
    lines = []
    for k in range(0, len(dots), CHUNK):
        line = jnp.zeros((1, 128), F32)
        for m, dot in enumerate(dots[k : k + CHUNK]):
            line = jnp.where(column == m, dot, line)
        lines.append(line)

    def send(half, carry):
        for r in range(ROWS):
            i = half * 2 + r
            tiles = [start[k, i] for k in range(8)]
            tiles += [update[v * 8 + c, i] for v in range(2) for c in range(4)]
            prior = pltpu.roll(first[0, i], SPARE - BETA_ROW, 0)
            tiles[0] = jnp.where(sub == SPARE, prior, tiles[0])
            for k, line in enumerate(lines):
                tiles[k] = jnp.where(sub == 7, line, tiles[k])
            message[pl.ds(half * SLOTS, SLOTS), r] = turned(jnp.stack(tiles))
        return carry

    lax.fori_loop(0, 2, send, 0)


def steps(image2, residual_image, residual_last, image_last, last2):
    one = (residual_image + image2) / (image2 + EPSILON)
    off = 1.0 - one
    along = off * residual_image + one * residual_last + off * off * image2 + off * one * image_last
    squared = off * off * image2 + 2.0 * off * one * image_last + one * one * last2
    two = along / (squared + EPSILON)
    return one + two * off, one * two


def gather_kernel(block, lines):
    total = None
    for k in range(block.shape[0]):
        total = block[k, 0] if total is None else total + block[k, 0]
    lane, sub = iota((8, 128), 1), iota((8, 128), 0)
    out = jnp.zeros((8, 128), F32)
    for i in range(8):
        keep = (sub == i) & (lane % CHUNK == 7)
        out += pltpu.roll(jnp.where(keep, total, 0.0), (i - 7) % 128, 1)
    lines[...] = jnp.broadcast_to(jnp.sum(out, axis=0, keepdims=True), lines.shape)


def final_kernel(dots, block, grounded, vel, hessian, adjoint):
    line = jnp.sum(dots[...], axis=0, keepdims=True)
    lane = iota((1, 128), 1)

    def get(k):
        return jnp.sum(jnp.where(lane == k, line, 0.0), axis=1, keepdims=True)

    a, b = steps(*[get(k) for k in range(5)])
    kinds = []
    for k in range(5):
        at = 5 + 3 * k
        kinds.append(a * a * get(at) + a * b * get(at + 1) + b * b * get(at + 2))
    p, q = steps(*kinds)
    weights = (p * a, p * b, q * a, q * b)
    turn = lax.axis_index("gy") % 4
    for part in range(2):
        sources = [device_of(turn, part * SLOTS + k) for k in range(SLOTS)]
        for r in range(ROWS):
            tiles = turned(jnp.stack([block[source, r] for source in sources]))
            at = slice(part * 128, part * 128 + 128)
            heads = []
            for c in range(4):
                total = weights[0] * tiles[c]
                for v in range(1, 4):
                    total += weights[v] * tiles[v * 4 + c]
                adjoint[c, :, r, at] = total[0:LAYERS]
                heads.append(total[0:1])
            row = slice(r, r + 1)
            data = grounded[row, at].astype(F32) * (
                vel[0, row, at] * heads[0] + vel[1, row, at] * heads[1]
            )
            hessian[row, at] = data + PRIOR_WEIGHT * tiles[0, SPARE : SPARE + 1]


VMEM = pl.BlockSpec(memory_space=pltpu.VMEM)
SMEM = pl.BlockSpec(memory_space=pltpu.SMEM)
HBM = pl.BlockSpec(memory_space=pltpu.HBM)


def call(kernel, name, operands, in_specs, outs, scratch=()):
    return pl.pallas_call(
        kernel,
        out_shape=[jax.ShapeDtypeStruct(shape, F32) for shape in outs],
        in_specs=in_specs,
        out_specs=[VMEM] * len(outs),
        scratch_shapes=scratch,
        compiler_params=pltpu.CompilerParams(vmem_limit_bytes=(63 if name == "pack_tables" else 40) * 1024 * 1024),
        name=name,
    )(*operands)


def neighbour_pairs(step):
    n_gy = lax.axis_size("gy")
    places = [gx * n_gy + gy for gy in range(n_gy) for gx in ORDERS[gy % 4]]
    count = len(places)
    return [(places[i], places[i + step]) for i in range(count) if 0 <= i + step < count]


def per_device(
    diag_block,
    block_inverse,
    viscosity,
    coupling,
    active_layers,
    grounded,
    weight_pattern,
    beta_step,
    base_vel,
):
    n_gx, n_gy = lax.axis_size("gx"), lax.axis_size("gy")
    table = (16,) + viscosity.shape
    raw = [
        diag_block.reshape(table),
        block_inverse.reshape(table),
        viscosity,
        active_layers,
        grounded,
        weight_pattern,
        beta_step,
        base_vel,
    ]
    (sent,) = call(
        pack_kernel,
        "pack_tables",
        raw,
        [HBM] * 8,
        [(n_gx * CHUNK_ROWS, 128)],
        [pltpu.VMEM(x.shape, x.dtype) for x in raw]
        + [
            pltpu.VMEM((384, COLS), F32),
            pltpu.VMEM((LINES, COLS), F32),
            pltpu.VMEM((n_gx, 32, 128), F32),
            pltpu.SemaphoreType.DMA((8,)),
        ],
    )
    sent = sent.reshape(n_gx, CHUNK_ROWS // 2, 2, 128)
    mine = lax.all_to_all(sent, "gx", 0, 0, tiled=True)
    to_after = mine[:, TO_AFTER[0] // 2 : TO_AFTER[1] // 2]
    to_before = mine[:, TO_BEFORE[0] // 2 : TO_BEFORE[1] // 2]
    low = lax.ppermute(to_after, ("gx", "gy"), neighbour_pairs(1))
    high = lax.ppermute(to_before, ("gx", "gy"), neighbour_pairs(-1))
    blocks = [x.reshape(-1, 128) for x in (low, mine, high)]

    def field(count):
        return pltpu.VMEM((count, 4, 8, 128), F32)

    (back,) = call(
        solve_kernel,
        "solve_both",
        [coupling.reshape(96)] + blocks,
        [SMEM] + [VMEM] * 3,
        [(n_gx, 2, 8, 128)],
        [
            field(64),
            field(64),
            field(4),
            field(3),
            field(16),
            field(4),
            field(12),
            field(16),
            field(16),
            pltpu.VMEM((5, GROUPS * 32, 512), F32),
            pltpu.VMEM((5, GROUPS * 32, 512), F32),
            field(16),
            field(16),
            field(16),
            field(8),
            pltpu.VMEM((392, 128), F32),
        ]
        + [pltpu.VMEM((GROUPS * 32, len(PASSES) * 32), jnp.bfloat16)] * 2,
    )
    block = lax.all_to_all(back, "gx", 0, 0, tiled=True)
    (lines,) = call(gather_kernel, "sum_gx", [block], [VMEM], [(n_gy, 128)])
    lines = lax.all_to_all(lines, "gy", 0, 0, tiled=True)
    hessian_vec, adjoint = call(
        final_kernel,
        "combine",
        [lines, block, grounded, base_vel],
        [VMEM] * 4,
        [beta_step.shape, (4,) + viscosity.shape],
    )
    return hessian_vec, adjoint


def solution(mesh):
    placed = (
        P(None, None, None, "gx", "gy"),
        P(None, None, None, "gx", "gy"),
        P(None, "gx", "gy"),
        P(),
        P("gx", "gy"),
        P("gx", "gy"),
        P("gx", "gy"),
        P("gx", "gy"),
        P(None, "gx", "gy"),
    )
    return jax.shard_map(
        per_device,
        mesh=mesh,
        in_specs=placed,
        out_specs=(P("gx", "gy"), P(None, None, "gx", "gy")),
        check_vma=False,
    )
```

```python
import jax
import jax.numpy as jnp
from jax import lax
from jax.experimental import pallas as pl
from jax.experimental.pallas import tpu as pltpu
from jax.sharding import PartitionSpec as P

PRIOR_WEIGHT = 0.05
EPSILON = 1e-06
OPPOSITE = (1, 0, 3, 2, 5, 4)
F32 = jnp.float32
LAYERS = 6
ROWS = 2
COLS = 256
CHUNK = 8
SLOTS = 16
OWN, NEAR = 1, 3
CHUNK_ROWS = 26
RUNS = (((0, 6, 7), (7, 7, 25)), ((0, 2, 4), (3, 7, 16)), ((0, 3, 0), (4, 7, 21)))
OTHER_ROWS = 14
TO_BEFORE, TO_AFTER = (0, 18), (8, 26)
LINES = 32
COUNT_ROW, PATTERN_ROW, RHS_ROW, BETA_ROW = 0, 1, 2, 4
SPARE = 6


def table_line(table, r, entry):
    return ((table * ROWS + r) * 16 + entry) * 2


def iota(shape, dim):
    return lax.broadcasted_iota(jnp.int32, shape, dim)


ORDERS = (
    (1, 29, 25, 21, 20, 23, 22, 18, 17, 16, 19, 15, 14, 13, 12, 8)
    + (9, 10, 11, 7, 6, 5, 4, 0, 3, 31, 28, 24, 27, 26, 30, 2),
    (2, 3, 7, 4, 8, 11, 15, 12, 16, 20, 24, 25, 26, 22, 21, 17)
    + (13, 9, 5, 1, 0, 28, 29, 30, 31, 27, 23, 19, 18, 14, 10, 6),
    (6, 7, 11, 10, 9, 8, 12, 13, 14, 15, 19, 16, 17, 18, 22, 23)
    + (20, 21, 25, 29, 1, 2, 30, 26, 27, 24, 28, 31, 3, 0, 4, 5),
    (5, 9, 13, 17, 21, 22, 26, 25, 24, 20, 16, 12, 15, 11, 8, 4)
    + (7, 3, 2, 6, 10, 14, 18, 19, 23, 27, 31, 30, 29, 28, 0, 1),
)


def pick(turn, choices):
    low = jnp.where(turn == 0, choices[0], choices[1])
    return jnp.where(turn < 2, low, jnp.where(turn == 2, choices[2], choices[3]))


def device_of(turn, chunk):
    return pick(turn, [order[chunk] for order in ORDERS])


def chunk_of(turn, gx):
    chunk = 0
    for k in range(len(ORDERS[0])):
        chunk = jnp.where(device_of(turn, k) == gx, k, chunk)
    return chunk


def turned(tiles):
    return tiles.reshape(128, 128).T.reshape(SLOTS, 8, 128)


def pack_kernel(
    diag_in, inv_in, visc_in, count_in, grounded_in, pattern_in, beta_in, vel_in, message,
    diag, inv, visc, count, grounded, pattern, beta, vel, folded, others, chunks, arrived,
):
    pairs = (
        (count_in, count), (diag_in, diag), (inv_in, inv), (visc_in, visc), (grounded_in, grounded),
        (pattern_in, pattern), (beta_in, beta), (vel_in, vel),
    )
    copies = [
        pltpu.make_async_copy(source, target, arrived.at[i])
        for i, (source, target) in enumerate(pairs)
    ]
    for copy in copies:
        copy.start()
    for copy in copies:
        copy.wait()
    layer = iota((LAYERS, COLS), 0)
    actives = [layer < count[r : r + 1, :] for r in range(ROWS)]
    for r in range(ROWS):
        for cp in range(16):
            eye = 1.0 if cp % 5 == 0 else 0.0
            for t, table in enumerate((inv, diag)):
                values = jnp.where(actives[r], table[cp, :, r, :], eye)
                for m in range(3):
                    at = m * 128 + table_line(t, r, cp)
                    folded[at : at + 2, :] = values[2 * m : 2 * m + 2]
    others[...] = jnp.zeros(others.shape, F32)
    for r in range(ROWS):
        row = slice(r, r + 1)
        force = -(grounded[row, :].astype(F32) * beta[row, :])
        others[r * 16 : r * 16 + LAYERS, :] = jnp.where(actives[r], visc[:, r, :], 0.0)
        lines = [count[row, :].astype(F32), pattern[row, :].astype(F32)]
        lines += [force * vel[0, row, :], force * vel[1, row, :], beta[row, :]]
        for k, line in enumerate(lines):
            others[r * 16 + 8 + k : r * 16 + 9 + k, :] = line
    for part in range(2):
        at = slice(part * 128, part * 128 + 128)
        moved = [pltpu.roll(others[:, at], 6 - 2 * m, 1) for m in range(3)] + [others[:, at]]
        tiles = jnp.concatenate(moved, axis=0).T
        targets = slice(part * SLOTS, part * SLOTS + SLOTS)
        rows = slice(OTHER_ROWS, OTHER_ROWS + 2)
        chunks[targets, rows, :] = tiles.reshape(SLOTS, 8, 128)[:, 6:8]
    for part in range(2):
        for m in range(3):
            tiles = folded[m * 128 : m * 128 + 128, part * 128 : part * 128 + 128].T
            tiles = tiles.reshape(SLOTS, 8, 128)
            targets = slice(part * SLOTS, part * SLOTS + SLOTS)
            for first, last, row in RUNS[m]:
                rows = slice(row, row + last - first + 1)
                chunks[targets, rows, :] = tiles[:, first : last + 1]
    turn = lax.axis_index("gy") % 4
    for device in range(2 * SLOTS):
        chunk = pick(turn, [order.index(device) for order in ORDERS])
        message[device * CHUNK_ROWS : (device + 1) * CHUNK_ROWS, :] = chunks[chunk, 0:CHUNK_ROWS, :]


def block_times(table, base, values, transposed, used=4):
    out = []
    for c in range(4):
        total = None
        for k in range(used):
            entry = table[base + (k * 4 + c if transposed else c * 4 + k)] * values[k]
            total = entry if total is None else total + entry
        out.append(total)
    return out


def split(values):
    parts = []
    for _ in range(3):
        parts.append(values.astype(jnp.bfloat16))
        values = values - parts[-1].astype(F32)
    return parts


PASSES = ((0, 0), (0, 1), (1, 0), (0, 2), (1, 1), (2, 0))
GROUPS = 5


def coupling_matrix(coupling, transposed):
    shape = (8, 32)
    source, layer = iota(shape, 1) // 8, iota(shape, 1) % 8 - iota(shape, 0)

    def line(direction, c):
        if transposed:
            entries = [coupling[OPPOSITE[direction] * 16 + k * 4 + c] for k in range(4)]
        else:
            entries = [coupling[direction * 16 + c * 4 + k] for k in range(4)]
        low = jnp.where(source == 0, entries[0], entries[1])
        high = jnp.where(source == 2, entries[2], entries[3])
        return jnp.where(source < 2, low, high)

    lines = []
    for c in range(4):
        below = jnp.where(layer == -1, line(1, c), 0.0)
        lines.append(jnp.where(layer == 1, line(0, c), below))
    for direction in range(2, 6):
        lines += [jnp.where(layer == 0, line(direction, c), 0.0) for c in range(4)]
    parts = split(jnp.concatenate(lines, axis=0))
    return jnp.concatenate([parts[a] for a, _ in PASSES], axis=1)


def products(matrix, tiles, start=0):
    field = jnp.concatenate(
        [jnp.concatenate([tiles[c][i] for c in range(4)], axis=0) for i in range(4)], axis=1
    )
    parts = split(field)
    rows = jnp.concatenate([parts[b] for _, b in PASSES], axis=0)
    return jnp.dot(matrix[start:], rows, preferred_element_type=F32)


def x_plus(v):
    first = iota((8, 128), 1) < CHUNK
    inner = pltpu.roll(jnp.where(first, v[2], v[0]), 128 - CHUNK, 1)
    outer = pltpu.roll(jnp.where(first, 0.0, v[2]), 128 - CHUNK, 1)
    return jnp.stack([v[1], inner, v[3], outer])


def x_minus(v):
    last = iota((8, 128), 1) >= 128 - CHUNK
    outer = pltpu.roll(jnp.where(last, 0.0, v[1]), CHUNK, 1)
    inner = pltpu.roll(jnp.where(last, v[1], v[3]), CHUNK, 1)
    return jnp.stack([outer, v[0], inner, v[2]])


def y_plus(v, after):
    column = iota((4, 8, 128), 2) % CHUNK
    return jnp.where(
        column < CHUNK - 1, pltpu.roll(v, 127, 2), pltpu.roll(after, CHUNK - 1, 2)
    )


def y_minus(v, before):
    column = iota((4, 8, 128), 2) % CHUNK
    return jnp.where(column > 0, pltpu.roll(v, 1, 2), pltpu.roll(before, 128 - CHUNK + 1, 2))


def stencil(field, place, kappa):
    at, after, before = place

    def group(block, g):
        return [
            jnp.stack(
                [field[block, (g * 4 + c) * 8 : (g * 4 + c) * 8 + 8, pl.ds(i * 128, 128)] for i in range(4)]
            )
            for c in range(4)
        ]

    moved = [
        [x_plus(t) for t in group(at, 1)],
        [x_minus(t) for t in group(at, 2)],
        [y_plus(t, n) for t, n in zip(group(at, 3), group(after, 3))],
        [y_minus(t, n) for t, n in zip(group(at, 4), group(before, 4))],
    ]
    sums = group(at, 0)
    for direction, tiles in enumerate(moved):
        if kappa is not None:
            weight = kappa(direction)
            tiles = [weight * t for t in tiles]
        sums = [a + b for a, b in zip(sums, tiles)]
    return sums


class Forward:
    count, transposed, own = 3, False, 1

    def block(i):
        return i

    def place(i):
        return i + 1, i + 2, i


class Adjoint:
    count, transposed, own = 4, True, 2

    def block(i):
        return (i % 2) * 2 + 1

    def place(i):
        other = i + 1 - 2 * (i % 2)
        return i, other, other


def run_all(count, step):
    for i in range(count):
        step(i, 0)


def sweep(kind, res, first, carried, carried_on, update, image, own_only, tables):
    inv, diag, vis, kappa, matrices = tables
    transposed = kind.transposed
    matrix = matrices[int(transposed)]
    from_top = not own_only

    def initial(i, carry):
        j = kind.block(i)
        at = kind.place(i)[0]
        nu = vis[j]
        values = [res[i * 4 + c] for c in range(4)]
        y0 = block_times(inv, j * 16, values, transposed, 2 if from_top else 4)
        for c in range(4):
            first[i * 4 + c] = y0[c]
        carried[at] = products(matrix, [nu * y for y in y0])
        return carry

    run_all(kind.count, initial)

    def correct(i, carry):
        j = kind.block(i)
        nu = vis[j]
        sums = stencil(carried, kind.place(i), lambda d: kappa[j * 4 + d])
        y0 = [first[i * 4 + c] for c in range(4)]
        own = block_times(diag, j * 16, y0, transposed)
        rest = [res[i * 4 + c] - own[c] + nu * sums[c] for c in range(4)]
        at = kind.place(i)[0]
        y = block_times(inv, j * 16, rest, transposed)
        z = [a + b for a, b in zip(y0, y)]
        for c in range(4):
            update[i * 4 + c] = z[c]
        start = 3 * 32 if own_only and j != OWN else 0
        carried_on[at, start:] = products(matrix, [nu * t for t in z], start)
        return carry

    run_all(kind.count, correct)

    def apply(i, carry):
        if own_only:
            i = i * 2 if kind is Adjoint else 1
        j = kind.block(i)
        sums = stencil(carried_on, kind.place(i), None)
        values = [update[i * 4 + c] for c in range(4)]
        own = block_times(diag, j * 16, values, transposed)
        nu = vis[j]
        for c in range(4):
            image[i * 4 + c] = own[c] - nu * sums[c]
        return carry

    run_all(kind.own if own_only else kind.count, apply)


def dots_of(residual, image, last, at_of, vectors):
    sums = None
    for c in range(4):
        e, q, p = [[ref[at_of(v) + c] for v in range(vectors)] for ref in (residual, image, last)]
        parts = []
        for x, y in ((q, q), (e, q), (e, p), (q, p), (p, p)):
            parts.append(x[0] * y[0])
            if vectors == 2:
                mixed = x[0] * y[1]
                parts.append(mixed + mixed if x is y else mixed + x[1] * y[0])
                parts.append(x[1] * y[1])
        parts = [(a[0] + a[1]) + (a[2] + a[3]) for a in parts]
        sums = parts if sums is None else [a + b for a, b in zip(sums, parts)]
    lines = [jnp.sum(tile, axis=0, keepdims=True) for tile in sums]
    return [jnp.sum(line, axis=1, keepdims=True) for line in lines]


def merged(after, before):
    return jnp.where(iota((4, 8, 128), 2) % CHUNK < CHUNK // 2, after, before)


def layer_sums(update, spread, target, vector):
    for i, j in enumerate((OWN, NEAR)):
        weight = spread[j]
        active = jnp.where(weight < 0.0, 1.0, 0.0)
        at = (vector * 2 + i) * 4
        for c in range(2):
            tile = update[4 + c] if j == OWN else merged(update[8 + c], update[c])
            target[at + c] = weight * jnp.sum(active * tile, axis=1, keepdims=True)
        for c in range(2, 4):
            target[at + c] = jnp.zeros((4, 8, 128), F32)


def unpack(block, part, j, inv, diag, vis, small, turned_rows):
    sub = iota((8, 128), 0)
    pair = iota((LINES, 128), 1) % CHUNK // 2
    size = part[1] - part[0]
    last_start = 2 * SLOTS * size - 8

    def eight(start):
        if start < 0:
            return pltpu.roll(block[pl.ds(0, 8), :], -start, 0)
        if start > last_start:
            return pltpu.roll(block[pl.ds(last_start, 8), :], 8 + last_start - start, 0)
        return block[pl.ds(start, 8), :]

    for half in range(2):
        bases = [(half * SLOTS + s) * size - part[0] for s in range(SLOTS)]
        for m in range(3):
            tiles = [jnp.zeros((8, 128), F32)] * SLOTS
            for first, last, row in RUNS[m]:
                from_row, to_row = max(row, part[0]), min(row + last - first, part[1] - 1)
                if from_row > to_row:
                    continue
                keep = (sub >= from_row - row + first) & (sub <= to_row - row + first)
                tiles = [
                    jnp.where(keep, eight(base + row - first), tile)
                    for base, tile in zip(bases, tiles)
                ]
            turned_rows[m * 128 : m * 128 + 128, :] = jnp.concatenate(tiles, axis=0).T
        for r in range(ROWS):
            for t, target in enumerate((inv, diag)):
                for cp in range(16):
                    line = table_line(t, r, cp)
                    tile = jnp.zeros((8, 128), F32)
                    for m in range(3):
                        layers = turned_rows[pl.ds(m * 128 + line - 2 * m, 8), :]
                        tile = jnp.where(sub // 2 == m, layers, tile)
                    target[j * 16 + cp, half * 2 + r] = tile
        tiles = [eight(base + OTHER_ROWS - 6) for base in bases]
        others = jnp.concatenate(tiles, axis=0).T
        lines = others[3 * LINES :]
        for m in range(3):
            moved = pltpu.roll(others[m * LINES : (m + 1) * LINES], (2 * m - 6) % 128, 1)
            lines = jnp.where(pair == m, moved, lines)
        for r in range(ROWS):
            vis[j, half * 2 + r] = lines[r * 16 : r * 16 + 8]
            small[j, half * 2 + r] = lines[r * 16 + 8 : r * 16 + 16]


def solve_kernel(
    coupling, low, mine, high, message,
    inv, diag, vis, small, kappa, spread, res, res_two, first, carried, carried_on, update, image, last, start, turned_rows,
    matrix_forward, matrix_adjoint,
):
    gx, gy = lax.axis_index("gx"), lax.axis_index("gy")
    nx, ny = lax.axis_size("gx"), lax.axis_size("gy")
    chunk = chunk_of(gy % 4, gx)
    parts = ((low, TO_AFTER), (mine, (0, CHUNK_ROWS)), (high, TO_BEFORE))
    for j, (block, part) in enumerate(parts):
        unpack(block, part, j, inv, diag, vis, small, turned_rows)
    for field in (carried, carried_on):
        for empty in (0, 4):
            field[empty] = jnp.zeros(field.shape[1:], F32)
    for transposed, matrix in enumerate((matrix_forward, matrix_adjoint)):
        matrix[...] = coupling_matrix(coupling, transposed)

    shape = (4, 8, 128)
    layer = iota(shape, 1)
    lane = iota(shape, 2)
    source = (iota(shape, 0) // 2) * SLOTS + lane // CHUNK
    low_row = iota(shape, 0) % 2 == 0
    for j in range(3):
        tiles = small[j]
        counts = tiles[:, COUNT_ROW : COUNT_ROW + 1, :]
        whole = jnp.maximum(counts, 1.0)
        active = jnp.where(layer.astype(F32) < counts, 1.0, 0.0)
        spread[j] = -active / (whole * whole)
        for c in range(2):
            rhs = tiles[:, RHS_ROW + c : RHS_ROW + c + 1, :]
            res[j * 4 + c] = jnp.where(layer == 0, rhs, 0.0)
        for c in range(2, 4):
            res[j * 4 + c] = jnp.zeros(shape, F32)
        column = (gy * COLS + (chunk + j - OWN) * CHUNK) + lane % CHUNK
        within = column & (COLS - 1)
        south_on = jnp.where((within == 0) & (column > 0), 1.0, 0.0)
        north_on = jnp.where((within == COLS - 1) & (column < ny * COLS - 1), 1.0, 0.0)
        south_in = jnp.where(within == 0, 0.0, 1.0)
        north_in = jnp.where(within == COLS - 1, 0.0, 1.0)
        side_exists = (low_row & (source > 0)) | (jnp.logical_not(low_row) & (source < nx - 1))
        side = jnp.where(side_exists, 1.0, 0.0)
        shared = south_on + north_on + side
        level = (1.0 + tiles[:, PATTERN_ROW : PATTERN_ROW + 1, :]) / 5.0
        own_weight = jnp.where(shared > 0.0, level, 1.0)
        near = (1.0 - own_weight) / jnp.maximum(shared, 1.0)
        inward = own_weight + near * (south_on + north_on)
        outward = own_weight + near * side
        kappa[j * 4] = jnp.where(low_row, inward, outward)
        kappa[j * 4 + 1] = jnp.where(low_row, outward, inward)
        kappa[j * 4 + 2] = own_weight + near * (north_on + side * north_in)
        kappa[j * 4 + 3] = own_weight + near * (south_on + side * south_in)

    for table, size in ((inv, 16), (diag, 16), (kappa, 4), (vis, 1), (spread, 1)):
        for k in range(size):
            table[NEAR * size + k] = merged(table[2 * size + k], table[k])

    tables = (inv, diag, vis, kappa, (matrix_forward, matrix_adjoint))
    sweep(Forward, res, first, carried, carried_on, update, image, False, tables)
    layer_sums(update, spread, res_two, 0)
    for t in range(12):
        res[t] = res[t] - image[t]
    sweep(Forward, res, first, carried, carried_on, update, last, True, tables)
    layer_sums(update, spread, res_two, 1)
    dots = dots_of(res, image, last, lambda v: 4, 1)

    sweep(Adjoint, res_two, first, carried, carried_on, update, image, False, tables)
    for v in range(2):
        for c in range(4):
            start[v * 4 + c] = update[v * 8 + c]
    for t in range(16):
        res_two[t] = res_two[t] - image[t]
    sweep(Adjoint, res_two, first, carried, carried_on, update, last, True, tables)
    dots += dots_of(res_two, image, last, lambda v: v * 8, 2)

    before, here, after = small[0], small[1], small[2]
    around = x_plus(here) + x_minus(here) + y_plus(here, after) + y_minus(here, before)
    first[0] = 4.0 * here - around
    sub = iota((8, 128), 0)
    column = iota((1, 128), 1) % CHUNK
    lines = []
    for k in range(0, len(dots), CHUNK):
        line = jnp.zeros((1, 128), F32)
        for m, dot in enumerate(dots[k : k + CHUNK]):
            line = jnp.where(column == m, dot, line)
        lines.append(line)

    def send(half, carry):
        for r in range(ROWS):
            i = half * 2 + r
            tiles = [start[k, i] for k in range(8)]
            tiles += [update[v * 8 + c, i] for v in range(2) for c in range(4)]
            prior = pltpu.roll(first[0, i], SPARE - BETA_ROW, 0)
            tiles[0] = jnp.where(sub == SPARE, prior, tiles[0])
            for k, line in enumerate(lines):
                tiles[k] = jnp.where(sub == 7, line, tiles[k])
            message[pl.ds(half * SLOTS, SLOTS), r] = turned(jnp.stack(tiles))
        return carry

    lax.fori_loop(0, 2, send, 0)


def steps(image2, residual_image, residual_last, image_last, last2):
    one = (residual_image + image2) / (image2 + EPSILON)
    off = 1.0 - one
    along = off * residual_image + one * residual_last + off * off * image2 + off * one * image_last
    squared = off * off * image2 + 2.0 * off * one * image_last + one * one * last2
    two = along / (squared + EPSILON)
    return one + two * off, one * two


def gather_kernel(block, lines):
    total = None
    for k in range(block.shape[0]):
        total = block[k, 0] if total is None else total + block[k, 0]
    lane, sub = iota((8, 128), 1), iota((8, 128), 0)
    out = jnp.zeros((8, 128), F32)
    for i in range(8):
        keep = (sub == i) & (lane % CHUNK == 7)
        out += pltpu.roll(jnp.where(keep, total, 0.0), (i - 7) % 128, 1)
    lines[...] = jnp.broadcast_to(jnp.sum(out, axis=0, keepdims=True), lines.shape)


def final_kernel(dots, block, grounded, vel, hessian, adjoint):
    line = jnp.sum(dots[...], axis=0, keepdims=True)
    lane = iota((1, 128), 1)

    def get(k):
        return jnp.sum(jnp.where(lane == k, line, 0.0), axis=1, keepdims=True)

    a, b = steps(*[get(k) for k in range(5)])
    kinds = []
    for k in range(5):
        at = 5 + 3 * k
        kinds.append(a * a * get(at) + a * b * get(at + 1) + b * b * get(at + 2))
    p, q = steps(*kinds)
    weights = (p * a, p * b, q * a, q * b)
    turn = lax.axis_index("gy") % 4
    for part in range(2):
        sources = [device_of(turn, part * SLOTS + k) for k in range(SLOTS)]
        for r in range(ROWS):
            tiles = turned(jnp.stack([block[source, r] for source in sources]))
            at = slice(part * 128, part * 128 + 128)
            heads = []
            for c in range(4):
                total = weights[0] * tiles[c]
                for v in range(1, 4):
                    total += weights[v] * tiles[v * 4 + c]
                adjoint[c, :, r, at] = total[0:LAYERS]
                heads.append(total[0:1])
            row = slice(r, r + 1)
            data = grounded[row, at].astype(F32) * (
                vel[0, row, at] * heads[0] + vel[1, row, at] * heads[1]
            )
            hessian[row, at] = data + PRIOR_WEIGHT * tiles[0, SPARE : SPARE + 1]


VMEM = pl.BlockSpec(memory_space=pltpu.VMEM)
SMEM = pl.BlockSpec(memory_space=pltpu.SMEM)
HBM = pl.BlockSpec(memory_space=pltpu.HBM)


def call(kernel, name, operands, in_specs, outs, scratch=()):
    return pl.pallas_call(
        kernel,
        out_shape=[jax.ShapeDtypeStruct(shape, F32) for shape in outs],
        in_specs=in_specs,
        out_specs=[VMEM] * len(outs),
        scratch_shapes=scratch,
        compiler_params=pltpu.CompilerParams(vmem_limit_bytes=(63 if name == "pack_tables" else 40) * 1024 * 1024),
        name=name,
    )(*operands)


def neighbour_pairs(step):
    n_gy = lax.axis_size("gy")
    places = [gx * n_gy + gy for gy in range(n_gy) for gx in ORDERS[gy % 4]]
    count = len(places)
    return [(places[i], places[i + step]) for i in range(count) if 0 <= i + step < count]


def per_device(
    diag_block,
    block_inverse,
    viscosity,
    coupling,
    active_layers,
    grounded,
    weight_pattern,
    beta_step,
    base_vel,
):
    n_gx, n_gy = lax.axis_size("gx"), lax.axis_size("gy")
    table = (16,) + viscosity.shape
    raw = [
        diag_block.reshape(table),
        block_inverse.reshape(table),
        viscosity,
        active_layers,
        grounded,
        weight_pattern,
        beta_step,
        base_vel,
    ]
    (sent,) = call(
        pack_kernel,
        "pack_tables",
        raw,
        [HBM] * 8,
        [(n_gx * CHUNK_ROWS, 128)],
        [pltpu.VMEM(x.shape, x.dtype) for x in raw]
        + [
            pltpu.VMEM((384, COLS), F32),
            pltpu.VMEM((LINES, COLS), F32),
            pltpu.VMEM((n_gx, 32, 128), F32),
            pltpu.SemaphoreType.DMA((8,)),
        ],
    )
    sent = sent.reshape(n_gx, CHUNK_ROWS // 2, 2, 128)
    mine = lax.all_to_all(sent, "gx", 0, 0, tiled=True)
    to_after = mine[:, TO_AFTER[0] // 2 : TO_AFTER[1] // 2]
    to_before = mine[:, TO_BEFORE[0] // 2 : TO_BEFORE[1] // 2]
    low = lax.ppermute(to_after, ("gx", "gy"), neighbour_pairs(1))
    high = lax.ppermute(to_before, ("gx", "gy"), neighbour_pairs(-1))
    blocks = [x.reshape(-1, 128) for x in (low, mine, high)]

    def field(count):
        return pltpu.VMEM((count, 4, 8, 128), F32)

    (back,) = call(
        solve_kernel,
        "solve_both",
        [coupling.reshape(96)] + blocks,
        [SMEM] + [VMEM] * 3,
        [(n_gx, 2, 8, 128)],
        [
            field(64),
            field(64),
            field(4),
            field(3),
            field(16),
            field(4),
            field(12),
            field(16),
            field(16),
            pltpu.VMEM((5, GROUPS * 32, 512), F32),
            pltpu.VMEM((5, GROUPS * 32, 512), F32),
            field(16),
            field(16),
            field(16),
            field(8),
            pltpu.VMEM((392, 128), F32),
        ]
        + [pltpu.VMEM((GROUPS * 32, len(PASSES) * 32), jnp.bfloat16)] * 2,
    )
    block = lax.all_to_all(back, "gx", 0, 0, tiled=True)
    (lines,) = call(gather_kernel, "sum_gx", [block], [VMEM], [(n_gy, 128)])
    lines = lax.all_to_all(lines, "gy", 0, 0, tiled=True)
    hessian_vec, adjoint = call(
        final_kernel,
        "combine",
        [lines, block, grounded, base_vel],
        [VMEM] * 4,
        [beta_step.shape, (4,) + viscosity.shape],
    )
    return hessian_vec, adjoint


def solution(mesh):
    placed = (
        P(None, None, None, "gx", "gy"),
        P(None, None, None, "gx", "gy"),
        P(None, "gx", "gy"),
        P(),
        P("gx", "gy"),
        P("gx", "gy"),
        P("gx", "gy"),
        P("gx", "gy"),
        P(None, "gx", "gy"),
    )
    return jax.shard_map(
        per_device,
        mesh=mesh,
        in_specs=placed,
        out_specs=(P("gx", "gy"), P(None, None, "gx", "gy")),
        check_vma=False,
    )
```
